32 devices in a mesh: grp: 4 (over y, x), dev: 8 (over z, core).
Axes of the slice: x: 2, y: 2, z: 4, core: 2. Of those that a mesh axis runs over, the one named last changes fastest.
Arguments:
- displacement: float32 [3, 16, 32, 32], P(None, 'dev')
- external_force: float32 [3, 16, 32, 32], P(None, 'dev'), may hold values from -6 to 6
- element_sample: int32 [16, 32, 32], P('dev'), may hold values from 0 to 31, as said below
- lame_field: bfloat16 [32, 32, 1024], P('grp', 'dev'), may hold values from 0.5 to 2
- shear_field: bfloat16 [32, 32, 1024], P('grp', 'dev'), may hold values from 0.29882812 to 3
- plastic_steps: int32 [32], replicated, may hold values from 1 to 4
- owner_slot: int32 [32], replicated, may hold values from 0 to 7, as said below
Outputs:
- displacement_next: float32 [3, 16, 32, 32], P(None, 'dev')
- sample_response: float32 [32, 8], P(('grp', 'dev'))
- micro_strain: float32 [6, 32, 32, 1024], P(None, 'grp', 'dev')
The draws below stay inside these ranges and needn't reach their ends.
Inputs may be any that keep to these rules, and one draw needn't show every extreme that they name: `element_sample`: every value from 0 to 31 is taken by at least one element. `owner_slot`: within each aligned block of 8 RVEs a permutation of 0 to 7; slot s of a block belongs to the block's owner s.
All inputs are finite; a program needn't handle non-finite values.
Results may differ from the reference program's by a relative error of at most 0.0009.
Values may be sent and summed in bfloat16 or wider, within the bound.
No kernel may reach another device: no remote copies, remote signals or barrier semaphores. Data moves between devices by JAX's collectives and lax.ppermute only.
A program may use at most 64 MiB of HBM per device.

```python
import math
import jax
import jax.numpy as jnp
from jax import lax

VOX = 32
RVE_DEV = 1
RVE_GRP = 8
RVES = 32
MY = 32
MZ = 32
NX = 16
ITERS = 1
KMAX = 4
CG_STEPS = 3


def draw_displacement(key, part):
    keys = jax.random.split(jax.random.fold_in(key, 37), 4)
    waves = jax.random.randint(keys[0], (6, 3), 1, 4).astype(jnp.float32)
    amplitude = 2.0 * jax.random.normal(keys[1], (3, 6), jnp.float32)
    phase = jax.random.uniform(keys[2], (6,), jnp.float32, 0.0, 2.0 * jnp.pi)
    along_x = jnp.arange(NX, dtype=jnp.float32) / NX
    along_y = jnp.arange(MY, dtype=jnp.float32) / MY
    along_z = jnp.arange(MZ, dtype=jnp.float32) / MZ
    angle = 2.0 * jnp.pi * (waves[:, 0, None, None, None] * along_x[None, :, None, None] + waves[:, 1, None, None, None] * along_y[None, None, :, None] + waves[:, 2, None, None, None] * along_z[None, None, None, :]) + phase[:, None, None, None]
    smooth = jnp.einsum('cm,mxyz->cxyz', amplitude, jnp.sin(angle))
    rough = 0.3 * jax.random.normal(keys[3], (3, NX, MY, MZ), jnp.float32)
    return (smooth + rough).astype(jnp.float32)


def draw_element_sample(key, part):
    total = NX * MY * MZ
    plane = MY * MZ
    chosen = jax.random.permutation(jax.random.fold_in(key, 11), total)[:RVES].astype(jnp.int32)
    seed_x = chosen // plane
    seed_y = chosen // MZ % MY
    seed_z = chosen % MZ
    labels = jnp.arange(RVES, dtype=jnp.int32)

    def nearest(layer):
        within = jnp.arange(plane, dtype=jnp.int32)
        offset_x = layer - seed_x[None, :]
        offset_y = (within // MZ)[:, None] - seed_y[None, :]
        offset_z = (within % MZ)[:, None] - seed_z[None, :]
        score = (offset_x * offset_x + offset_y * offset_y + offset_z * offset_z) * RVES + labels[None, :]
        return jnp.argmin(score, axis=1).astype(jnp.int32)
    return lax.map(nearest, jnp.arange(NX, dtype=jnp.int32)).reshape(NX, MY, MZ)


def plastic_table(key):
    keys = jax.random.split(jax.random.fold_in(key, 23), 3)
    index = jnp.arange(RVES, dtype=jnp.int32)
    zone_start = jax.random.randint(keys[0], (), 0, RVES)
    in_zone = (index - zone_start) % RVES < RVES // 4
    light = jax.random.randint(keys[1], (RVES,), 1, 3)
    heavy = jax.random.randint(keys[2], (RVES,), KMAX // 2, KMAX + 1)
    steps = jnp.where(in_zone, heavy, light)
    return jnp.where(index == zone_start, KMAX, steps).astype(jnp.int32)


def draw_plastic_steps(key, part):
    return plastic_table(key)


def draw_owner_slot(key, part):
    steps = plastic_table(key)
    blocks = steps.reshape(RVES // RVE_GRP, RVE_GRP)
    owners = RVE_GRP // RVE_DEV

    def assign(row):
        ranked = jnp.argsort(-row, stable=True).astype(jnp.int32)
        place = jnp.arange(RVE_GRP, dtype=jnp.int32)
        lap_number = place // owners
        column = place % owners
        owner = jnp.where(lap_number % 2 == 0, column, owners - 1 - column)
        slot_of_rank = owner * RVE_DEV + lap_number
        return jnp.zeros((RVE_GRP,), jnp.int32).at[ranked].set(slot_of_rank)
    return jax.vmap(assign)(blocks).reshape(RVES).astype(jnp.int32)


def level_of(rng, shape, cuts, least, top_value):
    factor_of = 1.0
    for position, shards_of in cuts:
        heights = jax.random.uniform(jax.random.fold_in(jax.random.fold_in(rng, 6), position), (shards_of,), jnp.float32, least / len(cuts), top_value / len(cuts))
        factor_of = factor_of * jnp.repeat(jnp.exp(heights), shape[position] // shards_of).reshape((-1,) + (1,) * (len(shape) - 1 - position))
    return factor_of


def gaussian(key, dims, scale, reach, shards=(), kind=jnp.bfloat16):
    values = scale * jax.random.normal(key, dims, jnp.float32)
    if shards:
        values = values * level_of(key, dims, shards, -0.22, 0.18)
    return jnp.clip(values, -reach, reach).astype(kind)


def setup_inputs(seed: int = 0) -> dict:
    key_of = jax.random.split(jax.random.key(seed), 8)
    displacement = draw_displacement(jax.random.fold_in(key_of[7], 71), 0)
    external_force = gaussian(key_of[1], (3, NX, MY, MZ), 1.0, 6.0, ((1, 8),), jnp.float32)
    element_sample = draw_element_sample(jax.random.fold_in(key_of[7], 71), 0)
    lame_field = jnp.clip(0.5 + 1.5 * jax.random.uniform(key_of[3], (RVES, VOX, VOX * VOX), jnp.float32) ** level_of(key_of[3], (RVES, VOX, VOX * VOX), ((0, 4), (1, 8)), -0.2, 0.2), 0.5, 2.0).astype(jnp.bfloat16)
    shear_field = jnp.clip(jnp.exp(math.log(3.0) - 2.306499 * jax.random.uniform(key_of[4], (RVES, VOX, VOX * VOX), jnp.float32) ** level_of(key_of[4], (RVES, VOX, VOX * VOX), ((0, 4), (1, 8)), -0.2, 0.2)), 0.29882812, 3.0).astype(jnp.bfloat16)
    plastic_steps = draw_plastic_steps(jax.random.fold_in(key_of[7], 71), 0)
    owner_slot = draw_owner_slot(jax.random.fold_in(key_of[7], 71), 0)
    return {"displacement": displacement, "external_force": external_force, "element_sample": element_sample, "lame_field": lame_field, "shear_field": shear_field, "plastic_steps": plastic_steps, "owner_slot": owner_slot}


shear_ref = 1.65
lame_ref = 1.25
green_ratio = (lame_ref + shear_ref) / (lame_ref + 2.0 * shear_ref)
relax_rate = 0.35
flow_scale = 4.0
spring_rate = 0.2


def wave_at(count, index):
    angle = (2.0 * jnp.pi / count) * index.astype(jnp.float32)
    return jnp.where(index % (count // 2) == 0, 0.0, jnp.sin(angle)).astype(jnp.float32)


def inverse_square(first, second, third):
    square = first * first + second * second + third * third
    live = square > 0.0
    return jnp.where(live, 1.0 / jnp.where(live, square, 1.0), 0.0)


def green_parts(parts, first, second, third, inverse):
    xx, yy, zz, yz, xz, xy = parts
    along_first = xx * first + xy * second + xz * third
    along_second = xy * first + yy * second + yz * third
    along_third = xz * first + yz * second + zz * third
    inner = first * along_first + second * along_second + third * along_third
    scaled = green_ratio * inner * inverse
    push_first = (along_first - scaled * first) * inverse / shear_ref
    push_second = (along_second - scaled * second) * inverse / shear_ref
    push_third = (along_third - scaled * third) * inverse / shear_ref
    return (first * push_first, second * push_second, third * push_third,
            0.5 * (second * push_third + third * push_second),
            0.5 * (first * push_third + third * push_first),
            0.5 * (first * push_second + second * push_first))


def measure(stress):
    return (stress[0] * stress[0] + stress[1] * stress[1] + stress[2] * stress[2]
            + 2.0 * (stress[3] * stress[3] + stress[4] * stress[4] + stress[5] * stress[5]))


def material(strain, lame, shear, steps, bound):
    trace = strain[0] + strain[1] + strain[2]
    third_trace = trace / 3.0
    deviator = jnp.concatenate([strain[:3] - third_trace, strain[3:]])

    def relax(count, plastic):
        ratio = measure(2.0 * shear * (deviator - plastic)) / flow_scale
        moved = plastic + relax_rate * (deviator - plastic) * (ratio / (1.0 + ratio))
        return jnp.where(count < steps, moved, plastic)

    plastic = lax.fori_loop(0, bound, relax, jnp.zeros_like(deviator))
    elastic = strain - plastic
    stress = jnp.concatenate([2.0 * shear * elastic[:3] + lame * trace, 2.0 * shear * elastic[3:]])
    ratio = measure(2.0 * shear * (deviator - plastic)) / flow_scale
    return stress, ratio


def green_real(stress, first, second, third, inverse):
    spectrum = jnp.fft.fftn(stress, axes=(1, 2, 3))
    parts = green_parts(tuple(spectrum[part] for part in range(6)), first, second, third, inverse)
    return jnp.real(jnp.fft.ifftn(jnp.stack(parts), axes=(1, 2, 3)))


def sample_solve(item, first, second, third, inverse):
    lame, shear, count, load = item
    lame = lame.astype(jnp.float32).reshape(VOX, VOX, VOX)
    shear = shear.astype(jnp.float32).reshape(VOX, VOX, VOX)
    strain = jnp.broadcast_to(load[:, None, None, None], (6, VOX, VOX, VOX))
    for sweep in range(ITERS):
        stress, ratio = material(strain, lame, shear, count, KMAX)
        strain = strain - green_real(stress, first, second, third, inverse)
    stress, ratio = material(strain, lame, shear, count, KMAX)
    response = jnp.concatenate([jnp.sum(stress, axis=(1, 2, 3)), jnp.sum(lame)[None],
                                jnp.sum(shear / (1.0 + ratio))[None]]) / (VOX ** 3)
    return strain, response


def shifted(field, axis, upward):
    extent = field.shape[axis]
    zero = jnp.zeros_like(lax.slice_in_dim(field, 0, 1, axis=axis))
    if upward:
        return jnp.concatenate([lax.slice_in_dim(field, 1, extent, axis=axis), zero], axis=axis)
    return jnp.concatenate([zero, lax.slice_in_dim(field, 0, extent - 1, axis=axis)], axis=axis)


def average_next(field, axis):
    return 0.5 * (field + shifted(field, axis, True))


def differ_next(field, axis):
    return shifted(field, axis, True) - field


def average_back(field, axis):
    return 0.5 * (field + shifted(field, axis, False))


def differ_back(field, axis):
    return shifted(field, axis, False) - field


def assemble(slope_x, slope_y, slope_z):
    return jnp.stack([slope_x[0], slope_y[1], slope_z[2], 0.5 * (slope_y[2] + slope_z[1]),
                      0.5 * (slope_x[2] + slope_z[0]), 0.5 * (slope_x[1] + slope_y[0])])


def strain_of(field):
    smooth_z = average_next(field, 3)
    slope_x = differ_next(average_next(smooth_z, 2), 1)
    slope_y = average_next(differ_next(smooth_z, 2), 1)
    slope_z = average_next(average_next(differ_next(field, 3), 2), 1)
    return assemble(slope_x, slope_y, slope_z)


def force_of(stress):
    xx, yy, zz, yz, xz, xy = stress
    along_x = jnp.stack([xx, xy, xz])
    along_y = jnp.stack([xy, yy, yz])
    along_z = jnp.stack([xz, yz, zz])
    first = average_back(average_back(along_x, 3), 2)
    rest = differ_back(average_back(along_y, 3), 2) + average_back(differ_back(along_z, 3), 2)
    return differ_back(first, 1) + average_back(rest, 1)


def stiffness(field, lame_cells, shear_cells):
    strain = strain_of(field)
    trace = strain[0] + strain[1] + strain[2]
    stress = jnp.concatenate([2.0 * shear_cells * strain[:3] + lame_cells * trace, 2.0 * shear_cells * strain[3:]])
    return force_of(stress) + spring_rate * field


def reference(displacement, external_force, element_sample, lame_field, shear_field, plastic_steps, owner_slot):
    element_strain = strain_of(displacement)
    flat_sample = element_sample.reshape(-1).astype(jnp.int32)
    sums = jax.ops.segment_sum(element_strain.reshape(6, -1).T, flat_sample, num_segments=RVES)
    counts = jax.ops.segment_sum(jnp.ones(flat_sample.shape, jnp.float32), flat_sample, num_segments=RVES)
    loads = sums / counts[:, None]
    index = jnp.arange(VOX, dtype=jnp.int32)
    waves = wave_at(VOX, index)
    first = waves[:, None, None]
    second = waves[None, :, None]
    third = waves[None, None, :]
    inverse = inverse_square(first, second, third)

    def solve_one(item):
        return sample_solve(item, first, second, third, inverse)

    strains, responses = lax.map(solve_one, (lame_field, shear_field, plastic_steps, loads))
    micro_strain = jnp.transpose(strains, (1, 0, 2, 3, 4)).reshape(6, RVES, VOX, VOX * VOX)
    rows = jnp.arange(RVES, dtype=jnp.int32)
    destination = (rows // RVE_GRP) * RVE_GRP + owner_slot.astype(jnp.int32)
    sample_response = jnp.zeros((RVES, 8), jnp.float32).at[destination].set(responses)
    element_table = jnp.take(responses, flat_sample, axis=0)
    fields = element_table.T.reshape((8,) + displacement.shape[1:])
    element_stress = fields[:6]
    lame_cells = fields[6]
    shear_cells = fields[7]
    residual = external_force - force_of(element_stress) - spring_rate * displacement
    update = jnp.zeros_like(displacement)
    remainder = residual
    direction = residual
    norm_now = jnp.sum(remainder * remainder)
    for turn in range(CG_STEPS):
        image = stiffness(direction, lame_cells, shear_cells)
        alpha = norm_now / jnp.sum(direction * image)
        update = update + alpha * direction
        remainder = remainder - alpha * image
        if turn + 1 < CG_STEPS:
            norm_next = jnp.sum(remainder * remainder)
            direction = remainder + (norm_next / norm_now) * direction
            norm_now = norm_next
    return displacement + update, sample_response, micro_strain
```

```python
import functools
import jax
import jax.numpy as jnp
import numpy as np
from jax import lax
from jax.experimental import pallas as pl
from jax.experimental.pallas import tpu as pltpu
from jax.sharding import PartitionSpec as P

CG_STEPS = 3
shear_ref = 1.65
lame_ref = 1.25
green_ratio = (lame_ref + shear_ref) / (lame_ref + 2.0 * shear_ref)
relax_rate = 0.35
flow_scale = 4.0
spring_rate = 0.2
f32 = jnp.float32
bf16 = jnp.bfloat16
DIAG = ((0, 0), (1, 1), (2, 2))
PAIRS = ((0, 0), (1, 1), (2, 2), (1, 2), (0, 2), (0, 1))
SLOT = {(0, 0): 0, (1, 1): 1, (2, 2): 2, (1, 2): 3, (2, 1): 3, (0, 2): 4, (2, 0): 4, (0, 1): 5, (1, 0): 5}


def split_table(table):
    high = table.astype(np.float32).astype(bf16)
    low = (table - high.astype(np.float64)).astype(np.float32).astype(bf16)
    return np.stack([high, low])


def tables(vox):
    half = vox // 2
    n = np.arange(vox)[:, None]
    k = np.arange(half)[None, :]
    angle = 2.0 * np.pi * (n * k % vox) / vox
    cosine = np.cos(angle) * np.sqrt(2.0 / vox)
    sine = np.sin(angle) * np.sqrt(2.0 / vox)
    cosine[:, 0] = 1.0 / np.sqrt(vox)
    sine[:, 0] = (1.0 - 2.0 * (np.arange(vox) % 2)) / np.sqrt(vox)
    basis = np.concatenate([cosine, sine], axis=1)
    by_parity = basis.reshape(vox, 2, half)
    plane = np.einsum("ypk,zql->yzqpkl", by_parity, by_parity).reshape(vox * vox, vox * vox)
    line = basis.T
    forward_line = np.kron(np.eye(2), line)
    backward_line = np.kron(np.eye(6), line.T)
    wave = np.sin(2.0 * np.pi * np.arange(half) / vox)
    wave[0] = 0.0
    first = np.broadcast_to(wave[:, None, None], (half, half, half))
    second = np.broadcast_to(wave[None, :, None], (half, half, half))
    third = np.broadcast_to(wave[None, None, :], (half, half, half))
    square = first**2 + second**2 + third**2
    inverse = np.where(square > 0.0, 1.0 / np.where(square > 0.0, square, 1.0), 0.0)
    waves = (first, second, third)
    products = [waves[a] * waves[b] for a, b in PAIRS]
    rows = products + [inverse / shear_ref, green_ratio * inverse]
    multipliers = np.stack(rows).reshape(len(rows), half, half * half).astype(np.float32)
    return split_table(plane), split_table(forward_line), split_table(backward_line), multipliers


def split(value):
    high = value.astype(bf16)
    return high, (value - high.astype(f32)).astype(bf16)


def dot(left, right):
    return lax.dot_general(left, right, (((1,), (0,)), ((), ())), preferred_element_type=f32)


def dot_t(left, right):
    return lax.dot_general(left, right, (((1,), (1,)), ((), ())), preferred_element_type=f32)


def by_table(value, high, low, contract):
    rows = value.shape[0]
    value_high, value_low = split(value)
    both = contract(jnp.concatenate([value_high, value_low], axis=0), high)
    return both[:rows] + both[rows:] + contract(value_high, low)


def table_by(high, low, value):
    rows = high.shape[0]
    value_high, value_low = split(value)
    both = dot(jnp.concatenate([high, low], axis=0), value_high)
    return both[:rows] + both[rows:] + dot(high, value_low)


def lane_position(shape):
    return lax.broadcasted_iota(jnp.int32, shape, 1)


def row_position(shape):
    return lax.broadcasted_iota(jnp.int32, shape, 0)


class Stencil:
    def __init__(self, shape, width):
        self.rows, self.columns = shape
        self.width = width
        lane = lane_position(shape)
        row = row_position(shape)
        self.last_z = lane % width == width - 1
        self.first_z = lane % width == 0
        self.last_y = lane >= self.columns - width
        self.first_y = lane < width
        self.last_x = row == self.rows - 1
        self.first_x = row == 0

    def up_z(self, v):
        return jnp.where(self.last_z, 0.0, pltpu.roll(v, self.columns - 1, 1))

    def up_y(self, v):
        return jnp.where(self.last_y, 0.0, pltpu.roll(v, self.columns - self.width, 1))

    def up_x(self, v):
        return jnp.where(self.last_x, 0.0, pltpu.roll(v, self.rows - 1, 0))

    def down_z(self, v):
        return jnp.where(self.first_z, 0.0, pltpu.roll(v, 1, 1))

    def down_y(self, v):
        return jnp.where(self.first_y, 0.0, pltpu.roll(v, self.width, 1))

    def down_x(self, v):
        return jnp.where(self.first_x, 0.0, pltpu.roll(v, 1, 0))

    def strain(self, field):
        slopes = []
        for v in field:
            next_z = self.up_z(v)
            sum_z = v + next_z
            dif_z = next_z - v
            next_y = self.up_y(sum_z)
            sums = sum_z + next_y
            along_y = next_y - sum_z
            along_z = dif_z + self.up_y(dif_z)
            slopes.append((self.up_x(sums) - sums, along_y + self.up_x(along_y), along_z + self.up_x(along_z)))
        return [
            0.25 * slopes[0][0],
            0.25 * slopes[1][1],
            0.25 * slopes[2][2],
            0.125 * (slopes[2][1] + slopes[1][2]),
            0.125 * (slopes[2][0] + slopes[0][2]),
            0.125 * (slopes[1][0] + slopes[0][1]),
        ]

    def force(self, stress):
        result = []
        for b in range(3):
            along_x, along_y, along_z = (stress[SLOT[(a, b)]] for a in range(3))
            sum_x = along_x + self.down_z(along_x)
            first = sum_x + self.down_y(sum_x)
            sum_y = along_y + self.down_z(along_y)
            dif_z = self.down_z(along_z) - along_z
            back = self.down_y(sum_y)
            rest = (back - sum_y) + (dif_z + self.down_y(dif_z))
            result.append(0.25 * ((self.down_x(first) - first) + (rest + self.down_x(rest))))
        return result


def total(value):
    return jnp.sum(jnp.sum(value, axis=0, keepdims=True), axis=1, keepdims=True)


def measure(stress):
    return (
        stress[0] * stress[0]
        + stress[1] * stress[1]
        + stress[2] * stress[2]
        + 2.0 * (stress[3] * stress[3] + stress[4] * stress[4] + stress[5] * stress[5])
    )


def remaining(shear, size, steps, most):
    stiff = (2.0 * shear) * (2.0 * shear) * size

    def relax(count, left):
        ratio = stiff * left * left
        return left * ((1.0 - relax_rate) + relax_rate / (1.0 + ratio))

    left = lax.fori_loop(0, steps, relax, jnp.ones_like(stiff))
    return left, stiff * left * left


def deviator_of(strain):
    trace = strain[0] + strain[1] + strain[2]
    third = trace / 3.0
    return trace, [strain[0] - third, strain[1] - third, strain[2] - third] + list(strain[3:])


def gather_rows(source, target):
    devices, parts, planes, _ = source.shape
    for part in range(parts):
        for device in range(devices):
            target[part, device * planes : (device + 1) * planes, :] = source[device, part]


def micro_kernel(
    local, local_count, steps_ref, mesh_ref, lame_ref_, shear_ref_, mult_ref, fwd_ref, bwd_ref, table_hbm,
    strain_ref, response_ref, fields, table, sem, spectrum
):
    vox, columns = lame_ref_.shape
    half = vox // 2
    quarter = half * half
    width = vox_width(fields.shape[2])
    copies = [pltpu.make_async_copy(table_hbm.at[i], table.at[i], sem.at[i]) for i in range(2)]
    for copy in copies:
        copy.start()
    own = (lax.axis_index("grp") * lax.axis_size("dev") + lax.axis_index("dev")) * local_count + local
    steps = steps_ref[own]
    gather_rows(mesh_ref, fields)
    stencil = Stencil(fields.shape[1:], width)
    mesh_strain = stencil.strain([fields[c] for c in range(3)])
    mine = fields[3] == own.astype(f32)
    count = total(jnp.where(mine, 1.0, 0.0))
    load = [total(jnp.where(mine, part, 0.0)) / count for part in mesh_strain]
    trace, dev = deviator_of(load)
    lame = lame_ref_[...].astype(f32)
    shear = shear_ref_[...].astype(f32)
    size = measure([0.5 * part for part in dev])
    left, _ = remaining(shear, jnp.broadcast_to(size, shear.shape), steps, 4)
    bulk = lame + (2.0 / 3.0) * shear
    sources = jnp.concatenate([bulk * trace, 2.0 * shear * left], axis=0)
    for copy in copies:
        copy.wait()
    spectral = table_by(fwd_ref[0], fwd_ref[1], by_table(sources, table[0], table[1], dot))

    def block(field, px, py, pz):
        rows = slice(field * vox + px * half, field * vox + (px + 1) * half)
        lanes = slice((pz * 2 + py) * quarter, (pz * 2 + py + 1) * quarter)
        return rows, lanes

    parities = [(px, py, pz) for px in range(2) for py in range(2) for pz in range(2)]
    product = [mult_ref[i] for i in range(6)]
    inverse = mult_ref[6]
    scaled = mult_ref[7]

    def second(blocks, parity, a, b):
        if a == b:
            return -(product[SLOT[(a, b)]] * blocks[parity])
        other = tuple(1 - p if axis in (a, b) else p for axis, p in enumerate(parity))
        value = product[SLOT[(a, b)]] * blocks[other]
        return value if parity[a] == parity[b] else -value

    psi = {}
    raw = {}
    for parity in parities:
        rows, lanes = block(1, *parity)
        raw[parity] = spectral[rows, lanes]
        psi[parity] = inverse * raw[parity]
    phi = {}
    for parity in parities:
        rows, lanes = block(0, *parity)
        pressed = sum(
            (1.0 if a == b else 2.0) * dev[SLOT[(a, b)]] * second(psi, parity, a, b) for a, b in PAIRS
        )
        phi[parity] = (1.0 - green_ratio) * inverse * spectral[rows, lanes] + scaled * pressed
    for parity in parities:
        curl = {pair: second(psi, parity, *pair) for pair in PAIRS}
        for index, (a, b) in enumerate(PAIRS):
            def at(i, j):
                return curl[(min(i, j), max(i, j))]
            if a == b:
                sheared = sum(dev[SLOT[(b, c)]] * at(a, c) for c in range(3))
            else:
                sheared = 0.5 * sum(dev[SLOT[(b, c)]] * at(a, c) + dev[SLOT[(a, c)]] * at(b, c) for c in range(3))
            rows, lanes = block(index, *parity)
            spectrum[rows, lanes] = second(phi, parity, a, b) + sheared
    moved = table_by(bwd_ref[0], bwd_ref[1], by_table(spectrum[...], table[0], table[1], dot_t))
    strain = [load[i] + moved[i * vox : (i + 1) * vox] for i in range(6)]
    planes = strain_ref.shape[2]
    for i in range(6):
        for device in range(strain_ref.shape[0]):
            strain_ref[device, i] = strain[i][device * planes : (device + 1) * planes]
    trace, dev = deviator_of(strain)
    left, ratio = remaining(shear, measure([0.5 * part for part in dev]), steps, 4)
    push = bulk * trace
    pull = 2.0 * shear * left
    stress = [push + pull * dev[i] for i in range(3)] + [pull * dev[i] for i in range(3, 6)]
    parts = stress + [lame, shear / (1.0 + ratio)]
    lane = lane_position(response_ref.shape)
    row = jnp.zeros(response_ref.shape, f32)
    for index, part in enumerate(parts):
        row = jnp.where(lane == index, total(part) / float(vox * columns), row)
    response_ref[...] = row


def vox_width(columns):
    width = int(round(columns**0.5))
    return width


def macro_kernel(
    slots_ref, table_ref, table_v_ref, mesh_ref, force_in_ref, next_ref, row_ref, fields, forces, cells, result
):
    devices, _, planes, columns = mesh_ref.shape
    samples = table_v_ref.shape[0]
    rank = lax.axis_index("dev")
    group = lax.axis_index("grp")
    local_count = row_ref.shape[0]
    group_size = local_count * devices
    start = group * group_size
    for local in range(local_count):
        chosen = jnp.int32(0)
        for j in range(group_size):
            chosen = jnp.where(slots_ref[start + j] == rank * local_count + local, start + j, chosen)
        row_ref[local : local + 1, :] = table_v_ref[pl.ds(chosen, 1), :]
    gather_rows(mesh_ref, fields)
    gather_rows(force_in_ref, forces)
    rows = fields.shape[1]
    height = min(8, rows)
    span = min(512, columns)
    for top in range(0, rows, height):
        for side in range(0, columns, span):
            where = (slice(top, top + height), slice(side, side + span))
            label = fields[(3,) + where]

            def pick(sample, held):
                here = label == sample.astype(f32)
                return tuple(jnp.where(here, table_ref[sample, c], held[c]) for c in range(8))

            zero = jnp.zeros((height, span), f32)
            held = lax.fori_loop(0, samples, pick, (zero,) * 8, unroll=4)
            for c in range(8):
                cells[(c,) + where] = held[c]
    stencil = Stencil(fields.shape[1:], vox_width(columns))
    stress = [cells[c] for c in range(6)]
    pulled = stencil.force(stress)
    remainder = [forces[b] - pulled[b] - spring_rate * fields[b] for b in range(3)]
    direction = remainder
    norm_now = total(sum(r * r for r in remainder))
    update = None
    lame = cells[6]
    shear = 2.0 * cells[7]
    for turn in range(CG_STEPS):
        strain = stencil.strain(direction)
        pressure = lame * (strain[0] + strain[1] + strain[2])
        stress = [shear * strain[i] + pressure for i in range(3)] + [shear * strain[i] for i in range(3, 6)]
        pulled = stencil.force(stress)
        image = [pulled[b] + spring_rate * direction[b] for b in range(3)]
        alpha = norm_now / total(sum(direction[b] * image[b] for b in range(3)))
        moved = [alpha * direction[b] for b in range(3)]
        update = moved if update is None else [update[b] + moved[b] for b in range(3)]
        if turn + 1 < CG_STEPS:
            remainder = [remainder[b] - alpha * image[b] for b in range(3)]
            norm_next = total(sum(r * r for r in remainder))
            grow = norm_next / norm_now
            direction = [remainder[b] + grow * direction[b] for b in range(3)]
            norm_now = norm_next
    for b in range(3):
        done = fields[b] + update[b]
        for device in range(devices):
            result[device, b] = done[device * planes : (device + 1) * planes]
    next_ref[...] = result[rank]


def vmem():
    return pl.BlockSpec(memory_space=pltpu.VMEM)


def smem():
    return pl.BlockSpec(memory_space=pltpu.SMEM)


def shards(
    displacement, external_force, element_sample, lame_field, shear_field, plastic_steps, owner_slot
):
    group_size, planes, columns = lame_field.shape
    devices = lax.axis_size("dev")
    groups = lax.axis_size("grp")
    local_count = group_size // devices
    vox = planes * devices
    layers = displacement.shape[1]
    width = displacement.shape[2] * displacement.shape[3]
    plane, forward_line, backward_line, multipliers = tables(vox)
    params = pltpu.CompilerParams(vmem_limit_bytes=48 * 1024 * 1024)

    def spread(block):
        return lax.all_to_all(
            jnp.broadcast_to(block[None], (devices,) + block.shape), "dev", split_axis=0, concat_axis=0, tiled=True
        )

    mesh_part = jnp.concatenate([displacement, element_sample[None].astype(f32)]).reshape(4, layers, width)
    mesh_all = spread(mesh_part)
    force_all = spread(external_force.reshape(3, layers, width))
    moduli = []
    for field in (lame_field, shear_field):
        own = lax.all_to_all(
            field.reshape(devices, local_count, planes, columns), "dev", split_axis=0, concat_axis=0, tiled=True
        )
        moduli.append(own)
    strains = []
    rows = []
    for local in range(local_count):
        lame_own, shear_own = (field[:, local].reshape(vox, columns) for field in moduli)
        strain, response = pl.pallas_call(
            functools.partial(micro_kernel, local, local_count),
            name="micro",
            out_shape=(
                jax.ShapeDtypeStruct((devices, 6, planes, columns), f32),
                jax.ShapeDtypeStruct((1, 8), f32),
            ),
            in_specs=[smem()] + [vmem()] * 6 + [pl.BlockSpec(memory_space=pl.ANY)],
            out_specs=(vmem(), vmem()),
            scratch_shapes=[
                pltpu.VMEM((4, devices * layers, width), f32),
                pltpu.VMEM(plane.shape, bf16),
                pltpu.SemaphoreType.DMA((2,)),
                pltpu.VMEM((6 * vox, columns), f32),
            ],
            compiler_params=params,
        )(plastic_steps, mesh_all, lame_own, shear_own, multipliers, forward_line, backward_line, plane)
        strains.append(strain)
        rows.append(response)
    own_rows = rows[0] if local_count == 1 else jnp.concatenate(rows)
    everyone = groups * devices
    gathered = lax.all_to_all(
        jnp.broadcast_to(own_rows[None], (everyone,) + own_rows.shape),
        ("grp", "dev"), split_axis=0, concat_axis=0, tiled=True,
    ).reshape(everyone * local_count, 8)
    sent = jnp.stack(strains, axis=1)
    moved = lax.all_to_all(sent, "dev", split_axis=0, concat_axis=0, tiled=True)
    micro_strain = jnp.transpose(moved, (2, 0, 1, 3, 4)).reshape(6, group_size, planes, columns)
    following, picked = pl.pallas_call(
        macro_kernel,
        name="macro",
        out_shape=(
            jax.ShapeDtypeStruct((3, layers, width), f32),
            jax.ShapeDtypeStruct((local_count, 8), f32),
        ),
        in_specs=[smem(), smem()] + [vmem()] * 3,
        out_specs=(vmem(), vmem()),
        scratch_shapes=[
            pltpu.VMEM((4, devices * layers, width), f32),
            pltpu.VMEM((3, devices * layers, width), f32),
            pltpu.VMEM((8, devices * layers, width), f32),
            pltpu.VMEM((devices, 3, layers, width), f32),
        ],
        compiler_params=params,
    )(owner_slot, gathered, gathered, mesh_all, force_all)
    return (following.reshape(displacement.shape), picked, micro_strain)


def solution(mesh):
    in_specs = (
        P(None, "dev", None, None),
        P(None, "dev", None, None),
        P("dev", None, None),
        P("grp", "dev", None),
        P("grp", "dev", None),
        P(),
        P(),
    )
    out_specs = (P(None, "dev", None, None), P(("grp", "dev"), None), P(None, "grp", "dev", None))
    return jax.shard_map(shards, mesh=mesh, in_specs=in_specs, out_specs=out_specs, check_vma=False)
```

```python
import functools
import jax
import jax.numpy as jnp
import numpy as np
from jax import lax
from jax.experimental import pallas as pl
from jax.experimental.pallas import tpu as pltpu
from jax.sharding import PartitionSpec as P

CG_STEPS = 3
shear_ref = 1.65
lame_ref = 1.25
green_ratio = (lame_ref + shear_ref) / (lame_ref + 2.0 * shear_ref)
relax_rate = 0.35
flow_scale = 4.0
spring_rate = 0.2
f32 = jnp.float32
bf16 = jnp.bfloat16
DIAG = ((0, 0), (1, 1), (2, 2))
PAIRS = ((0, 0), (1, 1), (2, 2), (1, 2), (0, 2), (0, 1))
SLOT = {(0, 0): 0, (1, 1): 1, (2, 2): 2, (1, 2): 3, (2, 1): 3, (0, 2): 4, (2, 0): 4, (0, 1): 5, (1, 0): 5}


def split_table(table):
    high = table.astype(np.float32).astype(bf16)
    low = (table - high.astype(np.float64)).astype(np.float32).astype(bf16)
    return np.stack([high, low])


def tables(vox):
    half = vox // 2
    n = np.arange(vox)[:, None]
    k = np.arange(half)[None, :]
    angle = 2.0 * np.pi * (n * k % vox) / vox
    cosine = np.cos(angle) * np.sqrt(2.0 / vox)
    sine = np.sin(angle) * np.sqrt(2.0 / vox)
    cosine[:, 0] = 1.0 / np.sqrt(vox)
    sine[:, 0] = (1.0 - 2.0 * (np.arange(vox) % 2)) / np.sqrt(vox)
    basis = np.concatenate([cosine, sine], axis=1)
    by_parity = basis.reshape(vox, 2, half)
    plane = np.einsum("ypk,zql->yzqpkl", by_parity, by_parity).reshape(vox * vox, vox * vox)
    line = basis.T
    forward_line = np.kron(np.eye(2), line)
    backward_line = np.kron(np.eye(6), line.T)
    wave = np.sin(2.0 * np.pi * np.arange(half) / vox)
    wave[0] = 0.0
    first = np.broadcast_to(wave[:, None, None], (half, half, half))
    second = np.broadcast_to(wave[None, :, None], (half, half, half))
    third = np.broadcast_to(wave[None, None, :], (half, half, half))
    square = first**2 + second**2 + third**2
    inverse = np.where(square > 0.0, 1.0 / np.where(square > 0.0, square, 1.0), 0.0)
    waves = (first, second, third)
    products = [waves[a] * waves[b] for a, b in PAIRS]
    rows = products + [inverse / shear_ref, green_ratio * inverse]
    multipliers = np.stack(rows).reshape(len(rows), half, half * half).astype(np.float32)
    return split_table(plane), split_table(forward_line), split_table(backward_line), multipliers


def split(value):
    high = value.astype(bf16)
    return high, (value - high.astype(f32)).astype(bf16)


def dot(left, right):
    return lax.dot_general(left, right, (((1,), (0,)), ((), ())), preferred_element_type=f32)


def dot_t(left, right):
    return lax.dot_general(left, right, (((1,), (1,)), ((), ())), preferred_element_type=f32)


def by_table(value, high, low, contract):
    rows = value.shape[0]
    value_high, value_low = split(value)
    both = contract(jnp.concatenate([value_high, value_low], axis=0), high)
    return both[:rows] + both[rows:] + contract(value_high, low)


def table_by(high, low, value):
    rows = high.shape[0]
    value_high, value_low = split(value)
    both = dot(jnp.concatenate([high, low], axis=0), value_high)
    return both[:rows] + both[rows:] + dot(high, value_low)


def lane_position(shape):
    return lax.broadcasted_iota(jnp.int32, shape, 1)


def row_position(shape):
    return lax.broadcasted_iota(jnp.int32, shape, 0)


class Stencil:
    def __init__(self, shape, width, devices):
        self.rows, self.columns = shape
        self.width = width
        self.devices = devices
        lane = lane_position(shape)
        row = row_position((devices, self.columns))
        self.last_z = lane % width == width - 1
        self.first_z = lane % width == 0
        self.last_y = lane >= self.columns - width
        self.first_y = lane < width
        self.last_x = row == devices - 1
        self.first_x = row == 0

    def up_z(self, v):
        return jnp.where(self.last_z, 0.0, pltpu.roll(v, self.columns - 1, 1))

    def up_y(self, v):
        return jnp.where(self.last_y, 0.0, pltpu.roll(v, self.columns - self.width, 1))

    def up_x(self, v):
        wrapped = jnp.where(self.last_x, 0.0, pltpu.roll(v[: self.devices], self.devices - 1, 0))
        return jnp.concatenate([v[self.devices :], wrapped], axis=0)

    def down_z(self, v):
        return jnp.where(self.first_z, 0.0, pltpu.roll(v, 1, 1))

    def down_y(self, v):
        return jnp.where(self.first_y, 0.0, pltpu.roll(v, self.width, 1))

    def down_x(self, v):
        wrapped = jnp.where(self.first_x, 0.0, pltpu.roll(v[self.rows - self.devices :], 1, 0))
        return jnp.concatenate([wrapped, v[: self.rows - self.devices]], axis=0)

    def strain(self, field):
        slopes = []
        for v in field:
            next_z = self.up_z(v)
            sum_z = v + next_z
            dif_z = next_z - v
            next_y = self.up_y(sum_z)
            sums = sum_z + next_y
            along_y = next_y - sum_z
            along_z = dif_z + self.up_y(dif_z)
            slopes.append((self.up_x(sums) - sums, along_y + self.up_x(along_y), along_z + self.up_x(along_z)))
        return [
            0.25 * slopes[0][0],
            0.25 * slopes[1][1],
            0.25 * slopes[2][2],
            0.125 * (slopes[2][1] + slopes[1][2]),
            0.125 * (slopes[2][0] + slopes[0][2]),
            0.125 * (slopes[1][0] + slopes[0][1]),
        ]

    def force(self, stress):
        result = []
        for b in range(3):
            along_x, along_y, along_z = (stress[SLOT[(a, b)]] for a in range(3))
            sum_x = along_x + self.down_z(along_x)
            first = sum_x + self.down_y(sum_x)
            sum_y = along_y + self.down_z(along_y)
            dif_z = self.down_z(along_z) - along_z
            back = self.down_y(sum_y)
            rest = (back - sum_y) + (dif_z + self.down_y(dif_z))
            result.append(0.25 * ((self.down_x(first) - first) + (rest + self.down_x(rest))))
        return result


def total(value):
    return jnp.sum(jnp.sum(value, axis=0, keepdims=True), axis=1, keepdims=True)


def measure(stress):
    return (
        stress[0] * stress[0]
        + stress[1] * stress[1]
        + stress[2] * stress[2]
        + 2.0 * (stress[3] * stress[3] + stress[4] * stress[4] + stress[5] * stress[5])
    )


def remaining(shear, size, steps, most):
    stiff = (2.0 * shear) * (2.0 * shear) * size

    def relax(count, left):
        ratio = stiff * left * left
        return left * ((1.0 - relax_rate) + relax_rate / (1.0 + ratio))

    left = lax.fori_loop(0, steps, relax, jnp.ones_like(stiff))
    return left, stiff * left * left


def deviator_of(strain):
    trace = strain[0] + strain[1] + strain[2]
    third = trace / 3.0
    return trace, [strain[0] - third, strain[1] - third, strain[2] - third] + list(strain[3:])


LAME_UNIT = 2.0**8
SHEAR_UNIT = 2.0**9
CODE_BASE = 2.0**11
LABEL_BASE = 2.0**12
LANES = 128


def encode(lame, shear):
    return (lame.astype(f32) * LAME_UNIT) * CODE_BASE + shear.astype(f32) * SHEAR_UNIT


def decode(code):
    high = jnp.floor(code * (1.0 / CODE_BASE))
    return high * (1.0 / LAME_UNIT), (code - high * CODE_BASE) * (1.0 / SHEAR_UNIT)


def pack_kernel(layers, moved_ref, force_ref, sample_ref, lame_ref, shear_ref, packet_ref, wide):
    devices, local_count, planes, columns = lame_ref.shape
    tiles = columns // LANES
    for device in range(devices):
        for local in range(local_count):
            code = encode(lame_ref[device, local], shear_ref[device, local])
            for tile in range(tiles):
                packet_ref[device, pl.ds(local * planes * tiles + tile, planes, stride=tiles), :] = code[
                    :, tile * LANES : (tile + 1) * LANES
                ]
    width = moved_ref.shape[1]
    beside = LANES // width
    start = 0
    for ref in (moved_ref, force_ref, sample_ref):
        rows = ref.shape[0]
        wide[start : start + rows, :] = jnp.concatenate([ref[...].astype(f32)] * beside, axis=1)
        start += rows
    count = start // beside
    slot = lane_position((count, LANES)) // width
    merged = wide[pl.ds(0, count, stride=beside), :]
    for place in range(1, beside):
        merged = jnp.where(slot == place, wide[pl.ds(place, count, stride=beside), :], merged)
    nodes = 6 * count // 7
    each = (count - nodes) // layers
    base = local_count * planes * tiles
    for device in range(devices):
        packet_ref[device, base : base + nodes, :] = merged[:nodes]
    for pair in range((layers + 1) // 2):
        first = merged[nodes + 2 * pair * each : nodes + (2 * pair + 1) * each]
        if 2 * pair + 1 < layers:
            first = first * LABEL_BASE + merged[nodes + (2 * pair + 1) * each : nodes + (2 * pair + 2) * each]
        else:
            first = first * LABEL_BASE
        for device in range(devices):
            packet_ref[device, base + nodes + pair * each : base + nodes + (pair + 1) * each, :] = first


def read_fields(packet_ref, base, layers, fields):
    parts, rows, columns = fields.shape
    devices = rows // layers
    tiles = columns // LANES
    step = packet_ref.shape[0] // devices
    for part in range(parts):
        for layer in range(layers):
            for tile in range(tiles):
                if part < 6:
                    at = base + (part * layers + layer) * tiles + tile
                    piece = packet_ref[pl.ds(at, devices, stride=step), :]
                else:
                    at = base + (6 * layers + layer // 2) * tiles + tile
                    both = packet_ref[pl.ds(at, devices, stride=step), :]
                    high = jnp.floor(both * (1.0 / LABEL_BASE))
                    piece = high if layer % 2 == 0 else both - high * LABEL_BASE
                fields[part, layer * devices : (layer + 1) * devices, tile * LANES : (tile + 1) * LANES] = piece


def micro_kernel(
    local, local_count, layers, steps_ref, packet_ref, mult_hbm, fwd_hbm, bwd_hbm, table_hbm,
    sent_ref, response_ref, fields, moduli, mult_ref, fwd_ref, bwd_ref, table, spectrum, ordered, sem
):
    devices, planes = sent_ref.shape[0], sent_ref.shape[1] // 6
    vox, columns = moduli.shape[1:]
    half = vox // 2
    quarter = half * half
    width = vox_width(fields.shape[2])
    pairs = [(mult_hbm, mult_ref), (fwd_hbm, fwd_ref), (bwd_hbm, bwd_ref)]
    pieces = sem.shape[0] - len(pairs)
    height = columns // (pieces // 2)
    for piece in range(pieces):
        where = (piece * height // columns, pl.ds(piece * height % columns, height))
        pairs.append((table_hbm.at[where], table.at[where]))
    copies = [pltpu.make_async_copy(source, target, sem.at[i]) for i, (source, target) in enumerate(pairs)]
    for copy in copies:
        copy.start()
    own = (lax.axis_index("grp") * lax.axis_size("dev") + lax.axis_index("dev")) * local_count + local
    steps = steps_ref[own]
    tiles = columns // LANES
    step = packet_ref.shape[0] // devices
    read_fields(packet_ref, local_count * planes * tiles, layers, fields)
    for device in range(devices):
        for tile in range(tiles):
            at = device * step + local * planes * tiles + tile
            code = packet_ref[pl.ds(at, planes, stride=tiles), :]
            for kind, value in enumerate(decode(code)):
                moduli[
                    kind, device * planes : (device + 1) * planes, tile * LANES : (tile + 1) * LANES
                ] = value
    stencil = Stencil(fields.shape[1:], width, fields.shape[1] // layers)
    mesh_strain = stencil.strain([fields[c] for c in range(3)])
    mine = fields[6] == own.astype(f32)
    count = total(jnp.where(mine, 1.0, 0.0))
    load = [total(jnp.where(mine, part, 0.0)) / count for part in mesh_strain]
    trace, dev = deviator_of(load)
    lame = moduli[0]
    shear = moduli[1]
    size = measure([0.5 * part for part in dev])
    left, _ = remaining(shear, jnp.broadcast_to(size, shear.shape), steps, 4)
    bulk = lame + (2.0 / 3.0) * shear
    sources = jnp.concatenate([bulk * trace, 2.0 * shear * left], axis=0)
    for copy in copies:
        copy.wait()
    spectral = table_by(fwd_ref[0], fwd_ref[1], by_table(sources, table[0], table[1], dot))

    def block(field, px, py, pz):
        rows = slice(field * vox + px * half, field * vox + (px + 1) * half)
        lanes = slice((pz * 2 + py) * quarter, (pz * 2 + py + 1) * quarter)
        return rows, lanes

    parities = [(px, py, pz) for px in range(2) for py in range(2) for pz in range(2)]
    product = [mult_ref[i] for i in range(6)]
    inverse = mult_ref[6]
    scaled = mult_ref[7]

    def second(blocks, parity, a, b):
        if a == b:
            return -(product[SLOT[(a, b)]] * blocks[parity])
        other = tuple(1 - p if axis in (a, b) else p for axis, p in enumerate(parity))
        value = product[SLOT[(a, b)]] * blocks[other]
        return value if parity[a] == parity[b] else -value

    psi = {}
    raw = {}
    for parity in parities:
        rows, lanes = block(1, *parity)
        raw[parity] = spectral[rows, lanes]
        psi[parity] = inverse * raw[parity]
    phi = {}
    for parity in parities:
        rows, lanes = block(0, *parity)
        pressed = sum(
            (1.0 if a == b else 2.0) * dev[SLOT[(a, b)]] * second(psi, parity, a, b) for a, b in PAIRS
        )
        phi[parity] = (1.0 - green_ratio) * inverse * spectral[rows, lanes] + scaled * pressed
    for parity in parities:
        curl = {pair: second(psi, parity, *pair) for pair in PAIRS}
        for index, (a, b) in enumerate(PAIRS):
            def at(i, j):
                return curl[(min(i, j), max(i, j))]
            if a == b:
                sheared = sum(dev[SLOT[(b, c)]] * at(a, c) for c in range(3))
            else:
                sheared = 0.5 * sum(dev[SLOT[(b, c)]] * at(a, c) + dev[SLOT[(a, c)]] * at(b, c) for c in range(3))
            rows, lanes = block(index, *parity)
            spectrum[rows, lanes] = second(phi, parity, a, b) + sheared
    moved = table_by(bwd_ref[0], bwd_ref[1], by_table(spectrum[...], table[0], table[1], dot_t))
    if 2 * planes == 8:
        low = row_position((2 * planes, columns)) < planes
        for pair in range(3):
            for chip in range(devices // 2):
                first, second_ = (
                    moved[i * vox + 2 * chip * planes : i * vox + 2 * (chip + 1) * planes]
                    for i in (2 * pair, 2 * pair + 1)
                )
                rows = slice(2 * pair * planes, 2 * (pair + 1) * planes)
                ordered[2 * chip, rows] = jnp.where(low, first, pltpu.roll(second_, planes, 0))
                ordered[2 * chip + 1, rows] = jnp.where(low, pltpu.roll(first, planes, 0), second_)
    else:
        for i in range(6):
            for device in range(devices):
                ordered[device, i * planes : (i + 1) * planes] = moved[
                    i * vox + device * planes : i * vox + (device + 1) * planes
                ]
    for device in range(devices):
        sent_ref[device] = ordered[device].astype(bf16)
    strain = [load[i] + moved[i * vox : (i + 1) * vox] for i in range(6)]
    trace, dev = deviator_of(strain)
    left, ratio = remaining(shear, measure([0.5 * part for part in dev]), steps, 4)
    push = bulk * trace
    pull = 2.0 * shear * left
    stress = [push + pull * dev[i] for i in range(3)] + [pull * dev[i] for i in range(3, 6)]
    parts = stress + [lame, shear / (1.0 + ratio)]
    lane = lane_position((1, response_ref.shape[1]))
    row = jnp.zeros(lane.shape, f32)
    for index, part in enumerate(parts):
        row = jnp.where(lane == index, total(part) / float(vox * columns), row)
    for index, part in enumerate(load):
        row = jnp.where(lane == 8 + index, part, row)
    response_ref[...] = jnp.broadcast_to(row, response_ref.shape)


def vox_width(columns):
    width = int(round(columns**0.5))
    return width


def macro_kernel(
    layers, base, slots_ref, table_ref, table_v_ref, packet_ref, next_ref, row_ref, fields, cells, result
):
    columns = next_ref.shape[2]
    devices = fields.shape[1] // layers
    samples = table_v_ref.shape[0]
    rank = lax.axis_index("dev")
    group = lax.axis_index("grp")
    local_count = row_ref.shape[0]
    group_size = local_count * devices
    start = group * group_size
    for local in range(local_count):
        chosen = jnp.int32(0)
        for j in range(group_size):
            chosen = jnp.where(slots_ref[start + j] == rank * local_count + local, start + j, chosen)
        row_ref[local : local + 1, :] = table_v_ref[pl.ds(chosen, 1), 0:8]
    read_fields(packet_ref, base, layers, fields)
    rows = fields.shape[1]
    height = min(8, rows)
    span = min(512, columns)
    for top in range(0, rows, height):
        for side in range(0, columns, span):
            where = (slice(top, top + height), slice(side, side + span))
            label = fields[(6,) + where]

            def pick(sample, held):
                here = label == sample.astype(f32)
                return tuple(jnp.where(here, table_ref[sample, c], held[c]) for c in range(8))

            zero = jnp.zeros((height, span), f32)
            held = lax.fori_loop(0, samples, pick, (zero,) * 8, unroll=4)
            for c in range(8):
                cells[(c,) + where] = held[c]
    stencil = Stencil(fields.shape[1:], vox_width(columns), devices)
    stress = [cells[c] for c in range(6)]
    pulled = stencil.force(stress)
    remainder = [fields[3 + b] - pulled[b] - spring_rate * fields[b] for b in range(3)]
    direction = remainder
    norm_now = total(sum(r * r for r in remainder))
    update = None
    lame = cells[6]
    shear = 2.0 * cells[7]
    for turn in range(CG_STEPS):
        strain = stencil.strain(direction)
        pressure = lame * (strain[0] + strain[1] + strain[2])
        stress = [shear * strain[i] + pressure for i in range(3)] + [shear * strain[i] for i in range(3, 6)]
        pulled = stencil.force(stress)
        image = [pulled[b] + spring_rate * direction[b] for b in range(3)]
        alpha = norm_now / total(sum(direction[b] * image[b] for b in range(3)))
        moved = [alpha * direction[b] for b in range(3)]
        update = moved if update is None else [update[b] + moved[b] for b in range(3)]
        if turn + 1 < CG_STEPS:
            remainder = [remainder[b] - alpha * image[b] for b in range(3)]
            norm_next = total(sum(r * r for r in remainder))
            grow = norm_next / norm_now
            direction = [remainder[b] + grow * direction[b] for b in range(3)]
            norm_now = norm_next
    for b in range(3):
        done = fields[b] + update[b]
        result[b] = done
        for layer in range(layers):
            next_ref[b, layer : layer + 1, :] = result[b, pl.ds(layer * devices + rank, 1), :]


def vmem():
    return pl.BlockSpec(memory_space=pltpu.VMEM)


def smem():
    return pl.BlockSpec(memory_space=pltpu.SMEM)


def shards(
    displacement, external_force, element_sample, lame_field, shear_field, plastic_steps, owner_slot
):
    group_size, planes, columns = lame_field.shape
    devices = lax.axis_size("dev")
    groups = lax.axis_size("grp")
    local_count = group_size // devices
    vox = planes * devices
    layers = displacement.shape[1]
    width = displacement.shape[2] * displacement.shape[3]
    plane, forward_line, backward_line, multipliers = tables(vox)
    params = pltpu.CompilerParams(vmem_limit_bytes=60 * 1024 * 1024)

    side = displacement.shape[3]
    lines = layers * displacement.shape[2]
    tiles = columns // LANES
    base = local_count * planes * tiles
    length = base + (6 * layers + (layers + 1) // 2) * tiles
    packet = pl.pallas_call(
        functools.partial(pack_kernel, layers),
        name="pack",
        out_shape=jax.ShapeDtypeStruct((devices, length, LANES), f32),
        in_specs=[vmem()] * 5,
        out_specs=vmem(),
        scratch_shapes=[pltpu.VMEM((7 * lines, LANES), f32)],
        compiler_params=params,
    )(
        displacement.reshape(3 * lines, side), external_force.reshape(3 * lines, side),
        element_sample.reshape(lines, side),
        lame_field.reshape(devices, local_count, planes, columns),
        shear_field.reshape(devices, local_count, planes, columns),
    )
    packets = lax.all_to_all(packet, "dev", split_axis=0, concat_axis=0, tiled=True).reshape(devices * length, LANES)
    everyone = groups * devices
    sents = []
    rows = []
    for local in range(local_count):
        sent, response = pl.pallas_call(
            functools.partial(micro_kernel, local, local_count, layers),
            name="micro",
            out_shape=(
                jax.ShapeDtypeStruct((devices, 6 * planes, columns), bf16),
                jax.ShapeDtypeStruct((everyone, 16), f32),
            ),
            in_specs=[smem(), vmem()] + [pl.BlockSpec(memory_space=pltpu.HBM)] * 4,
            out_specs=(vmem(), vmem()),
            scratch_shapes=[
                pltpu.VMEM((7, devices * layers, width), f32),
                pltpu.VMEM((2, vox, columns), f32),
                pltpu.VMEM(multipliers.shape, f32),
                pltpu.VMEM(forward_line.shape, bf16),
                pltpu.VMEM(backward_line.shape, bf16),
                pltpu.VMEM(plane.shape, bf16),
                pltpu.VMEM((6 * vox, columns), f32),
                pltpu.VMEM((devices, 6 * planes, columns), f32),
                pltpu.SemaphoreType.DMA((3 + 16,)),
            ],
            compiler_params=params,
        )(
            plastic_steps, packets, multipliers, forward_line, backward_line, plane,
        )
        sents.append(sent)
        rows.append(response)
    gathered = lax.all_to_all(
        jnp.stack(rows, axis=1), ("grp", "dev"), split_axis=0, concat_axis=0, tiled=True
    ).reshape(everyone * local_count, 16)
    moved = lax.all_to_all(jnp.stack(sents, axis=1), "dev", split_axis=0, concat_axis=0, tiled=True)
    group_rows = lax.dynamic_slice_in_dim(gathered, lax.axis_index("grp") * group_size, group_size)
    loads = group_rows[:, 8:14].T
    change = jnp.transpose(moved.reshape(group_size, 6, planes, columns), (1, 0, 2, 3))
    micro_strain = loads[:, :, None, None] + change.astype(f32)
    following, picked = pl.pallas_call(
        functools.partial(macro_kernel, layers, base),
        name="macro",
        out_shape=(
            jax.ShapeDtypeStruct((3, layers, width), f32),
            jax.ShapeDtypeStruct((local_count, 8), f32),
        ),
        in_specs=[smem(), smem()] + [vmem()] * 2,
        out_specs=(vmem(), vmem()),
        scratch_shapes=[
            pltpu.VMEM((7, devices * layers, width), f32),
            pltpu.VMEM((8, devices * layers, width), f32),
            pltpu.VMEM((3, devices * layers, width), f32),
        ],
        compiler_params=params,
    )(owner_slot, gathered, gathered, packets)
    return (following.reshape(displacement.shape), picked, micro_strain)


def solution(mesh):
    in_specs = (
        P(None, "dev", None, None),
        P(None, "dev", None, None),
        P("dev", None, None),
        P("grp", "dev", None),
        P("grp", "dev", None),
        P(),
        P(),
    )
    out_specs = (P(None, "dev", None, None), P(("grp", "dev"), None), P(None, "grp", "dev", None))
    return jax.shard_map(shards, mesh=mesh, in_specs=in_specs, out_specs=out_specs, check_vma=False)
```

```python
import functools
import jax
import jax.numpy as jnp
import numpy as np
from jax import lax
from jax.experimental import pallas as pl
from jax.experimental.pallas import tpu as pltpu
from jax.sharding import PartitionSpec as P

CG_STEPS = 3
shear_ref = 1.65
lame_ref = 1.25
green_ratio = (lame_ref + shear_ref) / (lame_ref + 2.0 * shear_ref)
relax_rate = 0.35
flow_scale = 4.0
spring_rate = 0.2
f32 = jnp.float32
bf16 = jnp.bfloat16
DIAG = ((0, 0), (1, 1), (2, 2))
PAIRS = ((0, 0), (1, 1), (2, 2), (1, 2), (0, 2), (0, 1))
SLOT = {(0, 0): 0, (1, 1): 1, (2, 2): 2, (1, 2): 3, (2, 1): 3, (0, 2): 4, (2, 0): 4, (0, 1): 5, (1, 0): 5}


def split_table(table):
    high = table.astype(np.float32).astype(bf16)
    low = (table - high.astype(np.float64)).astype(np.float32).astype(bf16)
    return np.stack([high, low])


def tables(vox):
    half = vox // 2
    n = np.arange(vox)[:, None]
    k = np.arange(half)[None, :]
    angle = 2.0 * np.pi * (n * k % vox) / vox
    cosine = np.cos(angle) * np.sqrt(2.0 / vox)
    sine = np.sin(angle) * np.sqrt(2.0 / vox)
    cosine[:, 0] = 1.0 / np.sqrt(vox)
    sine[:, 0] = (1.0 - 2.0 * (np.arange(vox) % 2)) / np.sqrt(vox)
    basis = np.concatenate([cosine, sine], axis=1)
    order = np.concatenate([np.arange(0, half, 2), np.arange(1, half, 2)])
    by_parity = basis.reshape(vox, 2, half)
    folded = by_parity[:half, :, order].reshape(half, 2, 2, half // 2)
    plane = np.einsum("ypek,zql->eyzqpkl", folded, by_parity).reshape(2, half * vox, half * vox)
    line = basis.T
    forward_line = np.kron(np.eye(2), line)
    backward_line = np.kron(np.eye(6), line.T)
    wave = np.sin(2.0 * np.pi * np.arange(half) / vox)
    wave[0] = 0.0
    first = np.broadcast_to(wave[:, None, None], (half, half, half))
    second = np.broadcast_to(wave[order][None, :, None], (half, half, half))
    third = np.broadcast_to(wave[None, None, :], (half, half, half))
    square = first**2 + second**2 + third**2
    inverse = np.where(square > 0.0, 1.0 / np.where(square > 0.0, square, 1.0), 0.0)
    waves = (first, second, third)
    products = [waves[a] * waves[b] for a, b in PAIRS]
    rows = products + [inverse / shear_ref, green_ratio * inverse]
    multipliers = np.stack(rows).reshape(len(rows), half, half * half).astype(np.float32)
    return split_table(plane), split_table(forward_line), split_table(backward_line), multipliers


def split(value):
    high = value.astype(bf16)
    return high, (value - high.astype(f32)).astype(bf16)


def dot(left, right):
    return lax.dot_general(left, right, (((1,), (0,)), ((), ())), preferred_element_type=f32)


def dot_t(left, right):
    return lax.dot_general(left, right, (((1,), (1,)), ((), ())), preferred_element_type=f32)


def by_table(value, high, low, contract):
    rows = value.shape[0]
    value_high, value_low = split(value)
    both = contract(jnp.concatenate([value_high, value_low], axis=0), high)
    return both[:rows] + both[rows:] + contract(value_high, low)


def table_by(high, low, value):
    rows = high.shape[0]
    value_high, value_low = split(value)
    both = dot(jnp.concatenate([high, low], axis=0), value_high)
    return both[:rows] + both[rows:] + dot(high, value_low)


def forward_plane(value, table):
    half = value.shape[1] // 2
    low, high = value[:, :half], value[:, half:]
    even = by_table(low + high, table[0, 0], table[1, 0], dot)
    odd = by_table(low - high, table[0, 1], table[1, 1], dot)
    return jnp.concatenate([even, odd], axis=1)


def backward_plane(value, table):
    half = value.shape[1] // 2
    even = by_table(value[:, :half], table[0, 0], table[1, 0], dot_t)
    odd = by_table(value[:, half:], table[0, 1], table[1, 1], dot_t)
    return jnp.concatenate([even + odd, even - odd], axis=1)


def lane_position(shape):
    return lax.broadcasted_iota(jnp.int32, shape, 1)


def row_position(shape):
    return lax.broadcasted_iota(jnp.int32, shape, 0)


class Stencil:
    def __init__(self, shape, width, devices):
        self.rows, self.columns = shape
        self.width = width
        self.devices = devices
        lane = lane_position(shape)
        row = row_position((devices, self.columns))
        self.last_z = lane % width == width - 1
        self.first_z = lane % width == 0
        self.last_y = lane >= self.columns - width
        self.first_y = lane < width
        self.last_x = row == devices - 1
        self.first_x = row == 0

    def up_z(self, v):
        return jnp.where(self.last_z, 0.0, pltpu.roll(v, self.columns - 1, 1))

    def up_y(self, v):
        return jnp.where(self.last_y, 0.0, pltpu.roll(v, self.columns - self.width, 1))

    def up_x(self, v):
        wrapped = jnp.where(self.last_x, 0.0, pltpu.roll(v[: self.devices], self.devices - 1, 0))
        return jnp.concatenate([v[self.devices :], wrapped], axis=0)

    def down_z(self, v):
        return jnp.where(self.first_z, 0.0, pltpu.roll(v, 1, 1))

    def down_y(self, v):
        return jnp.where(self.first_y, 0.0, pltpu.roll(v, self.width, 1))

    def down_x(self, v):
        wrapped = jnp.where(self.first_x, 0.0, pltpu.roll(v[self.rows - self.devices :], 1, 0))
        return jnp.concatenate([wrapped, v[: self.rows - self.devices]], axis=0)

    def strain(self, field):
        slopes = []
        for v in field:
            next_z = self.up_z(v)
            sum_z = v + next_z
            dif_z = next_z - v
            next_y = self.up_y(sum_z)
            sums = sum_z + next_y
            along_y = next_y - sum_z
            along_z = dif_z + self.up_y(dif_z)
            slopes.append((self.up_x(sums) - sums, along_y + self.up_x(along_y), along_z + self.up_x(along_z)))
        return [
            0.25 * slopes[0][0],
            0.25 * slopes[1][1],
            0.25 * slopes[2][2],
            0.125 * (slopes[2][1] + slopes[1][2]),
            0.125 * (slopes[2][0] + slopes[0][2]),
            0.125 * (slopes[1][0] + slopes[0][1]),
        ]

    def force(self, stress):
        result = []
        for b in range(3):
            along_x, along_y, along_z = (stress[SLOT[(a, b)]] for a in range(3))
            sum_x = along_x + self.down_z(along_x)
            first = sum_x + self.down_y(sum_x)
            sum_y = along_y + self.down_z(along_y)
            dif_z = self.down_z(along_z) - along_z
            back = self.down_y(sum_y)
            rest = (back - sum_y) + (dif_z + self.down_y(dif_z))
            result.append(0.25 * ((self.down_x(first) - first) + (rest + self.down_x(rest))))
        return result


def total(value):
    return jnp.sum(jnp.sum(value, axis=0, keepdims=True), axis=1, keepdims=True)


def measure(stress):
    return (
        stress[0] * stress[0]
        + stress[1] * stress[1]
        + stress[2] * stress[2]
        + 2.0 * (stress[3] * stress[3] + stress[4] * stress[4] + stress[5] * stress[5])
    )


def remaining(shear, size, steps, most):
    stiff = (2.0 * shear) * (2.0 * shear) * size

    def relax(count, left):
        ratio = stiff * left * left
        return left * ((1.0 - relax_rate) + relax_rate / (1.0 + ratio))

    left = lax.fori_loop(0, steps, relax, jnp.ones_like(stiff))
    return left, stiff * left * left


def deviator_of(strain):
    trace = strain[0] + strain[1] + strain[2]
    third = trace / 3.0
    return trace, [strain[0] - third, strain[1] - third, strain[2] - third] + list(strain[3:])


LAME_UNIT = 2.0**8
SHEAR_UNIT = 2.0**9
CODE_BASE = 2.0**11
LABEL_BASE = 2.0**12
LANES = 128


def encode(lame, shear):
    return (lame.astype(f32) * LAME_UNIT) * CODE_BASE + shear.astype(f32) * SHEAR_UNIT


def decode(code):
    high = jnp.floor(code * (1.0 / CODE_BASE))
    return high * (1.0 / LAME_UNIT), (code - high * CODE_BASE) * (1.0 / SHEAR_UNIT)


def pack_kernel(layers, moved_ref, sample_ref, force_ref, lame_ref, shear_ref, packet_ref, wide):
    devices, local_count, planes, columns = lame_ref.shape
    tiles = columns // LANES
    for device in range(devices):
        for local in range(local_count):
            code = encode(lame_ref[device, local], shear_ref[device, local])
            for tile in range(tiles):
                packet_ref[device, pl.ds(local * planes * tiles + tile, planes, stride=tiles), :] = code[
                    :, tile * LANES : (tile + 1) * LANES
                ]
    width = moved_ref.shape[1]
    beside = LANES // width
    start = 0
    for ref in (moved_ref, sample_ref, force_ref):
        rows = ref.shape[0]
        wide[start : start + rows, :] = jnp.concatenate([ref[...].astype(f32)] * beside, axis=1)
        start += rows
    count = start // beside
    slot = lane_position((count, LANES)) // width
    merged = wide[pl.ds(0, count, stride=beside), :]
    for place in range(1, beside):
        merged = jnp.where(slot == place, wide[pl.ds(place, count, stride=beside), :], merged)
    nodes = 3 * count // 7
    each = nodes // (3 * layers)
    base = local_count * planes * tiles
    spare = base + nodes + (layers + 1) // 2 * each
    for device in range(devices):
        packet_ref[device, base : base + nodes, :] = merged[:nodes]
    for pair in range((layers + 1) // 2):
        at = nodes + 2 * pair * each
        label = merged[at : at + each] * LABEL_BASE
        if 2 * pair + 1 < layers:
            label = label + merged[at + each : at + 2 * each]
        for device in range(devices):
            packet_ref[device, base + nodes + pair * each : base + nodes + (pair + 1) * each, :] = label
    part = force_rows(layers) * each
    for device in range(devices):
        start = count - nodes if device % 2 == 0 else count - part
        packet_ref[device, spare : spare + part, :] = merged[start : start + part]


def force_rows(layers):
    return (3 * layers + 1) // 2


def read_fields(packet_ref, base, layers, fields):
    _, rows, columns = fields.shape
    devices = rows // layers
    tiles = columns // LANES
    step = packet_ref.shape[0] // devices
    for part in range(4):
        for layer in range(layers):
            for tile in range(tiles):
                row = part * layers + (layer if part < 3 else layer // 2)
                piece = packet_ref[pl.ds(base + row * tiles + tile, devices, stride=step), :]
                if part == 3:
                    high = jnp.floor(piece * (1.0 / LABEL_BASE))
                    piece = high if layer % 2 == 0 else piece - high * LABEL_BASE
                fields[part, layer * devices : (layer + 1) * devices, tile * LANES : (tile + 1) * LANES] = piece


def read_force(packet_ref, other_ref, base, layers, forces, even):
    _, rows, columns = forces.shape
    devices = rows // layers
    tiles = columns // LANES
    step = packet_ref.shape[0] // devices
    start = base + (3 * layers + (layers + 1) // 2) * tiles
    held = force_rows(layers)
    for part in range(3):
        for layer in range(layers):
            row = part * layers + layer
            first = row < held
            local = row if first else row - (3 * layers - held)
            for tile in range(tiles):
                at = pl.ds(start + local * tiles + tile, devices, stride=step)
                mine, other = packet_ref[at, :], other_ref[at, :]
                piece = jnp.where(even, mine, other) if first else jnp.where(even, other, mine)
                forces[part, layer * devices : (layer + 1) * devices, tile * LANES : (tile + 1) * LANES] = piece


def micro_kernel(
    local, local_count, layers, steps_hbm, packet_hbm, mult_hbm, fwd_hbm, bwd_hbm, table_hbm,
    sent_hbm, response_ref, packet_ref, fields, moduli, mult_ref, fwd_ref, bwd_ref, table, spectrum, ordered, sent_ref, steps_ref, sem
):
    devices, planes = sent_ref.shape[0], sent_ref.shape[1] // 6
    vox, columns = moduli.shape[1:]
    half = vox // 2
    quarter = half * half
    width = vox_width(fields.shape[2])
    pairs = [(packet_hbm, packet_ref), (steps_hbm, steps_ref)]
    pairs += [(table_hbm.at[part, fold], table.at[part, fold]) for fold in range(2) for part in range(2)]
    pairs += [(fwd_hbm, fwd_ref), (mult_hbm, mult_ref), (bwd_hbm, bwd_ref)]
    copies = [pltpu.make_async_copy(source, target, sem.at[i]) for i, (source, target) in enumerate(pairs)]
    for copy in copies:
        copy.start()
    own = (lax.axis_index("grp") * lax.axis_size("dev") + lax.axis_index("dev")) * local_count + local
    copies[1].wait()
    steps = steps_ref[own]
    copies[0].wait()
    tiles = columns // LANES
    step = packet_ref.shape[0] // devices
    read_fields(packet_ref, local_count * planes * tiles, layers, fields)
    for device in range(devices):
        for tile in range(tiles):
            at = device * step + local * planes * tiles + tile
            code = packet_ref[pl.ds(at, planes, stride=tiles), :]
            for kind, value in enumerate(decode(code)):
                moduli[
                    kind, device * planes : (device + 1) * planes, tile * LANES : (tile + 1) * LANES
                ] = value
    stencil = Stencil(fields.shape[1:], width, fields.shape[1] // layers)
    mesh_strain = stencil.strain([fields[c] for c in range(3)])
    mine = fields[3] == own.astype(f32)
    count = total(jnp.where(mine, 1.0, 0.0))
    load = [total(jnp.where(mine, part, 0.0)) / count for part in mesh_strain]
    trace, dev = deviator_of(load)
    lame = moduli[0]
    shear = moduli[1]
    size = measure([0.5 * part for part in dev])
    left, _ = remaining(shear, jnp.broadcast_to(size, shear.shape), steps, 4)
    bulk = lame + (2.0 / 3.0) * shear
    sources = jnp.concatenate([bulk * trace, 2.0 * shear * left], axis=0)
    for copy in copies[2:]:
        copy.wait()
    spectral = table_by(fwd_ref[0], fwd_ref[1], forward_plane(sources, table))

    def block(field, px, py, pz):
        rows = slice(field * vox + px * half, field * vox + (px + 1) * half)
        start = (pz * 2 + py) * quarter // 2
        return rows, [slice(fold * 2 * quarter + start, fold * 2 * quarter + start + quarter // 2) for fold in range(2)]

    def take(field, parity):
        rows, pieces = block(field, *parity)
        return jnp.concatenate([spectral[rows, lanes] for lanes in pieces], axis=1)

    parities = [(px, py, pz) for px in range(2) for py in range(2) for pz in range(2)]
    product = [mult_ref[i] for i in range(6)]
    inverse = mult_ref[6]
    scaled = mult_ref[7]

    def second(blocks, parity, a, b):
        if a == b:
            return -(product[SLOT[(a, b)]] * blocks[parity])
        other = tuple(1 - p if axis in (a, b) else p for axis, p in enumerate(parity))
        value = product[SLOT[(a, b)]] * blocks[other]
        return value if parity[a] == parity[b] else -value

    psi = {}
    raw = {}
    for parity in parities:
        raw[parity] = take(1, parity)
        psi[parity] = inverse * raw[parity]
    phi = {}
    for parity in parities:
        pressed = sum(
            (1.0 if a == b else 2.0) * dev[SLOT[(a, b)]] * second(psi, parity, a, b) for a, b in PAIRS
        )
        phi[parity] = (1.0 - green_ratio) * inverse * take(0, parity) + scaled * pressed
    for parity in parities:
        curl = {pair: second(psi, parity, *pair) for pair in PAIRS}
        for index, (a, b) in enumerate(PAIRS):
            def at(i, j):
                return curl[(min(i, j), max(i, j))]
            if a == b:
                sheared = sum(dev[SLOT[(b, c)]] * at(a, c) for c in range(3))
            else:
                sheared = 0.5 * sum(dev[SLOT[(b, c)]] * at(a, c) + dev[SLOT[(a, c)]] * at(b, c) for c in range(3))
            value = second(phi, parity, a, b) + sheared
            rows, pieces = block(index, *parity)
            for fold, lanes in enumerate(pieces):
                spectrum[rows, lanes] = value[:, fold * quarter // 2 : (fold + 1) * quarter // 2]
    moved = table_by(bwd_ref[0], bwd_ref[1], backward_plane(spectrum[...], table))
    if 2 * planes == 8:
        low = row_position((2 * planes, columns)) < planes
        for pair in range(3):
            for chip in range(devices // 2):
                first, second_ = (
                    moved[i * vox + 2 * chip * planes : i * vox + 2 * (chip + 1) * planes]
                    for i in (2 * pair, 2 * pair + 1)
                )
                rows = slice(2 * pair * planes, 2 * (pair + 1) * planes)
                ordered[2 * chip, rows] = jnp.where(low, first, pltpu.roll(second_, planes, 0))
                ordered[2 * chip + 1, rows] = jnp.where(low, pltpu.roll(first, planes, 0), second_)
    else:
        for i in range(6):
            for device in range(devices):
                ordered[device, i * planes : (i + 1) * planes] = moved[
                    i * vox + device * planes : i * vox + (device + 1) * planes
                ]
    for device in range(devices):
        sent_ref[device] = ordered[device].astype(bf16)
    send = pltpu.make_async_copy(sent_ref, sent_hbm, sem.at[len(pairs)])
    send.start()
    strain = [load[i] + moved[i * vox : (i + 1) * vox] for i in range(6)]
    trace, dev = deviator_of(strain)
    left, ratio = remaining(shear, measure([0.5 * part for part in dev]), steps, 4)
    push = bulk * trace
    pull = 2.0 * shear * left
    stress = [push + pull * dev[i] for i in range(3)] + [pull * dev[i] for i in range(3, 6)]
    parts = stress + [lame, shear / (1.0 + ratio)]
    lane = lane_position((1, response_ref.shape[1]))
    row = jnp.zeros(lane.shape, f32)
    for index, part in enumerate(parts):
        row = jnp.where(lane == index, total(part) / float(vox * columns), row)
    for index, part in enumerate(load):
        row = jnp.where(lane == 8 + index, part, row)
    response_ref[...] = jnp.broadcast_to(row, response_ref.shape)
    send.wait()


def vox_width(columns):
    width = int(round(columns**0.5))
    return width


def macro_kernel(
    layers, base, slots_ref, table_ref, table_v_ref, packet_ref, other_ref, next_ref, row_ref, fields, forces, cells, result
):
    columns = next_ref.shape[2]
    devices = fields.shape[1] // layers
    samples = table_v_ref.shape[0]
    rank = lax.axis_index("dev")
    group = lax.axis_index("grp")
    local_count = row_ref.shape[0]
    group_size = local_count * devices
    start = group * group_size
    for local in range(local_count):
        chosen = jnp.int32(0)
        for j in range(group_size):
            chosen = jnp.where(slots_ref[start + j] == rank * local_count + local, start + j, chosen)
        row_ref[local : local + 1, :] = table_v_ref[pl.ds(chosen, 1), 0:8]
    read_fields(packet_ref, base, layers, fields)
    read_force(packet_ref, other_ref, base, layers, forces, rank % 2 == 0)
    rows = fields.shape[1]
    height = min(8, rows)
    span = min(512, columns)
    for top in range(0, rows, height):
        for side in range(0, columns, span):
            where = (slice(top, top + height), slice(side, side + span))
            label = fields[(3,) + where]

            def pick(sample, held):
                here = label == sample.astype(f32)
                return tuple(jnp.where(here, table_ref[sample, c], held[c]) for c in range(8))

            zero = jnp.zeros((height, span), f32)
            held = lax.fori_loop(0, samples, pick, (zero,) * 8, unroll=4)
            for c in range(8):
                cells[(c,) + where] = held[c]
    stencil = Stencil(fields.shape[1:], vox_width(columns), devices)
    stress = [cells[c] for c in range(6)]
    pulled = stencil.force(stress)
    remainder = [forces[b] - pulled[b] - spring_rate * fields[b] for b in range(3)]
    direction = remainder
    norm_now = total(sum(r * r for r in remainder))
    update = None
    lame = cells[6]
    shear = 2.0 * cells[7]
    for turn in range(CG_STEPS):
        strain = stencil.strain(direction)
        pressure = lame * (strain[0] + strain[1] + strain[2])
        stress = [shear * strain[i] + pressure for i in range(3)] + [shear * strain[i] for i in range(3, 6)]
        pulled = stencil.force(stress)
        image = [pulled[b] + spring_rate * direction[b] for b in range(3)]
        alpha = norm_now / total(sum(direction[b] * image[b] for b in range(3)))
        moved = [alpha * direction[b] for b in range(3)]
        update = moved if update is None else [update[b] + moved[b] for b in range(3)]
        if turn + 1 < CG_STEPS:
            remainder = [remainder[b] - alpha * image[b] for b in range(3)]
            norm_next = total(sum(r * r for r in remainder))
            grow = norm_next / norm_now
            direction = [remainder[b] + grow * direction[b] for b in range(3)]
            norm_now = norm_next
    for b in range(3):
        done = fields[b] + update[b]
        result[b] = done
        for layer in range(layers):
            next_ref[b, layer : layer + 1, :] = result[b, pl.ds(layer * devices + rank, 1), :]


def vmem():
    return pl.BlockSpec(memory_space=pltpu.VMEM)


def hbm():
    return pl.BlockSpec(memory_space=pltpu.HBM)


def smem():
    return pl.BlockSpec(memory_space=pltpu.SMEM)


def shards(
    displacement, external_force, element_sample, lame_field, shear_field, plastic_steps, owner_slot
):
    group_size, planes, columns = lame_field.shape
    devices = lax.axis_size("dev")
    groups = lax.axis_size("grp")
    local_count = group_size // devices
    vox = planes * devices
    layers = displacement.shape[1]
    width = displacement.shape[2] * displacement.shape[3]
    plane, forward_line, backward_line, multipliers = tables(vox)
    params = pltpu.CompilerParams(vmem_limit_bytes=60 * 1024 * 1024)

    side = displacement.shape[3]
    lines = layers * displacement.shape[2]
    tiles = columns // LANES
    base = local_count * planes * tiles
    length = base + (3 * layers + (layers + 1) // 2 + force_rows(layers)) * tiles
    packet = pl.pallas_call(
        functools.partial(pack_kernel, layers),
        name="pack",
        out_shape=jax.ShapeDtypeStruct((devices, length, LANES), f32),
        in_specs=[vmem()] * 5,
        out_specs=vmem(),
        scratch_shapes=[pltpu.VMEM((7 * lines, LANES), f32)],
        compiler_params=params,
    )(
        displacement.reshape(3 * lines, side), element_sample.reshape(lines, side),
        external_force.reshape(3 * lines, side),
        lame_field.reshape(devices, local_count, planes, columns),
        shear_field.reshape(devices, local_count, planes, columns),
    )
    packets = lax.all_to_all(packet, "dev", split_axis=0, concat_axis=0, tiled=True).reshape(devices * length, LANES)
    neighbour = lax.ppermute(packets, "dev", [(i, i ^ 1) for i in range(devices)])
    everyone = groups * devices
    sents = []
    rows = []
    for local in range(local_count):
        sent, response = pl.pallas_call(
            functools.partial(micro_kernel, local, local_count, layers),
            name="micro",
            out_shape=(
                jax.ShapeDtypeStruct((devices, 6 * planes, columns), bf16),
                jax.ShapeDtypeStruct((everyone, 16), f32),
            ),
            in_specs=[hbm()] * 6,
            out_specs=(hbm(), vmem()),
            scratch_shapes=[
                pltpu.VMEM((devices * length, LANES), f32),
                pltpu.VMEM((4, devices * layers, width), f32),
                pltpu.VMEM((2, vox, columns), f32),
                pltpu.VMEM(multipliers.shape, f32),
                pltpu.VMEM(forward_line.shape, bf16),
                pltpu.VMEM(backward_line.shape, bf16),
                pltpu.VMEM(plane.shape, bf16),
                pltpu.VMEM((6 * vox, columns), f32),
                pltpu.VMEM((devices, 6 * planes, columns), f32),
                pltpu.VMEM((devices, 6 * planes, columns), bf16),
                pltpu.SMEM(plastic_steps.shape, jnp.int32),
                pltpu.SemaphoreType.DMA((10,)),
            ],
            compiler_params=params,
        )(
            plastic_steps, packets, multipliers, forward_line, backward_line, plane,
        )
        sents.append(sent)
        rows.append(response)
    gathered = lax.all_to_all(
        jnp.stack(rows, axis=1), ("grp", "dev"), split_axis=0, concat_axis=0, tiled=True
    ).reshape(everyone * local_count, 16)
    moved = lax.all_to_all(jnp.stack(sents, axis=1), "dev", split_axis=0, concat_axis=0, tiled=True)
    group_rows = lax.dynamic_slice_in_dim(gathered, lax.axis_index("grp") * group_size, group_size)
    loads = group_rows[:, 8:14].T
    change = jnp.transpose(moved.reshape(group_size, 6, planes, columns), (1, 0, 2, 3))
    micro_strain = loads[:, :, None, None] + change.astype(f32)
    following, picked = pl.pallas_call(
        functools.partial(macro_kernel, layers, base),
        name="macro",
        out_shape=(
            jax.ShapeDtypeStruct((3, layers, width), f32),
            jax.ShapeDtypeStruct((local_count, 8), f32),
        ),
        in_specs=[smem(), smem()] + [vmem()] * 3,
        out_specs=(vmem(), vmem()),
        scratch_shapes=[
            pltpu.VMEM((4, devices * layers, width), f32),
            pltpu.VMEM((3, devices * layers, width), f32),
            pltpu.VMEM((8, devices * layers, width), f32),
            pltpu.VMEM((3, devices * layers, width), f32),
        ],
        compiler_params=params,
    )(owner_slot, gathered, gathered, packets, neighbour)
    return (following.reshape(displacement.shape), picked, micro_strain)


def solution(mesh):
    in_specs = (
        P(None, "dev", None, None),
        P(None, "dev", None, None),
        P("dev", None, None),
        P("grp", "dev", None),
        P("grp", "dev", None),
        P(),
        P(),
    )
    out_specs = (P(None, "dev", None, None), P(("grp", "dev"), None), P(None, "grp", "dev", None))
    return jax.shard_map(shards, mesh=mesh, in_specs=in_specs, out_specs=out_specs, check_vma=False)
```

```python
import functools
import jax
import jax.numpy as jnp
import numpy as np
from jax import lax
from jax.experimental import pallas as pl
from jax.experimental.pallas import tpu as pltpu
from jax.sharding import PartitionSpec as P

CG_STEPS = 3
shear_ref = 1.65
lame_ref = 1.25
green_ratio = (lame_ref + shear_ref) / (lame_ref + 2.0 * shear_ref)
relax_rate = 0.35
flow_scale = 4.0
spring_rate = 0.2
f32 = jnp.float32
bf16 = jnp.bfloat16
DIAG = ((0, 0), (1, 1), (2, 2))
PAIRS = ((0, 0), (1, 1), (2, 2), (1, 2), (0, 2), (0, 1))
SLOT = {(0, 0): 0, (1, 1): 1, (2, 2): 2, (1, 2): 3, (2, 1): 3, (0, 2): 4, (2, 0): 4, (0, 1): 5, (1, 0): 5}


def split_table(table):
    high = table.astype(np.float32).astype(bf16)
    low = (table - high.astype(np.float64)).astype(np.float32).astype(bf16)
    return np.stack([high, low])


def tables(vox):
    half = vox // 2
    n = np.arange(vox)[:, None]
    k = np.arange(half)[None, :]
    angle = 2.0 * np.pi * (n * k % vox) / vox
    cosine = np.cos(angle) * np.sqrt(2.0 / vox)
    sine = np.sin(angle) * np.sqrt(2.0 / vox)
    cosine[:, 0] = 1.0 / np.sqrt(vox)
    sine[:, 0] = (1.0 - 2.0 * (np.arange(vox) % 2)) / np.sqrt(vox)
    basis = np.concatenate([cosine, sine], axis=1)
    order = np.concatenate([np.arange(0, half, 2), np.arange(1, half, 2)])
    by_parity = basis.reshape(vox, 2, half)
    folded = by_parity[:half, :, order].reshape(half, 2, 2, half // 2)
    plane = np.einsum("ypek,zql->eyzqpkl", folded, by_parity).reshape(2, half * vox, half * vox)
    line = basis.T
    forward_line = np.kron(np.eye(2), line)
    backward_line = np.kron(np.eye(6), line.T)
    wave = np.sin(2.0 * np.pi * np.arange(half) / vox)
    wave[0] = 0.0
    first = np.broadcast_to(wave[:, None, None], (half, half, half))
    second = np.broadcast_to(wave[order][None, :, None], (half, half, half))
    third = np.broadcast_to(wave[None, None, :], (half, half, half))
    square = first**2 + second**2 + third**2
    inverse = np.where(square > 0.0, 1.0 / np.where(square > 0.0, square, 1.0), 0.0)
    waves = (first, second, third)
    products = [waves[a] * waves[b] for a, b in PAIRS]
    rows = products + [inverse / shear_ref, green_ratio * inverse]
    multipliers = np.stack(rows).reshape(len(rows), half, half * half).astype(np.float32)
    return split_table(plane), split_table(forward_line), split_table(backward_line), multipliers


def split(value):
    high = value.astype(bf16)
    return high, (value - high.astype(f32)).astype(bf16)


def dot(left, right):
    return lax.dot_general(left, right, (((1,), (0,)), ((), ())), preferred_element_type=f32)


def dot_t(left, right):
    return lax.dot_general(left, right, (((1,), (1,)), ((), ())), preferred_element_type=f32)


def by_table(value, high, low, contract):
    rows = value.shape[0]
    value_high, value_low = split(value)
    both = contract(jnp.concatenate([value_high, value_low], axis=0), high)
    return both[:rows] + both[rows:] + contract(value_high, low)


def table_by(high, low, value):
    value_high, value_low = split(value)
    deep = jnp.concatenate([high, low, high], axis=1)
    return dot(deep, jnp.concatenate([value_high, value_high, value_low], axis=0))


def forward_plane(value, table):
    half = value.shape[1] // 2
    low, high = value[:, :half], value[:, half:]
    even = by_table(low + high, table[0, 0], table[1, 0], dot)
    odd = by_table(low - high, table[0, 1], table[1, 1], dot)
    return jnp.concatenate([even, odd], axis=1)


def backward_plane(value, table):
    half = value.shape[1] // 2
    even = by_table(value[:, :half], table[0, 0], table[1, 0], dot_t)
    odd = by_table(value[:, half:], table[0, 1], table[1, 1], dot_t)
    return jnp.concatenate([even + odd, even - odd], axis=1)


def lane_position(shape):
    return lax.broadcasted_iota(jnp.int32, shape, 1)


def row_position(shape):
    return lax.broadcasted_iota(jnp.int32, shape, 0)


class Stencil:
    def __init__(self, shape, width, devices):
        self.rows, self.columns = shape
        self.width = width
        self.devices = devices
        lane = lane_position(shape)
        row = row_position((devices, self.columns))
        self.last_z = lane % width == width - 1
        self.first_z = lane % width == 0
        self.last_y = lane >= self.columns - width
        self.first_y = lane < width
        self.last_x = row == devices - 1
        self.first_x = row == 0

    def up_z(self, v):
        return jnp.where(self.last_z, 0.0, pltpu.roll(v, self.columns - 1, 1))

    def up_y(self, v):
        return jnp.where(self.last_y, 0.0, pltpu.roll(v, self.columns - self.width, 1))

    def up_x(self, v):
        wrapped = jnp.where(self.last_x, 0.0, pltpu.roll(v[: self.devices], self.devices - 1, 0))
        return jnp.concatenate([v[self.devices :], wrapped], axis=0)

    def down_z(self, v):
        return jnp.where(self.first_z, 0.0, pltpu.roll(v, 1, 1))

    def down_y(self, v):
        return jnp.where(self.first_y, 0.0, pltpu.roll(v, self.width, 1))

    def down_x(self, v):
        wrapped = jnp.where(self.first_x, 0.0, pltpu.roll(v[self.rows - self.devices :], 1, 0))
        return jnp.concatenate([wrapped, v[: self.rows - self.devices]], axis=0)

    def strain(self, field):
        slopes = []
        for v in field:
            next_z = self.up_z(v)
            sum_z = v + next_z
            dif_z = next_z - v
            next_y = self.up_y(sum_z)
            sums = sum_z + next_y
            along_y = next_y - sum_z
            along_z = dif_z + self.up_y(dif_z)
            slopes.append((self.up_x(sums) - sums, along_y + self.up_x(along_y), along_z + self.up_x(along_z)))
        return [
            0.25 * slopes[0][0],
            0.25 * slopes[1][1],
            0.25 * slopes[2][2],
            0.125 * (slopes[2][1] + slopes[1][2]),
            0.125 * (slopes[2][0] + slopes[0][2]),
            0.125 * (slopes[1][0] + slopes[0][1]),
        ]

    def force(self, stress):
        result = []
        for b in range(3):
            along_x, along_y, along_z = (stress[SLOT[(a, b)]] for a in range(3))
            sum_x = along_x + self.down_z(along_x)
            first = sum_x + self.down_y(sum_x)
            sum_y = along_y + self.down_z(along_y)
            dif_z = self.down_z(along_z) - along_z
            back = self.down_y(sum_y)
            rest = (back - sum_y) + (dif_z + self.down_y(dif_z))
            result.append(0.25 * ((self.down_x(first) - first) + (rest + self.down_x(rest))))
        return result


def total(value):
    return jnp.sum(jnp.sum(value, axis=0, keepdims=True), axis=1, keepdims=True)


def measure(stress):
    return (
        stress[0] * stress[0]
        + stress[1] * stress[1]
        + stress[2] * stress[2]
        + 2.0 * (stress[3] * stress[3] + stress[4] * stress[4] + stress[5] * stress[5])
    )


def remaining(shear, size, steps, most):
    stiff = (2.0 * shear) * (2.0 * shear) * size

    def relax(count, left):
        ratio = stiff * left * left
        return left * ((1.0 - relax_rate) + relax_rate / (1.0 + ratio))

    left = lax.fori_loop(0, steps, relax, jnp.ones_like(stiff))
    return left, stiff * left * left


def deviator_of(strain):
    trace = strain[0] + strain[1] + strain[2]
    third = trace / 3.0
    return trace, [strain[0] - third, strain[1] - third, strain[2] - third] + list(strain[3:])


LAME_UNIT = 2.0**8
SHEAR_UNIT = 2.0**9
CODE_BASE = 2.0**11
LABEL_BASE = 2.0**12
LANES = 128


def encode(lame, shear):
    return (lame.astype(f32) * LAME_UNIT) * CODE_BASE + shear.astype(f32) * SHEAR_UNIT


def decode(code):
    high = jnp.floor(code * (1.0 / CODE_BASE))
    return high * (1.0 / LAME_UNIT), (code - high * CODE_BASE) * (1.0 / SHEAR_UNIT)


def pack_kernel(layers, moved_ref, sample_ref, force_ref, lame_ref, shear_ref, packet_ref, wide):
    devices, local_count, planes, columns = lame_ref.shape
    tiles = columns // LANES
    for device in range(devices):
        for local in range(local_count):
            code = encode(lame_ref[device, local], shear_ref[device, local])
            for tile in range(tiles):
                packet_ref[device, pl.ds(local * planes * tiles + tile, planes, stride=tiles), :] = code[
                    :, tile * LANES : (tile + 1) * LANES
                ]
    width = moved_ref.shape[1]
    beside = LANES // width
    start = 0
    for ref in (moved_ref, sample_ref, force_ref):
        rows = ref.shape[0]
        wide[start : start + rows, :] = jnp.concatenate([ref[...].astype(f32)] * beside, axis=1)
        start += rows
    count = start // beside
    slot = lane_position((count, LANES)) // width
    merged = wide[pl.ds(0, count, stride=beside), :]
    for place in range(1, beside):
        merged = jnp.where(slot == place, wide[pl.ds(place, count, stride=beside), :], merged)
    nodes = 3 * count // 7
    each = nodes // (3 * layers)
    base = local_count * planes * tiles
    spare = base + nodes + (layers + 1) // 2 * each
    for device in range(devices):
        packet_ref[device, base : base + nodes, :] = merged[:nodes]
    for pair in range((layers + 1) // 2):
        at = nodes + 2 * pair * each
        label = merged[at : at + each] * LABEL_BASE
        if 2 * pair + 1 < layers:
            label = label + merged[at + each : at + 2 * each]
        for device in range(devices):
            packet_ref[device, base + nodes + pair * each : base + nodes + (pair + 1) * each, :] = label
    part = force_rows(layers) * each
    for device in range(devices):
        start = count - nodes if device % 2 == 0 else count - part
        packet_ref[device, spare : spare + part, :] = merged[start : start + part]


def force_rows(layers):
    return (3 * layers + 1) // 2


def read_fields(packet_ref, base, layers, fields):
    _, rows, columns = fields.shape
    devices = rows // layers
    tiles = columns // LANES
    step = packet_ref.shape[0] // devices
    for part in range(4):
        for layer in range(layers):
            for tile in range(tiles):
                row = part * layers + (layer if part < 3 else layer // 2)
                piece = packet_ref[pl.ds(base + row * tiles + tile, devices, stride=step), :]
                if part == 3:
                    high = jnp.floor(piece * (1.0 / LABEL_BASE))
                    piece = high if layer % 2 == 0 else piece - high * LABEL_BASE
                fields[part, layer * devices : (layer + 1) * devices, tile * LANES : (tile + 1) * LANES] = piece


def read_force(packet_ref, other_ref, base, layers, forces, even):
    _, rows, columns = forces.shape
    devices = rows // layers
    tiles = columns // LANES
    step = packet_ref.shape[0] // devices
    start = base + (3 * layers + (layers + 1) // 2) * tiles
    held = force_rows(layers)
    for part in range(3):
        for layer in range(layers):
            row = part * layers + layer
            first = row < held
            local = row if first else row - (3 * layers - held)
            for tile in range(tiles):
                at = pl.ds(start + local * tiles + tile, devices, stride=step)
                mine, other = packet_ref[at, :], other_ref[at, :]
                piece = jnp.where(even, mine, other) if first else jnp.where(even, other, mine)
                forces[part, layer * devices : (layer + 1) * devices, tile * LANES : (tile + 1) * LANES] = piece


def micro_kernel(
    local, local_count, layers, steps_hbm, packet_hbm, mult_hbm, fwd_hbm, bwd_hbm, table_hbm,
    sent_hbm, response_hbm, packet_ref, fields, moduli, mult_ref, fwd_ref, bwd_ref, table, spectrum, ordered, sent_ref, response_ref, steps_ref, sem
):
    devices, planes = sent_ref.shape[0], sent_ref.shape[1] // 6
    vox, columns = moduli.shape[1:]
    half = vox // 2
    quarter = half * half
    width = vox_width(fields.shape[2])
    pairs = [(packet_hbm, packet_ref), (steps_hbm, steps_ref)]
    pairs += [(table_hbm.at[part, fold], table.at[part, fold]) for fold in range(2) for part in range(2)]
    pairs += [(fwd_hbm, fwd_ref), (mult_hbm, mult_ref), (bwd_hbm, bwd_ref)]
    copies = [pltpu.make_async_copy(source, target, sem.at[i]) for i, (source, target) in enumerate(pairs)]
    for copy in copies:
        copy.start()
    own = (lax.axis_index("grp") * lax.axis_size("dev") + lax.axis_index("dev")) * local_count + local
    copies[1].wait()
    steps = steps_ref[own]
    copies[0].wait()
    tiles = columns // LANES
    step = packet_ref.shape[0] // devices
    read_fields(packet_ref, local_count * planes * tiles, layers, fields)
    for device in range(devices):
        for tile in range(tiles):
            at = device * step + local * planes * tiles + tile
            code = packet_ref[pl.ds(at, planes, stride=tiles), :]
            for kind, value in enumerate(decode(code)):
                moduli[
                    kind, device * planes : (device + 1) * planes, tile * LANES : (tile + 1) * LANES
                ] = value
    stencil = Stencil(fields.shape[1:], width, fields.shape[1] // layers)
    mesh_strain = stencil.strain([fields[c] for c in range(3)])
    mine = fields[3] == own.astype(f32)
    count = total(jnp.where(mine, 1.0, 0.0))
    load = [total(jnp.where(mine, part, 0.0)) / count for part in mesh_strain]
    trace, dev = deviator_of(load)
    lame = moduli[0]
    shear = moduli[1]
    size = measure([0.5 * part for part in dev])
    left, _ = remaining(shear, jnp.broadcast_to(size, shear.shape), steps, 4)
    bulk = lame + (2.0 / 3.0) * shear
    sources = jnp.concatenate([bulk * trace, 2.0 * shear * left], axis=0)
    for copy in copies[2:]:
        copy.wait()
    spectral = table_by(fwd_ref[0], fwd_ref[1], forward_plane(sources, table))

    def block(field, px, py, pz):
        rows = slice(field * vox + px * half, field * vox + (px + 1) * half)
        start = (pz * 2 + py) * quarter // 2
        return rows, [slice(fold * 2 * quarter + start, fold * 2 * quarter + start + quarter // 2) for fold in range(2)]

    def take(field, parity):
        rows, pieces = block(field, *parity)
        return jnp.concatenate([spectral[rows, lanes] for lanes in pieces], axis=1)

    parities = [(px, py, pz) for px in range(2) for py in range(2) for pz in range(2)]
    product = [mult_ref[i] for i in range(6)]
    inverse = mult_ref[6]
    scaled = mult_ref[7]

    def second(blocks, parity, a, b):
        if a == b:
            return -(product[SLOT[(a, b)]] * blocks[parity])
        other = tuple(1 - p if axis in (a, b) else p for axis, p in enumerate(parity))
        value = product[SLOT[(a, b)]] * blocks[other]
        return value if parity[a] == parity[b] else -value

    psi = {}
    raw = {}
    for parity in parities:
        raw[parity] = take(1, parity)
        psi[parity] = inverse * raw[parity]
    phi = {}
    for parity in parities:
        pressed = sum(
            (1.0 if a == b else 2.0) * dev[SLOT[(a, b)]] * second(psi, parity, a, b) for a, b in PAIRS
        )
        phi[parity] = (1.0 - green_ratio) * inverse * take(0, parity) + scaled * pressed
    for parity in parities:
        curl = {pair: second(psi, parity, *pair) for pair in PAIRS}
        for index, (a, b) in enumerate(PAIRS):
            def at(i, j):
                return curl[(min(i, j), max(i, j))]
            if a == b:
                sheared = sum(dev[SLOT[(b, c)]] * at(a, c) for c in range(3))
            else:
                sheared = 0.5 * sum(dev[SLOT[(b, c)]] * at(a, c) + dev[SLOT[(a, c)]] * at(b, c) for c in range(3))
            value = second(phi, parity, a, b) + sheared
            rows, pieces = block(index, *parity)
            for fold, lanes in enumerate(pieces):
                spectrum[rows, lanes] = value[:, fold * quarter // 2 : (fold + 1) * quarter // 2]
    moved = table_by(bwd_ref[0], bwd_ref[1], backward_plane(spectrum[...], table))
    if 2 * planes == 8:
        low = row_position((2 * planes, columns)) < planes
        for pair in range(3):
            for chip in range(devices // 2):
                first, second_ = (
                    moved[i * vox + 2 * chip * planes : i * vox + 2 * (chip + 1) * planes]
                    for i in (2 * pair, 2 * pair + 1)
                )
                rows = slice(2 * pair * planes, 2 * (pair + 1) * planes)
                ordered[2 * chip, rows] = jnp.where(low, first, pltpu.roll(second_, planes, 0))
                ordered[2 * chip + 1, rows] = jnp.where(low, pltpu.roll(first, planes, 0), second_)
    else:
        for i in range(6):
            for device in range(devices):
                ordered[device, i * planes : (i + 1) * planes] = moved[
                    i * vox + device * planes : i * vox + (device + 1) * planes
                ]
    for device in range(devices):
        sent_ref[device] = ordered[device].astype(bf16)
    send = pltpu.make_async_copy(sent_ref, sent_hbm, sem.at[len(pairs)])
    send.start()
    strain = [load[i] + moved[i * vox : (i + 1) * vox] for i in range(6)]
    trace, dev = deviator_of(strain)
    left, ratio = remaining(shear, measure([0.5 * part for part in dev]), steps, 4)
    push = bulk * trace
    pull = 2.0 * shear * left
    stress = [push + pull * dev[i] for i in range(3)] + [pull * dev[i] for i in range(3, 6)]
    parts = stress + [lame, shear / (1.0 + ratio)]
    lane = lane_position((1, response_ref.shape[1]))
    row = jnp.zeros(lane.shape, f32)
    for index, part in enumerate(parts):
        row = jnp.where(lane == index, total(part) / float(vox * columns), row)
    for index, part in enumerate(load):
        row = jnp.where(lane == 8 + index, part, row)
    response_ref[...] = jnp.broadcast_to(row, response_ref.shape)
    answer = pltpu.make_async_copy(response_ref, response_hbm, sem.at[len(pairs) + 1])
    answer.start()
    send.wait()
    answer.wait()


def vox_width(columns):
    width = int(round(columns**0.5))
    return width


def macro_kernel(
    layers, base, slots_ref, table_ref, table_v_ref, packet_ref, other_ref, next_ref, row_ref, fields, forces, cells, result
):
    columns = next_ref.shape[2]
    devices = fields.shape[1] // layers
    samples = table_v_ref.shape[0]
    rank = lax.axis_index("dev")
    group = lax.axis_index("grp")
    local_count = row_ref.shape[0]
    group_size = local_count * devices
    start = group * group_size
    for local in range(local_count):
        chosen = jnp.int32(0)
        for j in range(group_size):
            chosen = jnp.where(slots_ref[start + j] == rank * local_count + local, start + j, chosen)
        row_ref[local : local + 1, :] = table_v_ref[pl.ds(chosen, 1), 0:8]
    read_fields(packet_ref, base, layers, fields)
    read_force(packet_ref, other_ref, base, layers, forces, rank % 2 == 0)
    rows = fields.shape[1]
    height = min(8, rows)
    span = min(512, columns)
    for top in range(0, rows, height):
        for side in range(0, columns, span):
            where = (slice(top, top + height), slice(side, side + span))
            label = fields[(3,) + where]

            def pick(sample, held):
                here = label == sample.astype(f32)
                return tuple(jnp.where(here, table_ref[sample, c], held[c]) for c in range(8))

            zero = jnp.zeros((height, span), f32)
            held = lax.fori_loop(0, samples, pick, (zero,) * 8, unroll=4)
            for c in range(8):
                cells[(c,) + where] = held[c]
    stencil = Stencil(fields.shape[1:], vox_width(columns), devices)
    stress = [cells[c] for c in range(6)]
    pulled = stencil.force(stress)
    remainder = [forces[b] - pulled[b] - spring_rate * fields[b] for b in range(3)]
    direction = remainder
    norm_now = total(sum(r * r for r in remainder))
    update = None
    lame = cells[6]
    shear = 2.0 * cells[7]
    for turn in range(CG_STEPS):
        strain = stencil.strain(direction)
        pressure = lame * (strain[0] + strain[1] + strain[2])
        stress = [shear * strain[i] + pressure for i in range(3)] + [shear * strain[i] for i in range(3, 6)]
        pulled = stencil.force(stress)
        image = [pulled[b] + spring_rate * direction[b] for b in range(3)]
        alpha = norm_now / total(sum(direction[b] * image[b] for b in range(3)))
        moved = [alpha * direction[b] for b in range(3)]
        update = moved if update is None else [update[b] + moved[b] for b in range(3)]
        if turn + 1 < CG_STEPS:
            remainder = [remainder[b] - alpha * image[b] for b in range(3)]
            norm_next = total(sum(r * r for r in remainder))
            grow = norm_next / norm_now
            direction = [remainder[b] + grow * direction[b] for b in range(3)]
            norm_now = norm_next
    for b in range(3):
        done = fields[b] + update[b]
        result[b] = done
        for layer in range(layers):
            next_ref[b, layer : layer + 1, :] = result[b, pl.ds(layer * devices + rank, 1), :]


def vmem():
    return pl.BlockSpec(memory_space=pltpu.VMEM)


def hbm():
    return pl.BlockSpec(memory_space=pltpu.HBM)


def smem():
    return pl.BlockSpec(memory_space=pltpu.SMEM)


def shards(
    displacement, external_force, element_sample, lame_field, shear_field, plastic_steps, owner_slot
):
    group_size, planes, columns = lame_field.shape
    devices = lax.axis_size("dev")
    groups = lax.axis_size("grp")
    local_count = group_size // devices
    vox = planes * devices
    layers = displacement.shape[1]
    width = displacement.shape[2] * displacement.shape[3]
    plane, forward_line, backward_line, multipliers = tables(vox)
    pack_params, params, macro_params = (
        pltpu.CompilerParams(vmem_limit_bytes=size * 1024 * 1024) for size in (60, 60, 16)
    )

    side = displacement.shape[3]
    lines = layers * displacement.shape[2]
    tiles = columns // LANES
    base = local_count * planes * tiles
    length = base + (3 * layers + (layers + 1) // 2 + force_rows(layers)) * tiles
    packet = pl.pallas_call(
        functools.partial(pack_kernel, layers),
        name="pack",
        out_shape=jax.ShapeDtypeStruct((devices, length, LANES), f32),
        in_specs=[vmem()] * 5,
        out_specs=vmem(),
        scratch_shapes=[pltpu.VMEM((7 * lines, LANES), f32)],
        compiler_params=pack_params,
    )(
        displacement.reshape(3 * lines, side), element_sample.reshape(lines, side),
        external_force.reshape(3 * lines, side),
        lame_field.reshape(devices, local_count, planes, columns),
        shear_field.reshape(devices, local_count, planes, columns),
    )
    packets = lax.all_to_all(packet, "dev", split_axis=0, concat_axis=0, tiled=True).reshape(devices * length, LANES)
    neighbour = lax.ppermute(packets, "dev", [(i, i ^ 1) for i in range(devices)])
    everyone = groups * devices
    sents = []
    rows = []
    for local in range(local_count):
        sent, response = pl.pallas_call(
            functools.partial(micro_kernel, local, local_count, layers),
            name="micro",
            out_shape=(
                jax.ShapeDtypeStruct((devices, 6 * planes, columns), bf16),
                jax.ShapeDtypeStruct((everyone, 16), f32),
            ),
            in_specs=[hbm()] * 6,
            out_specs=(hbm(), hbm()),
            scratch_shapes=[
                pltpu.VMEM((devices * length, LANES), f32),
                pltpu.VMEM((4, devices * layers, width), f32),
                pltpu.VMEM((2, vox, columns), f32),
                pltpu.VMEM(multipliers.shape, f32),
                pltpu.VMEM(forward_line.shape, bf16),
                pltpu.VMEM(backward_line.shape, bf16),
                pltpu.VMEM(plane.shape, bf16),
                pltpu.VMEM((6 * vox, columns), f32),
                pltpu.VMEM((devices, 6 * planes, columns), f32),
                pltpu.VMEM((devices, 6 * planes, columns), bf16),
                pltpu.VMEM((everyone, 16), f32),
                pltpu.SMEM(plastic_steps.shape, jnp.int32),
                pltpu.SemaphoreType.DMA((11,)),
            ],
            compiler_params=params,
        )(
            plastic_steps, packets, multipliers, forward_line, backward_line, plane,
        )
        sents.append(sent)
        rows.append(response)
    gathered = lax.all_to_all(
        jnp.stack(rows, axis=1), ("grp", "dev"), split_axis=0, concat_axis=0, tiled=True
    ).reshape(everyone * local_count, 16)
    moved = lax.all_to_all(jnp.stack(sents, axis=1), "dev", split_axis=0, concat_axis=0, tiled=True)
    group_rows = lax.dynamic_slice_in_dim(gathered, lax.axis_index("grp") * group_size, group_size)
    loads = group_rows[:, 8:14].T
    change = jnp.transpose(moved.reshape(group_size, 6, planes, columns), (1, 0, 2, 3))
    micro_strain = loads[:, :, None, None] + change.astype(f32)
    following, picked = pl.pallas_call(
        functools.partial(macro_kernel, layers, base),
        name="macro",
        out_shape=(
            jax.ShapeDtypeStruct((3, layers, width), f32),
            jax.ShapeDtypeStruct((local_count, 8), f32),
        ),
        in_specs=[smem(), smem()] + [vmem()] * 3,
        out_specs=(vmem(), vmem()),
        scratch_shapes=[
            pltpu.VMEM((4, devices * layers, width), f32),
            pltpu.VMEM((3, devices * layers, width), f32),
            pltpu.VMEM((8, devices * layers, width), f32),
            pltpu.VMEM((3, devices * layers, width), f32),
        ],
        compiler_params=macro_params,
    )(owner_slot, gathered, gathered, packets, neighbour)
    return (following.reshape(displacement.shape), picked, micro_strain)


def solution(mesh):
    in_specs = (
        P(None, "dev", None, None),
        P(None, "dev", None, None),
        P("dev", None, None),
        P("grp", "dev", None),
        P("grp", "dev", None),
        P(),
        P(),
    )
    out_specs = (P(None, "dev", None, None), P(("grp", "dev"), None), P(None, "grp", "dev", None))
    return jax.shard_map(shards, mesh=mesh, in_specs=in_specs, out_specs=out_specs, check_vma=False)
```

```python
import functools
import jax
import jax.numpy as jnp
import numpy as np
from jax import lax
from jax.experimental import pallas as pl
from jax.experimental.pallas import tpu as pltpu
from jax.sharding import PartitionSpec as P

CG_STEPS = 3
shear_ref = 1.65
lame_ref = 1.25
green_ratio = (lame_ref + shear_ref) / (lame_ref + 2.0 * shear_ref)
relax_rate = 0.35
flow_scale = 4.0
spring_rate = 0.2
f32 = jnp.float32
bf16 = jnp.bfloat16
DIAG = ((0, 0), (1, 1), (2, 2))
PAIRS = ((0, 0), (1, 1), (2, 2), (1, 2), (0, 2), (0, 1))
SLOT = {(0, 0): 0, (1, 1): 1, (2, 2): 2, (1, 2): 3, (2, 1): 3, (0, 2): 4, (2, 0): 4, (0, 1): 5, (1, 0): 5}


def split_table(table):
    high = table.astype(np.float32).astype(bf16)
    low = (table - high.astype(np.float64)).astype(np.float32).astype(bf16)
    return np.stack([high, low])


def tables(vox):
    half = vox // 2
    n = np.arange(vox)[:, None]
    k = np.arange(half)[None, :]
    angle = 2.0 * np.pi * (n * k % vox) / vox
    cosine = np.cos(angle) * np.sqrt(2.0 / vox)
    sine = np.sin(angle) * np.sqrt(2.0 / vox)
    cosine[:, 0] = 1.0 / np.sqrt(vox)
    sine[:, 0] = (1.0 - 2.0 * (np.arange(vox) % 2)) / np.sqrt(vox)
    basis = np.concatenate([cosine, sine], axis=1)
    order = np.concatenate([np.arange(0, half, 2), np.arange(1, half, 2)])
    by_parity = basis.reshape(vox, 2, half)
    folded = by_parity[:half, :, order].reshape(half, 2, 2, half // 2)
    plane = np.einsum("ypek,zql->eyzqpkl", folded, by_parity).reshape(2, half * vox, half * vox)
    line = basis.T
    forward_line = np.kron(np.eye(2), line)
    backward_line = np.kron(np.eye(6), line.T)
    wave = np.sin(2.0 * np.pi * np.arange(half) / vox)
    wave[0] = 0.0
    first = np.broadcast_to(wave[:, None, None], (half, half, half))
    second = np.broadcast_to(wave[order][None, :, None], (half, half, half))
    third = np.broadcast_to(wave[None, None, :], (half, half, half))
    square = first**2 + second**2 + third**2
    inverse = np.where(square > 0.0, 1.0 / np.where(square > 0.0, square, 1.0), 0.0)
    waves = (first, second, third)
    products = [waves[a] * waves[b] for a, b in PAIRS]
    rows = products + [inverse / shear_ref, green_ratio * inverse]
    multipliers = np.stack(rows).reshape(len(rows), half, half * half).astype(np.float32)
    return split_table(plane), split_table(forward_line), split_table(backward_line), multipliers


def split(value):
    high = value.astype(bf16)
    return high, (value - high.astype(f32)).astype(bf16)


def dot(left, right):
    return lax.dot_general(left, right, (((1,), (0,)), ((), ())), preferred_element_type=f32)


def dot_t(left, right):
    return lax.dot_general(left, right, (((1,), (1,)), ((), ())), preferred_element_type=f32)


def by_table(value, high, low, contract):
    rows = value.shape[0]
    value_high, value_low = split(value)
    both = contract(jnp.concatenate([value_high, value_low], axis=0), high)
    return both[:rows] + both[rows:] + contract(value_high, low)


def table_by(high, low, value):
    value_high, value_low = split(value)
    deep = jnp.concatenate([high, low, high], axis=1)
    return dot(deep, jnp.concatenate([value_high, value_high, value_low], axis=0))


def forward_plane(value, table):
    half = value.shape[1] // 2
    low, high = value[:, :half], value[:, half:]
    even = by_table(low + high, table[0, 0], table[1, 0], dot)
    odd = by_table(low - high, table[0, 1], table[1, 1], dot)
    return jnp.concatenate([even, odd], axis=1)


def backward_plane(value, table):
    half = value.shape[1] // 2
    even = by_table(value[:, :half], table[0, 0], table[1, 0], dot_t)
    odd = by_table(value[:, half:], table[0, 1], table[1, 1], dot_t)
    return jnp.concatenate([even + odd, even - odd], axis=1)


def lane_position(shape):
    return lax.broadcasted_iota(jnp.int32, shape, 1)


def row_position(shape):
    return lax.broadcasted_iota(jnp.int32, shape, 0)


def plane_slopes(stencil, v):
    next_z = stencil.up_z(v)
    sum_z = v + next_z
    dif_z = next_z - v
    next_y = stencil.up_y(sum_z)
    return sum_z + next_y, next_y - sum_z, dif_z + stencil.up_y(dif_z)


def strain_from(slopes):
    return [
        0.25 * slopes[0][0],
        0.25 * slopes[1][1],
        0.25 * slopes[2][2],
        0.125 * (slopes[2][1] + slopes[1][2]),
        0.125 * (slopes[2][0] + slopes[0][2]),
        0.125 * (slopes[1][0] + slopes[0][1]),
    ]


class TileStencil:
    def __init__(self, shape, width):
        self.rows, self.width = shape[0], width
        lane = lane_position(shape)
        self.last_z = lane % width == width - 1
        self.inside = lane < LANES - width
        self.last_y = (lane >= LANES - width) & (row_position(shape) == self.rows - 1)

    def up_z(self, v):
        return jnp.where(self.last_z, 0.0, pltpu.roll(v, LANES - 1, 1))

    def up_y(self, v):
        turned = pltpu.roll(v, LANES - self.width, 1)
        following = pltpu.roll(turned, self.rows - 1, 0)
        return jnp.where(self.last_y, 0.0, jnp.where(self.inside, turned, following))


class Stencil:
    def __init__(self, shape, width, devices):
        self.rows, self.columns = shape
        self.width = width
        self.devices = devices
        lane = lane_position(shape)
        row = row_position((devices, self.columns))
        self.last_z = lane % width == width - 1
        self.first_z = lane % width == 0
        self.last_y = lane >= self.columns - width
        self.first_y = lane < width
        self.last_x = row == devices - 1
        self.first_x = row == 0

    def up_z(self, v):
        return jnp.where(self.last_z, 0.0, pltpu.roll(v, self.columns - 1, 1))

    def up_y(self, v):
        return jnp.where(self.last_y, 0.0, pltpu.roll(v, self.columns - self.width, 1))

    def up_x(self, v):
        wrapped = jnp.where(self.last_x, 0.0, pltpu.roll(v[: self.devices], self.devices - 1, 0))
        return wrapped if self.rows == self.devices else jnp.concatenate([v[self.devices :], wrapped], axis=0)

    def down_z(self, v):
        return jnp.where(self.first_z, 0.0, pltpu.roll(v, 1, 1))

    def down_y(self, v):
        return jnp.where(self.first_y, 0.0, pltpu.roll(v, self.width, 1))

    def down_x(self, v):
        wrapped = jnp.where(self.first_x, 0.0, pltpu.roll(v[self.rows - self.devices :], 1, 0))
        return wrapped if self.rows == self.devices else jnp.concatenate([wrapped, v[: self.rows - self.devices]], axis=0)

    def strain(self, field):
        slopes = []
        for v in field:
            sums, along_y, along_z = plane_slopes(self, v)
            slopes.append((self.up_x(sums) - sums, along_y + self.up_x(along_y), along_z + self.up_x(along_z)))
        return strain_from(slopes)

    def force(self, stress):
        result = []
        for b in range(3):
            along_x, along_y, along_z = (stress[SLOT[(a, b)]] for a in range(3))
            sum_x = along_x + self.down_z(along_x)
            first = sum_x + self.down_y(sum_x)
            sum_y = along_y + self.down_z(along_y)
            dif_z = self.down_z(along_z) - along_z
            back = self.down_y(sum_y)
            rest = (back - sum_y) + (dif_z + self.down_y(dif_z))
            result.append(0.25 * ((self.down_x(first) - first) + (rest + self.down_x(rest))))
        return result


def total(value):
    return jnp.sum(jnp.sum(value, axis=0, keepdims=True), axis=1, keepdims=True)


def measure(stress):
    return (
        stress[0] * stress[0]
        + stress[1] * stress[1]
        + stress[2] * stress[2]
        + 2.0 * (stress[3] * stress[3] + stress[4] * stress[4] + stress[5] * stress[5])
    )


def remaining(shear, size, steps, most):
    stiff = (2.0 * shear) * (2.0 * shear) * size

    def relax(count, left):
        ratio = stiff * left * left
        return left * ((1.0 - relax_rate) + relax_rate / (1.0 + ratio))

    left = lax.fori_loop(0, steps, relax, jnp.ones_like(stiff))
    return left, stiff * left * left


def deviator_of(strain):
    trace = strain[0] + strain[1] + strain[2]
    third = trace / 3.0
    return trace, [strain[0] - third, strain[1] - third, strain[2] - third] + list(strain[3:])


LAME_UNIT = 2.0**8
SHEAR_UNIT = 2.0**9
CODE_BASE = 2.0**11
LABEL_BASE = 2.0**12
LANES = 128
SUM_ROWS = 8


def encode(lame, shear):
    return (lame.astype(f32) * LAME_UNIT) * CODE_BASE + shear.astype(f32) * SHEAR_UNIT


def decode(code):
    high = jnp.floor(code * (1.0 / CODE_BASE))
    return high * (1.0 / LAME_UNIT), (code - high * CODE_BASE) * (1.0 / SHEAR_UNIT)


def pack_kernel(layers, moved_ref, sample_ref, force_ref, lame_ref, shear_ref, packet_ref, wide):
    devices, local_count, planes, columns = lame_ref.shape
    tiles = columns // LANES
    for device in range(devices):
        for local in range(local_count):
            code = encode(lame_ref[device, local], shear_ref[device, local])
            for tile in range(tiles):
                packet_ref[device, pl.ds(local * planes * tiles + tile, planes, stride=tiles), :] = code[
                    :, tile * LANES : (tile + 1) * LANES
                ]
    width = moved_ref.shape[1]
    beside = LANES // width
    start = 0
    for ref in (moved_ref, sample_ref, force_ref):
        rows = ref.shape[0]
        wide[start : start + rows, :] = jnp.concatenate([ref[...].astype(f32)] * beside, axis=1)
        start += rows
    count = start // beside
    slot = lane_position((count, LANES)) // width
    merged = wide[pl.ds(0, count, stride=beside), :]
    for place in range(1, beside):
        merged = jnp.where(slot == place, wide[pl.ds(place, count, stride=beside), :], merged)
    nodes = 3 * count // 7
    each = nodes // (3 * layers)
    labels = [merged[nodes + layer * each : nodes + (layer + 1) * each] for layer in range(layers)]
    at = local_count * planes * tiles
    for part in range(3):
        for device in range(devices):
            packet_ref[device, at : at + each, :] = merged[part * layers * each : (part * layers + 1) * each]
        at += each
    for first in range(0, layers, 2):
        pair = labels[first] * LABEL_BASE
        if first + 1 < layers:
            pair = pair + labels[first + 1]
        for device in range(devices):
            packet_ref[device, at : at + each, :] = pair
        at += each
    pull = merged[count - nodes :] - spring_rate * merged[:nodes]
    part = force_rows(layers) * each
    for device in range(devices):
        packet_ref[device, at : at + part, :] = pull[:part] if device % 2 == 0 else pull[nodes - part :]
    at += part
    stencil = TileStencil((each, LANES), width)
    slopes = [
        [plane_slopes(stencil, merged[(c * layers + layer) * each : (c * layers + layer + 1) * each]) for c in range(3)]
        for layer in range(layers)
    ]
    strains = []
    for layer in range(layers):
        below = [(-sums, along_y, along_z) for sums, along_y, along_z in slopes[layer]]
        if layer + 1 < layers:
            below = [tuple(low + high for low, high in zip(*both)) for both in zip(below, slopes[layer + 1])]
        strains.append(strain_from(below) + [jnp.ones((each, LANES), f32)])
    start = lax.axis_index("grp") * (devices * local_count)
    for device in range(devices):
        for local in range(local_count):
            own = (start + device * local_count + local).astype(f32)
            hits = [label == own for label in labels]
            for c in range(7):
                value = sum(jnp.where(hit, strain[c], 0.0) for hit, strain in zip(hits, strains))
                row = at + local * SUM_ROWS + c
                packet_ref[device, row : row + 1, :] = jnp.sum(value, axis=0, keepdims=True)
            packet_ref[device, at + local * SUM_ROWS + 7 : at + (local + 1) * SUM_ROWS, :] = jnp.zeros((1, LANES), f32)


def force_rows(layers):
    return (3 * layers + 1) // 2


def read_plane(packet_ref, row, devices, tiles):
    step = packet_ref.shape[0] // devices
    return jnp.concatenate(
        [packet_ref[pl.ds(row + tile, devices, stride=step), :] for tile in range(tiles)], axis=1
    )


def read_label(packet_ref, base, layer, devices, tiles):
    both = read_plane(packet_ref, base + (3 + layer // 2) * tiles, devices, tiles)
    high = jnp.floor(both * (1.0 / LABEL_BASE))
    return high if layer % 2 == 0 else both - high * LABEL_BASE


def read_force(packet_ref, other_ref, base, layers, forces, even):
    _, rows, columns = forces.shape
    devices = rows // layers
    tiles = columns // LANES
    step = packet_ref.shape[0] // devices
    start = base + (3 + (layers + 1) // 2) * tiles
    held = force_rows(layers)
    for part in range(3):
        for layer in range(layers):
            row = part * layers + layer
            first = row < held
            local = row if first else row - (3 * layers - held)
            for tile in range(tiles):
                at = pl.ds(start + local * tiles + tile, devices, stride=step)
                mine, other = packet_ref[at, :], other_ref[at, :]
                piece = jnp.where(even, mine, other) if first else jnp.where(even, other, mine)
                forces[part, layer * devices : (layer + 1) * devices, tile * LANES : (tile + 1) * LANES] = piece


def micro_kernel(
    local, local_count, layers, steps_hbm, packet_hbm, mult_hbm, fwd_hbm, bwd_hbm, table_hbm,
    sent_hbm, response_hbm, packet_ref, moduli, mult_ref, fwd_ref, bwd_ref, table, spectrum, ordered, sent_ref, response_ref, steps_ref, sem
):
    devices, planes = sent_ref.shape[0], sent_ref.shape[1] // 6
    vox, columns = moduli.shape[1:]
    half = vox // 2
    quarter = half * half
    pairs = [(packet_hbm, packet_ref), (steps_hbm, steps_ref)]
    pairs += [(table_hbm.at[part, fold], table.at[part, fold]) for fold in range(2) for part in range(2)]
    pairs += [(fwd_hbm, fwd_ref), (mult_hbm, mult_ref), (bwd_hbm, bwd_ref)]
    copies = [pltpu.make_async_copy(source, target, sem.at[i]) for i, (source, target) in enumerate(pairs)]
    for copy in copies:
        copy.start()
    own = (lax.axis_index("grp") * lax.axis_size("dev") + lax.axis_index("dev")) * local_count + local
    copies[1].wait()
    steps = steps_ref[own]
    copies[0].wait()
    tiles = columns // LANES
    step = packet_ref.shape[0] // devices
    for device in range(devices):
        for tile in range(tiles):
            at = device * step + local * planes * tiles + tile
            code = packet_ref[pl.ds(at, planes, stride=tiles), :]
            for kind, value in enumerate(decode(code)):
                moduli[
                    kind, device * planes : (device + 1) * planes, tile * LANES : (tile + 1) * LANES
                ] = value
    base = local_count * planes * tiles
    stencil = Stencil((devices, columns), vox_width(columns), devices)
    following = []
    for c in range(3):
        plane = read_plane(packet_ref, base + c * tiles, devices, tiles)
        following.append(plane_slopes(stencil, stencil.up_x(plane)))
    mine = read_label(packet_ref, base, layers - 1, devices, tiles) == own.astype(f32)
    sums = 0.0
    for device in range(devices):
        at = (device + 1) * step - (local_count - local) * SUM_ROWS
        sums = sums + packet_ref[at : at + SUM_ROWS, :]
    sums = jnp.sum(sums, axis=1, keepdims=True)
    load = [
        (sums[c : c + 1] + total(jnp.where(mine, part, 0.0))) / sums[6:7]
        for c, part in enumerate(strain_from(following))
    ]
    trace, dev = deviator_of(load)
    lame = moduli[0]
    shear = moduli[1]
    size = measure([0.5 * part for part in dev])
    left, _ = remaining(shear, jnp.broadcast_to(size, shear.shape), steps, 4)
    bulk = lame + (2.0 / 3.0) * shear
    sources = jnp.concatenate([bulk * trace, 2.0 * shear * left], axis=0)
    for copy in copies[2:]:
        copy.wait()
    spectral = table_by(fwd_ref[0], fwd_ref[1], forward_plane(sources, table))

    def block(field, px, py, pz):
        rows = slice(field * vox + px * half, field * vox + (px + 1) * half)
        start = (pz * 2 + py) * quarter // 2
        return rows, [slice(fold * 2 * quarter + start, fold * 2 * quarter + start + quarter // 2) for fold in range(2)]

    def take(field, parity):
        rows, pieces = block(field, *parity)
        return jnp.concatenate([spectral[rows, lanes] for lanes in pieces], axis=1)

    parities = [(px, py, pz) for px in range(2) for py in range(2) for pz in range(2)]
    product = [mult_ref[i] for i in range(6)]
    inverse = mult_ref[6]
    scaled = mult_ref[7]

    def second(blocks, parity, a, b):
        if a == b:
            return -(product[SLOT[(a, b)]] * blocks[parity])
        other = tuple(1 - p if axis in (a, b) else p for axis, p in enumerate(parity))
        value = product[SLOT[(a, b)]] * blocks[other]
        return value if parity[a] == parity[b] else -value

    psi = {}
    raw = {}
    for parity in parities:
        raw[parity] = take(1, parity)
        psi[parity] = inverse * raw[parity]
    phi = {}
    for parity in parities:
        pressed = sum(
            (1.0 if a == b else 2.0) * dev[SLOT[(a, b)]] * second(psi, parity, a, b) for a, b in PAIRS
        )
        phi[parity] = (1.0 - green_ratio) * inverse * take(0, parity) + scaled * pressed
    for parity in parities:
        curl = {pair: second(psi, parity, *pair) for pair in PAIRS}
        for index, (a, b) in enumerate(PAIRS):
            def at(i, j):
                return curl[(min(i, j), max(i, j))]
            if a == b:
                sheared = sum(dev[SLOT[(b, c)]] * at(a, c) for c in range(3))
            else:
                sheared = 0.5 * sum(dev[SLOT[(b, c)]] * at(a, c) + dev[SLOT[(a, c)]] * at(b, c) for c in range(3))
            value = second(phi, parity, a, b) + sheared
            rows, pieces = block(index, *parity)
            for fold, lanes in enumerate(pieces):
                spectrum[rows, lanes] = value[:, fold * quarter // 2 : (fold + 1) * quarter // 2]
    moved = table_by(bwd_ref[0], bwd_ref[1], backward_plane(spectrum[...], table))
    if 2 * planes == 8:
        low = row_position((2 * planes, columns)) < planes
        for pair in range(3):
            for chip in range(devices // 2):
                first, second_ = (
                    moved[i * vox + 2 * chip * planes : i * vox + 2 * (chip + 1) * planes]
                    for i in (2 * pair, 2 * pair + 1)
                )
                rows = slice(2 * pair * planes, 2 * (pair + 1) * planes)
                ordered[2 * chip, rows] = jnp.where(low, first, pltpu.roll(second_, planes, 0))
                ordered[2 * chip + 1, rows] = jnp.where(low, pltpu.roll(first, planes, 0), second_)
    else:
        for i in range(6):
            for device in range(devices):
                ordered[device, i * planes : (i + 1) * planes] = moved[
                    i * vox + device * planes : i * vox + (device + 1) * planes
                ]
    for device in range(devices):
        sent_ref[device] = ordered[device].astype(bf16)
    send = pltpu.make_async_copy(sent_ref, sent_hbm, sem.at[len(pairs)])
    send.start()
    strain = [load[i] + moved[i * vox : (i + 1) * vox] for i in range(6)]
    trace, dev = deviator_of(strain)
    left, ratio = remaining(shear, measure([0.5 * part for part in dev]), steps, 4)
    push = bulk * trace
    pull = 2.0 * shear * left
    stress = [push + pull * dev[i] for i in range(3)] + [pull * dev[i] for i in range(3, 6)]
    parts = stress + [lame, shear / (1.0 + ratio)]
    lane = lane_position((1, response_ref.shape[1]))
    row = jnp.zeros(lane.shape, f32)
    for index, part in enumerate(parts):
        row = jnp.where(lane == index, total(part) / float(vox * columns), row)
    for index, part in enumerate(load):
        row = jnp.where(lane == 8 + index, part, row)
    response_ref[...] = jnp.broadcast_to(row, response_ref.shape)
    answer = pltpu.make_async_copy(response_ref, response_hbm, sem.at[len(pairs) + 1])
    answer.start()
    send.wait()
    answer.wait()


def vox_width(columns):
    width = int(round(columns**0.5))
    return width


def macro_kernel(
    layers, base, slots_ref, table_ref, table_v_ref, packet_ref, other_ref, next_ref, row_ref, labels, forces, cells, result
):
    columns = next_ref.shape[2]
    devices = labels.shape[0] // layers
    samples = table_v_ref.shape[0]
    rank = lax.axis_index("dev")
    group = lax.axis_index("grp")
    local_count = row_ref.shape[0]
    group_size = local_count * devices
    start = group * group_size
    for local in range(local_count):
        chosen = jnp.int32(0)
        for j in range(group_size):
            chosen = jnp.where(slots_ref[start + j] == rank * local_count + local, start + j, chosen)
        row_ref[local : local + 1, :] = table_v_ref[pl.ds(chosen, 1), 0:8]
    for layer in range(layers):
        labels[layer * devices : (layer + 1) * devices, :] = read_label(
            packet_ref, base, layer, devices, columns // LANES
        )
    read_force(packet_ref, other_ref, base, layers, forces, rank % 2 == 0)
    rows = labels.shape[0]
    height = min(8, rows)
    span = min(512, columns)
    for top in range(0, rows, height):
        for side in range(0, columns, span):
            where = (slice(top, top + height), slice(side, side + span))
            label = labels[where]

            def pick(sample, held):
                here = label == sample.astype(f32)
                return tuple(jnp.where(here, table_ref[sample, c], held[c]) for c in range(8))

            zero = jnp.zeros((height, span), f32)
            held = lax.fori_loop(0, samples, pick, (zero,) * 8, unroll=4)
            for c in range(8):
                cells[(c,) + where] = held[c]
    stencil = Stencil(labels.shape, vox_width(columns), devices)
    stress = [cells[c] for c in range(6)]
    pulled = stencil.force(stress)
    remainder = [forces[b] - pulled[b] for b in range(3)]
    direction = remainder
    norm_now = total(sum(r * r for r in remainder))
    update = None
    lame = cells[6]
    shear = 2.0 * cells[7]
    for turn in range(CG_STEPS):
        strain = stencil.strain(direction)
        pressure = lame * (strain[0] + strain[1] + strain[2])
        stress = [shear * strain[i] + pressure for i in range(3)] + [shear * strain[i] for i in range(3, 6)]
        pulled = stencil.force(stress)
        image = [pulled[b] + spring_rate * direction[b] for b in range(3)]
        alpha = norm_now / total(sum(direction[b] * image[b] for b in range(3)))
        moved = [alpha * direction[b] for b in range(3)]
        update = moved if update is None else [update[b] + moved[b] for b in range(3)]
        if turn + 1 < CG_STEPS:
            remainder = [remainder[b] - alpha * image[b] for b in range(3)]
            norm_next = total(sum(r * r for r in remainder))
            grow = norm_next / norm_now
            direction = [remainder[b] + grow * direction[b] for b in range(3)]
            norm_now = norm_next
    for b in range(3):
        result[b] = update[b]
        for layer in range(layers):
            next_ref[b, layer : layer + 1, :] = result[b, pl.ds(layer * devices + rank, 1), :]


def vmem():
    return pl.BlockSpec(memory_space=pltpu.VMEM)


def hbm():
    return pl.BlockSpec(memory_space=pltpu.HBM)


def smem():
    return pl.BlockSpec(memory_space=pltpu.SMEM)


def shards(
    displacement, external_force, element_sample, lame_field, shear_field, plastic_steps, owner_slot
):
    group_size, planes, columns = lame_field.shape
    devices = lax.axis_size("dev")
    groups = lax.axis_size("grp")
    local_count = group_size // devices
    vox = planes * devices
    layers = displacement.shape[1]
    width = displacement.shape[2] * displacement.shape[3]
    plane, forward_line, backward_line, multipliers = tables(vox)
    pack_params, params, macro_params = (
        pltpu.CompilerParams(vmem_limit_bytes=size * 1024 * 1024) for size in (60, 60, 16)
    )

    side = displacement.shape[3]
    lines = layers * displacement.shape[2]
    tiles = columns // LANES
    base = local_count * planes * tiles
    length = base + (3 + (layers + 1) // 2 + force_rows(layers)) * tiles + local_count * SUM_ROWS
    packet = pl.pallas_call(
        functools.partial(pack_kernel, layers),
        name="pack",
        out_shape=jax.ShapeDtypeStruct((devices, length, LANES), f32),
        in_specs=[vmem()] * 5,
        out_specs=vmem(),
        scratch_shapes=[pltpu.VMEM((7 * lines, LANES), f32)],
        compiler_params=pack_params,
    )(
        displacement.reshape(3 * lines, side), element_sample.reshape(lines, side),
        external_force.reshape(3 * lines, side),
        lame_field.reshape(devices, local_count, planes, columns),
        shear_field.reshape(devices, local_count, planes, columns),
    )
    packets = lax.all_to_all(packet, "dev", split_axis=0, concat_axis=0, tiled=True).reshape(devices * length, LANES)
    neighbour = lax.ppermute(packets, "dev", [(i, i ^ 1) for i in range(devices)])
    everyone = groups * devices
    sents = []
    rows = []
    for local in range(local_count):
        sent, response = pl.pallas_call(
            functools.partial(micro_kernel, local, local_count, layers),
            name="micro",
            out_shape=(
                jax.ShapeDtypeStruct((devices, 6 * planes, columns), bf16),
                jax.ShapeDtypeStruct((everyone, 16), f32),
            ),
            in_specs=[hbm()] * 6,
            out_specs=(hbm(), hbm()),
            scratch_shapes=[
                pltpu.VMEM((devices * length, LANES), f32),
                pltpu.VMEM((2, vox, columns), f32),
                pltpu.VMEM(multipliers.shape, f32),
                pltpu.VMEM(forward_line.shape, bf16),
                pltpu.VMEM(backward_line.shape, bf16),
                pltpu.VMEM(plane.shape, bf16),
                pltpu.VMEM((6 * vox, columns), f32),
                pltpu.VMEM((devices, 6 * planes, columns), f32),
                pltpu.VMEM((devices, 6 * planes, columns), bf16),
                pltpu.VMEM((everyone, 16), f32),
                pltpu.SMEM(plastic_steps.shape, jnp.int32),
                pltpu.SemaphoreType.DMA((11,)),
            ],
            compiler_params=params,
        )(
            plastic_steps, packets, multipliers, forward_line, backward_line, plane,
        )
        sents.append(sent)
        rows.append(response)
    gathered = lax.all_to_all(
        jnp.stack(rows, axis=1), ("grp", "dev"), split_axis=0, concat_axis=0, tiled=True
    ).reshape(everyone * local_count, 16)
    moved = lax.all_to_all(jnp.stack(sents, axis=1), "dev", split_axis=0, concat_axis=0, tiled=True)
    group_rows = lax.dynamic_slice_in_dim(gathered, lax.axis_index("grp") * group_size, group_size)
    loads = group_rows[:, 8:14].T
    change = jnp.transpose(moved.reshape(group_size, 6, planes, columns), (1, 0, 2, 3))
    micro_strain = loads[:, :, None, None] + change.astype(f32)
    following, picked = pl.pallas_call(
        functools.partial(macro_kernel, layers, base),
        name="macro",
        out_shape=(
            jax.ShapeDtypeStruct((3, layers, width), f32),
            jax.ShapeDtypeStruct((local_count, 8), f32),
        ),
        in_specs=[smem(), smem()] + [vmem()] * 3,
        out_specs=(vmem(), vmem()),
        scratch_shapes=[
            pltpu.VMEM((devices * layers, width), f32),
            pltpu.VMEM((3, devices * layers, width), f32),
            pltpu.VMEM((8, devices * layers, width), f32),
            pltpu.VMEM((3, devices * layers, width), f32),
        ],
        compiler_params=macro_params,
    )(owner_slot, gathered, gathered, packets, neighbour)
    return (displacement + following.reshape(displacement.shape), picked, micro_strain)


def solution(mesh):
    in_specs = (
        P(None, "dev", None, None),
        P(None, "dev", None, None),
        P("dev", None, None),
        P("grp", "dev", None),
        P("grp", "dev", None),
        P(),
        P(),
    )
    out_specs = (P(None, "dev", None, None), P(("grp", "dev"), None), P(None, "grp", "dev", None))
    return jax.shard_map(shards, mesh=mesh, in_specs=in_specs, out_specs=out_specs, check_vma=False)
```

```python
import functools
import jax
import jax.numpy as jnp
import numpy as np
from jax import lax
from jax.experimental import pallas as pl
from jax.experimental.pallas import tpu as pltpu
from jax.sharding import PartitionSpec as P

CG_STEPS = 3
shear_ref = 1.65
lame_ref = 1.25
green_ratio = (lame_ref + shear_ref) / (lame_ref + 2.0 * shear_ref)
relax_rate = 0.35
flow_scale = 4.0
spring_rate = 0.2
f32 = jnp.float32
bf16 = jnp.bfloat16
DIAG = ((0, 0), (1, 1), (2, 2))
PAIRS = ((0, 0), (1, 1), (2, 2), (1, 2), (0, 2), (0, 1))
SLOT = {(0, 0): 0, (1, 1): 1, (2, 2): 2, (1, 2): 3, (2, 1): 3, (0, 2): 4, (2, 0): 4, (0, 1): 5, (1, 0): 5}


def split_table(table):
    high = table.astype(np.float32).astype(bf16)
    low = (table - high.astype(np.float64)).astype(np.float32).astype(bf16)
    return np.stack([high, low])


def tables(vox):
    half = vox // 2
    n = np.arange(vox)[:, None]
    k = np.arange(half)[None, :]
    angle = 2.0 * np.pi * (n * k % vox) / vox
    cosine = np.cos(angle) * np.sqrt(2.0 / vox)
    sine = np.sin(angle) * np.sqrt(2.0 / vox)
    cosine[:, 0] = 1.0 / np.sqrt(vox)
    sine[:, 0] = (1.0 - 2.0 * (np.arange(vox) % 2)) / np.sqrt(vox)
    basis = np.concatenate([cosine, sine], axis=1)
    order = np.concatenate([np.arange(0, half, 2), np.arange(1, half, 2)])
    by_parity = basis.reshape(vox, 2, half)
    folded = by_parity[:half, :, order].reshape(half, 2, 2, half // 2)
    plane = np.einsum("ypek,zql->eyzqpkl", folded, by_parity).reshape(2, half * vox, half * vox)
    line = basis.T
    forward_line = np.kron(np.eye(2), line)
    backward_line = np.kron(np.eye(6), line.T)
    wave = np.sin(2.0 * np.pi * np.arange(half) / vox)
    wave[0] = 0.0
    first = np.broadcast_to(wave[:, None, None], (half, half, half))
    second = np.broadcast_to(wave[order][None, :, None], (half, half, half))
    third = np.broadcast_to(wave[None, None, :], (half, half, half))
    square = first**2 + second**2 + third**2
    inverse = np.where(square > 0.0, 1.0 / np.where(square > 0.0, square, 1.0), 0.0)
    waves = (first, second, third)
    products = [waves[a] * waves[b] for a, b in PAIRS]
    rows = products + [inverse / shear_ref, green_ratio * inverse]
    multipliers = np.stack(rows).reshape(len(rows), half, half * half).astype(np.float32)
    return split_table(plane), split_table(forward_line), split_table(backward_line), multipliers


def split(value):
    high = value.astype(bf16)
    return high, (value - high.astype(f32)).astype(bf16)


def dot(left, right):
    return lax.dot_general(left, right, (((1,), (0,)), ((), ())), preferred_element_type=f32)


def dot_t(left, right):
    return lax.dot_general(left, right, (((1,), (1,)), ((), ())), preferred_element_type=f32)


def by_table(value, high, low, contract):
    rows = value.shape[0]
    value_high, value_low = split(value)
    both = contract(jnp.concatenate([value_high, value_low], axis=0), high)
    return both[:rows] + both[rows:] + contract(value_high, low)


def table_by(high, low, value):
    value_high, value_low = split(value)
    deep = jnp.concatenate([high, low, high], axis=1)
    return dot(deep, jnp.concatenate([value_high, value_high, value_low], axis=0))


def forward_plane(value, table):
    half = value.shape[1] // 2
    low, high = value[:, :half], value[:, half:]
    even = by_table(low + high, table[0, 0], table[1, 0], dot)
    odd = by_table(low - high, table[0, 1], table[1, 1], dot)
    return jnp.concatenate([even, odd], axis=1)


def backward_plane(value, table):
    half = value.shape[1] // 2
    even = by_table(value[:, :half], table[0, 0], table[1, 0], dot_t)
    odd = by_table(value[:, half:], table[0, 1], table[1, 1], dot_t)
    return jnp.concatenate([even + odd, even - odd], axis=1)


def lane_position(shape):
    return lax.broadcasted_iota(jnp.int32, shape, 1)


def row_position(shape):
    return lax.broadcasted_iota(jnp.int32, shape, 0)


def plane_slopes(stencil, v):
    next_z = stencil.up_z(v)
    sum_z = v + next_z
    dif_z = next_z - v
    next_y = stencil.up_y(sum_z)
    return sum_z + next_y, next_y - sum_z, dif_z + stencil.up_y(dif_z)


def strain_from(slopes):
    return [
        0.25 * slopes[0][0],
        0.25 * slopes[1][1],
        0.25 * slopes[2][2],
        0.125 * (slopes[2][1] + slopes[1][2]),
        0.125 * (slopes[2][0] + slopes[0][2]),
        0.125 * (slopes[1][0] + slopes[0][1]),
    ]


class TileStencil:
    def __init__(self, shape, width):
        self.rows, self.width = shape[0], width
        lane = lane_position(shape)
        self.last_z = lane % width == width - 1
        self.inside = lane < LANES - width
        self.last_y = (lane >= LANES - width) & (row_position(shape) == self.rows - 1)

    def up_z(self, v):
        return jnp.where(self.last_z, 0.0, pltpu.roll(v, LANES - 1, 1))

    def up_y(self, v):
        turned = pltpu.roll(v, LANES - self.width, 1)
        following = pltpu.roll(turned, self.rows - 1, 0)
        return jnp.where(self.last_y, 0.0, jnp.where(self.inside, turned, following))


class Stencil:
    def __init__(self, shape, width, devices):
        self.rows, self.columns = shape
        self.width = width
        self.devices = devices
        lane = lane_position(shape)
        row = row_position((devices, self.columns))
        self.last_z = lane % width == width - 1
        self.first_z = lane % width == 0
        self.last_y = lane >= self.columns - width
        self.first_y = lane < width
        self.last_x = row == devices - 1
        self.first_x = row == 0

    def up_z(self, v):
        return jnp.where(self.last_z, 0.0, pltpu.roll(v, self.columns - 1, 1))

    def up_y(self, v):
        return jnp.where(self.last_y, 0.0, pltpu.roll(v, self.columns - self.width, 1))

    def up_x(self, v):
        wrapped = jnp.where(self.last_x, 0.0, pltpu.roll(v[: self.devices], self.devices - 1, 0))
        return wrapped if self.rows == self.devices else jnp.concatenate([v[self.devices :], wrapped], axis=0)

    def down_z(self, v):
        return jnp.where(self.first_z, 0.0, pltpu.roll(v, 1, 1))

    def down_y(self, v):
        return jnp.where(self.first_y, 0.0, pltpu.roll(v, self.width, 1))

    def down_x(self, v):
        wrapped = jnp.where(self.first_x, 0.0, pltpu.roll(v[self.rows - self.devices :], 1, 0))
        return wrapped if self.rows == self.devices else jnp.concatenate([wrapped, v[: self.rows - self.devices]], axis=0)

    def strain(self, field):
        slopes = []
        for v in field:
            sums, along_y, along_z = plane_slopes(self, v)
            slopes.append((self.up_x(sums) - sums, along_y + self.up_x(along_y), along_z + self.up_x(along_z)))
        return strain_from(slopes)

    def force(self, stress):
        result = []
        for b in range(3):
            along_x, along_y, along_z = (stress[SLOT[(a, b)]] for a in range(3))
            sum_x = along_x + self.down_z(along_x)
            first = sum_x + self.down_y(sum_x)
            sum_y = along_y + self.down_z(along_y)
            dif_z = self.down_z(along_z) - along_z
            back = self.down_y(sum_y)
            rest = (back - sum_y) + (dif_z + self.down_y(dif_z))
            result.append(0.25 * ((self.down_x(first) - first) + (rest + self.down_x(rest))))
        return result


def total(value):
    return jnp.sum(jnp.sum(value, axis=0, keepdims=True), axis=1, keepdims=True)


def measure(stress):
    return (
        stress[0] * stress[0]
        + stress[1] * stress[1]
        + stress[2] * stress[2]
        + 2.0 * (stress[3] * stress[3] + stress[4] * stress[4] + stress[5] * stress[5])
    )


def remaining(shear, size, steps, most):
    stiff = (2.0 * shear) * (2.0 * shear) * size

    def relax(count, left):
        ratio = stiff * left * left
        return left * ((1.0 - relax_rate) + relax_rate / (1.0 + ratio))

    left = lax.fori_loop(0, steps, relax, jnp.ones_like(stiff))
    return left, stiff * left * left


def deviator_of(strain):
    trace = strain[0] + strain[1] + strain[2]
    third = trace / 3.0
    return trace, [strain[0] - third, strain[1] - third, strain[2] - third] + list(strain[3:])


LAME_UNIT = 2.0**8
SHEAR_UNIT = 2.0**9
CODE_BASE = 2.0**11
LABEL_BASE = 2.0**12
LANES = 128
SUM_ROWS = 4


def encode(lame, shear):
    return (lame.astype(f32) * LAME_UNIT) * CODE_BASE + shear.astype(f32) * SHEAR_UNIT


def decode(code):
    high = jnp.floor(code * (1.0 / CODE_BASE))
    return high * (1.0 / LAME_UNIT), (code - high * CODE_BASE) * (1.0 / SHEAR_UNIT)


def pack_kernel(layers, moved_ref, sample_ref, force_ref, lame_ref, shear_ref, packet_ref, wide):
    devices, local_count, planes, columns = lame_ref.shape
    tiles = columns // LANES
    for device in range(devices):
        for local in range(local_count):
            code = encode(lame_ref[device, local], shear_ref[device, local])
            for tile in range(tiles):
                packet_ref[device, pl.ds(local * planes * tiles + tile, planes, stride=tiles), :] = code[
                    :, tile * LANES : (tile + 1) * LANES
                ]
    width = moved_ref.shape[1]
    beside = LANES // width
    start = 0
    for ref in (moved_ref, sample_ref, force_ref):
        rows = ref.shape[0]
        wide[start : start + rows, :] = jnp.concatenate([ref[...].astype(f32)] * beside, axis=1)
        start += rows
    count = start // beside
    slot = lane_position((count, LANES)) // width
    merged = wide[pl.ds(0, count, stride=beside), :]
    for place in range(1, beside):
        merged = jnp.where(slot == place, wide[pl.ds(place, count, stride=beside), :], merged)
    nodes = 3 * count // 7
    each = nodes // (3 * layers)
    labels = [merged[nodes + layer * each : nodes + (layer + 1) * each] for layer in range(layers)]
    at = local_count * planes * tiles
    for part in range(3):
        for device in range(devices):
            packet_ref[device, at : at + each, :] = merged[part * layers * each : (part * layers + 1) * each]
        at += each
    for first in range(0, layers, 2):
        pair = labels[first] * LABEL_BASE
        if first + 1 < layers:
            pair = pair + labels[first + 1]
        for device in range(devices):
            packet_ref[device, at : at + each, :] = pair
        at += each
    pull = merged[count - nodes :] - spring_rate * merged[:nodes]
    part = nodes // 4
    upper = lax.axis_index("grp") % 2 == 1
    for core in range(2):
        quarter = jnp.where(upper, pull[(2 + core) * part : (3 + core) * part], pull[core * part : (core + 1) * part])
        for device in range(core, devices, 2):
            packet_ref[device, at : at + part, :] = quarter
    at += part
    stencil = TileStencil((each, LANES), width)
    slopes = [
        [plane_slopes(stencil, merged[(c * layers + layer) * each : (c * layers + layer + 1) * each]) for c in range(3)]
        for layer in range(layers)
    ]
    strains = []
    for layer in range(layers):
        below = [(-sums, along_y, along_z) for sums, along_y, along_z in slopes[layer]]
        if layer + 1 < layers:
            below = [tuple(low + high for low, high in zip(*both)) for both in zip(below, slopes[layer + 1])]
        strains.append(strain_from(below) + [jnp.ones((each, LANES), f32)])
    start = lax.axis_index("grp") * (devices * local_count)
    left = lane_position((1, LANES)) < LANES // 2
    for device in range(devices):
        for local in range(local_count):
            own = (start + device * local_count + local).astype(f32)
            hits = [label == own for label in labels]
            sums = []
            for c in range(7):
                value = sum(jnp.where(hit, strain[c], 0.0) for hit, strain in zip(hits, strains))
                value = jnp.sum(value, axis=0, keepdims=True)
                sums.append(value + pltpu.roll(value, LANES // 2, 1))
            sums.append(jnp.zeros((1, LANES), f32))
            for c in range(SUM_ROWS):
                row = at + local * SUM_ROWS + c
                packet_ref[device, row : row + 1, :] = jnp.where(left, sums[c], sums[c + SUM_ROWS])


def read_plane(packet_ref, row, devices, tiles):
    step = packet_ref.shape[0] // devices
    return jnp.concatenate(
        [packet_ref[pl.ds(row + tile, devices, stride=step), :] for tile in range(tiles)], axis=1
    )


def read_label(packet_ref, base, layer, devices, tiles):
    both = read_plane(packet_ref, base + (3 + layer // 2) * tiles, devices, tiles)
    high = jnp.floor(both * (1.0 / LABEL_BASE))
    return high if layer % 2 == 0 else both - high * LABEL_BASE


def read_force(tail_refs, layers, forces):
    _, rows, columns = forces.shape
    devices = rows // layers
    tiles = columns // LANES
    step = tail_refs[0].shape[0] // devices
    part = 3 * layers * tiles // 4
    odd_core = lax.axis_index("dev") % 2
    odd_group = lax.axis_index("grp") % 2
    for row in range(3 * layers):
        for tile in range(tiles):
            quarter, at = divmod(row * tiles + tile, part)
            own, core, side, across = (ref[pl.ds(at, devices, stride=step), :] for ref in tail_refs)
            same_core = odd_core == quarter % 2
            here, there = jnp.where(same_core, own, core), jnp.where(same_core, side, across)
            c, layer = divmod(row, layers)
            forces[c, layer * devices : (layer + 1) * devices, tile * LANES : (tile + 1) * LANES] = jnp.where(
                odd_group == quarter // 2, here, there
            )


def micro_kernel(
    local, local_count, layers, steps_hbm, packet_hbm, mult_hbm, fwd_hbm, bwd_hbm, table_hbm,
    sent_hbm, response_hbm, packet_ref, moduli, mult_ref, fwd_ref, bwd_ref, table, spectrum, ordered, sent_ref, response_ref, steps_ref, sem
):
    devices, planes = sent_ref.shape[0], sent_ref.shape[1] // 6
    vox, columns = moduli.shape[1:]
    half = vox // 2
    quarter = half * half
    pairs = [(packet_hbm, packet_ref), (steps_hbm, steps_ref)]
    pairs += [(table_hbm.at[part, fold], table.at[part, fold]) for fold in range(2) for part in range(2)]
    pairs += [(fwd_hbm, fwd_ref), (mult_hbm, mult_ref), (bwd_hbm, bwd_ref)]
    copies = [pltpu.make_async_copy(source, target, sem.at[i]) for i, (source, target) in enumerate(pairs)]
    for copy in copies:
        copy.start()
    own = (lax.axis_index("grp") * lax.axis_size("dev") + lax.axis_index("dev")) * local_count + local
    copies[1].wait()
    steps = steps_ref[own]
    copies[0].wait()
    tiles = columns // LANES
    step = packet_ref.shape[0] // devices
    for device in range(devices):
        for tile in range(tiles):
            at = device * step + local * planes * tiles + tile
            code = packet_ref[pl.ds(at, planes, stride=tiles), :]
            for kind, value in enumerate(decode(code)):
                moduli[
                    kind, device * planes : (device + 1) * planes, tile * LANES : (tile + 1) * LANES
                ] = value
    base = local_count * planes * tiles
    stencil = Stencil((devices, columns), vox_width(columns), devices)
    following = []
    for c in range(3):
        plane = read_plane(packet_ref, base + c * tiles, devices, tiles)
        following.append(plane_slopes(stencil, stencil.up_x(plane)))
    mine = read_label(packet_ref, base, layers - 1, devices, tiles) == own.astype(f32)
    sums = 0.0
    for device in range(devices):
        at = (device + 1) * step - (local_count - local) * SUM_ROWS
        sums = sums + packet_ref[at : at + SUM_ROWS, :]
    left_half = lane_position(sums.shape) < LANES // 2
    sums = [jnp.sum(jnp.where(left_half == side, sums, 0.0), axis=1, keepdims=True) for side in (True, False)]
    sums = [half_sums[row : row + 1] for half_sums in sums for row in range(SUM_ROWS)]
    load = [
        (sums[c] + total(jnp.where(mine, part, 0.0))) / sums[6] for c, part in enumerate(strain_from(following))
    ]
    trace, dev = deviator_of(load)
    lame = moduli[0]
    shear = moduli[1]
    size = measure([0.5 * part for part in dev])
    left, _ = remaining(shear, jnp.broadcast_to(size, shear.shape), steps, 4)
    bulk = lame + (2.0 / 3.0) * shear
    sources = jnp.concatenate([bulk * trace, 2.0 * shear * left], axis=0)
    for copy in copies[2:]:
        copy.wait()
    spectral = table_by(fwd_ref[0], fwd_ref[1], forward_plane(sources, table))

    def block(field, px, py, pz):
        rows = slice(field * vox + px * half, field * vox + (px + 1) * half)
        start = (pz * 2 + py) * quarter // 2
        return rows, [slice(fold * 2 * quarter + start, fold * 2 * quarter + start + quarter // 2) for fold in range(2)]

    def take(field, parity):
        rows, pieces = block(field, *parity)
        return jnp.concatenate([spectral[rows, lanes] for lanes in pieces], axis=1)

    parities = [(px, py, pz) for px in range(2) for py in range(2) for pz in range(2)]
    product = [mult_ref[i] for i in range(6)]
    inverse = mult_ref[6]
    scaled = mult_ref[7]

    def second(blocks, parity, a, b):
        if a == b:
            return -(product[SLOT[(a, b)]] * blocks[parity])
        other = tuple(1 - p if axis in (a, b) else p for axis, p in enumerate(parity))
        value = product[SLOT[(a, b)]] * blocks[other]
        return value if parity[a] == parity[b] else -value

    psi = {}
    raw = {}
    for parity in parities:
        raw[parity] = take(1, parity)
        psi[parity] = inverse * raw[parity]
    phi = {}
    for parity in parities:
        pressed = sum(
            (1.0 if a == b else 2.0) * dev[SLOT[(a, b)]] * second(psi, parity, a, b) for a, b in PAIRS
        )
        phi[parity] = (1.0 - green_ratio) * inverse * take(0, parity) + scaled * pressed
    for parity in parities:
        curl = {pair: second(psi, parity, *pair) for pair in PAIRS}
        for index, (a, b) in enumerate(PAIRS):
            def at(i, j):
                return curl[(min(i, j), max(i, j))]
            if a == b:
                sheared = sum(dev[SLOT[(b, c)]] * at(a, c) for c in range(3))
            else:
                sheared = 0.5 * sum(dev[SLOT[(b, c)]] * at(a, c) + dev[SLOT[(a, c)]] * at(b, c) for c in range(3))
            value = second(phi, parity, a, b) + sheared
            rows, pieces = block(index, *parity)
            for fold, lanes in enumerate(pieces):
                spectrum[rows, lanes] = value[:, fold * quarter // 2 : (fold + 1) * quarter // 2]
    moved = table_by(bwd_ref[0], bwd_ref[1], backward_plane(spectrum[...], table))
    if 2 * planes == 8:
        low = row_position((2 * planes, columns)) < planes
        for pair in range(3):
            for chip in range(devices // 2):
                first, second_ = (
                    moved[i * vox + 2 * chip * planes : i * vox + 2 * (chip + 1) * planes]
                    for i in (2 * pair, 2 * pair + 1)
                )
                rows = slice(2 * pair * planes, 2 * (pair + 1) * planes)
                ordered[2 * chip, rows] = jnp.where(low, first, pltpu.roll(second_, planes, 0))
                ordered[2 * chip + 1, rows] = jnp.where(low, pltpu.roll(first, planes, 0), second_)
    else:
        for i in range(6):
            for device in range(devices):
                ordered[device, i * planes : (i + 1) * planes] = moved[
                    i * vox + device * planes : i * vox + (device + 1) * planes
                ]
    for device in range(devices):
        sent_ref[device] = ordered[device].astype(bf16)
    send = pltpu.make_async_copy(sent_ref, sent_hbm, sem.at[len(pairs)])
    send.start()
    strain = [load[i] + moved[i * vox : (i + 1) * vox] for i in range(6)]
    trace, dev = deviator_of(strain)
    left, ratio = remaining(shear, measure([0.5 * part for part in dev]), steps, 4)
    push = bulk * trace
    pull = 2.0 * shear * left
    stress = [push + pull * dev[i] for i in range(3)] + [pull * dev[i] for i in range(3, 6)]
    parts = stress + [lame, shear / (1.0 + ratio)]
    lane = lane_position((1, response_ref.shape[1]))
    row = jnp.zeros(lane.shape, f32)
    for index, part in enumerate(parts):
        row = jnp.where(lane == index, total(part) / float(vox * columns), row)
    for index, part in enumerate(load):
        row = jnp.where(lane == 8 + index, part, row)
    response_ref[...] = jnp.broadcast_to(row, response_ref.shape)
    answer = pltpu.make_async_copy(response_ref, response_hbm, sem.at[len(pairs) + 1])
    answer.start()
    send.wait()
    answer.wait()


def vox_width(columns):
    width = int(round(columns**0.5))
    return width


def macro_kernel(
    layers, base, slots_ref, table_ref, table_v_ref, packet_ref, own_ref, core_ref, side_ref, across_ref, next_ref, row_ref, labels, forces, cells, result
):
    columns = next_ref.shape[2]
    devices = labels.shape[0] // layers
    samples = table_v_ref.shape[0]
    rank = lax.axis_index("dev")
    group = lax.axis_index("grp")
    local_count = row_ref.shape[0]
    group_size = local_count * devices
    start = group * group_size
    for local in range(local_count):
        chosen = jnp.int32(0)
        for j in range(group_size):
            chosen = jnp.where(slots_ref[start + j] == rank * local_count + local, start + j, chosen)
        row_ref[local : local + 1, :] = table_v_ref[pl.ds(chosen, 1), 0:8]
    for layer in range(layers):
        labels[layer * devices : (layer + 1) * devices, :] = read_label(
            packet_ref, base, layer, devices, columns // LANES
        )
    read_force((own_ref, core_ref, side_ref, across_ref), layers, forces)
    rows = labels.shape[0]
    height = min(8, rows)
    span = min(512, columns)
    for top in range(0, rows, height):
        for side in range(0, columns, span):
            where = (slice(top, top + height), slice(side, side + span))
            label = labels[where]

            def pick(sample, held):
                here = label == sample.astype(f32)
                return tuple(jnp.where(here, table_ref[sample, c], held[c]) for c in range(8))

            zero = jnp.zeros((height, span), f32)
            held = lax.fori_loop(0, samples, pick, (zero,) * 8, unroll=4)
            for c in range(8):
                cells[(c,) + where] = held[c]
    stencil = Stencil(labels.shape, vox_width(columns), devices)
    stress = [cells[c] for c in range(6)]
    pulled = stencil.force(stress)
    remainder = [forces[b] - pulled[b] for b in range(3)]
    direction = remainder
    norm_now = total(sum(r * r for r in remainder))
    update = None
    lame = cells[6]
    shear = 2.0 * cells[7]
    for turn in range(CG_STEPS):
        strain = stencil.strain(direction)
        pressure = lame * (strain[0] + strain[1] + strain[2])
        stress = [shear * strain[i] + pressure for i in range(3)] + [shear * strain[i] for i in range(3, 6)]
        pulled = stencil.force(stress)
        image = [pulled[b] + spring_rate * direction[b] for b in range(3)]
        alpha = norm_now / total(sum(direction[b] * image[b] for b in range(3)))
        moved = [alpha * direction[b] for b in range(3)]
        update = moved if update is None else [update[b] + moved[b] for b in range(3)]
        if turn + 1 < CG_STEPS:
            remainder = [remainder[b] - alpha * image[b] for b in range(3)]
            norm_next = total(sum(r * r for r in remainder))
            grow = norm_next / norm_now
            direction = [remainder[b] + grow * direction[b] for b in range(3)]
            norm_now = norm_next
    for b in range(3):
        result[b] = update[b]
        for layer in range(layers):
            next_ref[b, layer : layer + 1, :] = result[b, pl.ds(layer * devices + rank, 1), :]


def vmem():
    return pl.BlockSpec(memory_space=pltpu.VMEM)


def hbm():
    return pl.BlockSpec(memory_space=pltpu.HBM)


def smem():
    return pl.BlockSpec(memory_space=pltpu.SMEM)


def shards(
    displacement, external_force, element_sample, lame_field, shear_field, plastic_steps, owner_slot
):
    group_size, planes, columns = lame_field.shape
    devices = lax.axis_size("dev")
    groups = lax.axis_size("grp")
    local_count = group_size // devices
    vox = planes * devices
    layers = displacement.shape[1]
    width = displacement.shape[2] * displacement.shape[3]
    plane, forward_line, backward_line, multipliers = tables(vox)
    pack_params, params, macro_params = (
        pltpu.CompilerParams(vmem_limit_bytes=size * 1024 * 1024) for size in (60, 60, 16)
    )

    side = displacement.shape[3]
    lines = layers * displacement.shape[2]
    tiles = columns // LANES
    base = local_count * planes * tiles
    tail = base + (3 + (layers + 1) // 2) * tiles
    length = tail + 3 * layers * tiles // 4 + local_count * SUM_ROWS
    packet = pl.pallas_call(
        functools.partial(pack_kernel, layers),
        name="pack",
        out_shape=jax.ShapeDtypeStruct((devices, length, LANES), f32),
        in_specs=[vmem()] * 5,
        out_specs=vmem(),
        scratch_shapes=[pltpu.VMEM((7 * lines, LANES), f32)],
        compiler_params=pack_params,
    )(
        displacement.reshape(3 * lines, side), element_sample.reshape(lines, side),
        external_force.reshape(3 * lines, side),
        lame_field.reshape(devices, local_count, planes, columns),
        shear_field.reshape(devices, local_count, planes, columns),
    )
    packets = lax.all_to_all(packet, "dev", split_axis=0, concat_axis=0, tiled=True).reshape(devices * length, LANES)
    own_tail = packets.reshape(devices, length, LANES)[:, tail:].reshape(-1, LANES)
    tails = [own_tail, lax.ppermute(own_tail, "dev", [(i, i ^ 1) for i in range(devices)])]
    tails.append(lax.ppermute(own_tail, "grp", [(i, i ^ 1) for i in range(groups)]))
    flips = [(i, i ^ 1 ^ devices) for i in range(groups * devices)]
    tails.append(lax.ppermute(own_tail, ("grp", "dev"), flips))
    everyone = groups * devices
    sents = []
    rows = []
    for local in range(local_count):
        sent, response = pl.pallas_call(
            functools.partial(micro_kernel, local, local_count, layers),
            name="micro",
            out_shape=(
                jax.ShapeDtypeStruct((devices, 6 * planes, columns), bf16),
                jax.ShapeDtypeStruct((everyone, 16), f32),
            ),
            in_specs=[hbm()] * 6,
            out_specs=(hbm(), hbm()),
            scratch_shapes=[
                pltpu.VMEM((devices * length, LANES), f32),
                pltpu.VMEM((2, vox, columns), f32),
                pltpu.VMEM(multipliers.shape, f32),
                pltpu.VMEM(forward_line.shape, bf16),
                pltpu.VMEM(backward_line.shape, bf16),
                pltpu.VMEM(plane.shape, bf16),
                pltpu.VMEM((6 * vox, columns), f32),
                pltpu.VMEM((devices, 6 * planes, columns), f32),
                pltpu.VMEM((devices, 6 * planes, columns), bf16),
                pltpu.VMEM((everyone, 16), f32),
                pltpu.SMEM(plastic_steps.shape, jnp.int32),
                pltpu.SemaphoreType.DMA((11,)),
            ],
            compiler_params=params,
        )(
            plastic_steps, packets, multipliers, forward_line, backward_line, plane,
        )
        sents.append(sent)
        rows.append(response)
    gathered = lax.all_to_all(
        jnp.stack(rows, axis=1), ("grp", "dev"), split_axis=0, concat_axis=0, tiled=True
    ).reshape(everyone * local_count, 16)
    moved = lax.all_to_all(jnp.stack(sents, axis=1), "dev", split_axis=0, concat_axis=0, tiled=True)
    group_rows = lax.dynamic_slice_in_dim(gathered, lax.axis_index("grp") * group_size, group_size)
    loads = group_rows[:, 8:14].T
    change = jnp.transpose(moved.reshape(group_size, 6, planes, columns), (1, 0, 2, 3))
    micro_strain = loads[:, :, None, None] + change.astype(f32)
    following, picked = pl.pallas_call(
        functools.partial(macro_kernel, layers, base),
        name="macro",
        out_shape=(
            jax.ShapeDtypeStruct((3, layers, width), f32),
            jax.ShapeDtypeStruct((local_count, 8), f32),
        ),
        in_specs=[smem(), smem()] + [vmem()] * 6,
        out_specs=(vmem(), vmem()),
        scratch_shapes=[
            pltpu.VMEM((devices * layers, width), f32),
            pltpu.VMEM((3, devices * layers, width), f32),
            pltpu.VMEM((8, devices * layers, width), f32),
            pltpu.VMEM((3, devices * layers, width), f32),
        ],
        compiler_params=macro_params,
    )(owner_slot, gathered, gathered, packets, *tails)
    return (displacement + following.reshape(displacement.shape), picked, micro_strain)


def solution(mesh):
    in_specs = (
        P(None, "dev", None, None),
        P(None, "dev", None, None),
        P("dev", None, None),
        P("grp", "dev", None),
        P("grp", "dev", None),
        P(),
        P(),
    )
    out_specs = (P(None, "dev", None, None), P(("grp", "dev"), None), P(None, "grp", "dev", None))
    return jax.shard_map(shards, mesh=mesh, in_specs=in_specs, out_specs=out_specs, check_vma=False)
```

```python
import functools
import jax
import jax.numpy as jnp
import numpy as np
from jax import lax
from jax.experimental import pallas as pl
from jax.experimental.pallas import tpu as pltpu
from jax.sharding import PartitionSpec as P

CG_STEPS = 3
shear_ref = 1.65
lame_ref = 1.25
green_ratio = (lame_ref + shear_ref) / (lame_ref + 2.0 * shear_ref)
relax_rate = 0.35
flow_scale = 4.0
spring_rate = 0.2
f32 = jnp.float32
bf16 = jnp.bfloat16
DIAG = ((0, 0), (1, 1), (2, 2))
PAIRS = ((0, 0), (1, 1), (2, 2), (1, 2), (0, 2), (0, 1))
SLOT = {(0, 0): 0, (1, 1): 1, (2, 2): 2, (1, 2): 3, (2, 1): 3, (0, 2): 4, (2, 0): 4, (0, 1): 5, (1, 0): 5}


def split_table(table):
    high = table.astype(np.float32).astype(bf16)
    low = (table - high.astype(np.float64)).astype(np.float32).astype(bf16)
    return np.stack([high, low])


def tables(vox):
    half = vox // 2
    n = np.arange(vox)[:, None]
    k = np.arange(half)[None, :]
    angle = 2.0 * np.pi * (n * k % vox) / vox
    cosine = np.cos(angle) * np.sqrt(2.0 / vox)
    sine = np.sin(angle) * np.sqrt(2.0 / vox)
    cosine[:, 0] = 1.0 / np.sqrt(vox)
    sine[:, 0] = (1.0 - 2.0 * (np.arange(vox) % 2)) / np.sqrt(vox)
    basis = np.concatenate([cosine, sine], axis=1)
    order = np.concatenate([np.arange(0, half, 2), np.arange(1, half, 2)])
    by_parity = basis.reshape(vox, 2, half)
    folded = by_parity[:half, :, order].reshape(half, 2, 2, half // 2)
    plane = np.einsum("ypek,zql->eyzqpkl", folded, by_parity).reshape(2, half * vox, half * vox)
    line = basis.T
    forward_line = np.kron(np.eye(2), line)
    backward_line = np.kron(np.eye(2), line.T)
    wave = np.sin(2.0 * np.pi * np.arange(half) / vox)
    wave[0] = 0.0
    first = np.broadcast_to(wave[:, None, None], (half, half, half))
    second = np.broadcast_to(wave[order][None, :, None], (half, half, half))
    third = np.broadcast_to(wave[None, None, :], (half, half, half))
    square = first**2 + second**2 + third**2
    inverse = np.where(square > 0.0, 1.0 / np.where(square > 0.0, square, 1.0), 0.0)
    waves = (first, second, third)
    products = [waves[a] * waves[b] for a, b in PAIRS]
    rows = products + [inverse / shear_ref, green_ratio * inverse]
    multipliers = np.stack(rows).reshape(len(rows), half, half * half).astype(np.float32)
    return split_table(plane), split_table(forward_line), split_table(backward_line), multipliers


def split(value):
    high = value.astype(bf16)
    return high, (value - high.astype(f32)).astype(bf16)


def dot(left, right):
    return lax.dot_general(left, right, (((1,), (0,)), ((), ())), preferred_element_type=f32)


def dot_t(left, right):
    return lax.dot_general(left, right, (((1,), (1,)), ((), ())), preferred_element_type=f32)


def by_table(value, high, low, contract):
    rows = value.shape[0]
    value_high, value_low = split(value)
    both = contract(jnp.concatenate([value_high, value_low], axis=0), high)
    return both[:rows] + both[rows:] + contract(value_high, low)


def table_by(high, low, value):
    value_high, value_low = split(value)
    deep = jnp.concatenate([high, low, high], axis=1)
    return dot(deep, jnp.concatenate([value_high, value_high, value_low], axis=0))


def forward_plane(value, table):
    half = value.shape[1] // 2
    low, high = value[:, :half], value[:, half:]
    even = by_table(low + high, table[0, 0], table[1, 0], dot)
    odd = by_table(low - high, table[0, 1], table[1, 1], dot)
    return jnp.concatenate([even, odd], axis=1)


def backward_plane(value, table):
    half = value.shape[1] // 2
    even = by_table(value[:, :half], table[0, 0], table[1, 0], dot_t)
    odd = by_table(value[:, half:], table[0, 1], table[1, 1], dot_t)
    return jnp.concatenate([even + odd, even - odd], axis=1)


def lane_position(shape):
    return lax.broadcasted_iota(jnp.int32, shape, 1)


def row_position(shape):
    return lax.broadcasted_iota(jnp.int32, shape, 0)


def plane_slopes(stencil, v):
    next_z = stencil.up_z(v)
    sum_z = v + next_z
    dif_z = next_z - v
    next_y = stencil.up_y(sum_z)
    return sum_z + next_y, next_y - sum_z, dif_z + stencil.up_y(dif_z)


def strain_from(slopes):
    return [
        0.25 * slopes[0][0],
        0.25 * slopes[1][1],
        0.25 * slopes[2][2],
        0.125 * (slopes[2][1] + slopes[1][2]),
        0.125 * (slopes[2][0] + slopes[0][2]),
        0.125 * (slopes[1][0] + slopes[0][1]),
    ]


class TileStencil:
    def __init__(self, shape, width):
        self.rows, self.width = shape[0], width
        lane = lane_position(shape)
        self.last_z = lane % width == width - 1
        self.inside = lane < LANES - width
        self.last_y = (lane >= LANES - width) & (row_position(shape) == self.rows - 1)

    def up_z(self, v):
        return jnp.where(self.last_z, 0.0, pltpu.roll(v, LANES - 1, 1))

    def up_y(self, v):
        turned = pltpu.roll(v, LANES - self.width, 1)
        following = pltpu.roll(turned, self.rows - 1, 0)
        return jnp.where(self.last_y, 0.0, jnp.where(self.inside, turned, following))


class Stencil:
    def __init__(self, shape, width, devices):
        self.rows, self.columns = shape
        self.width = width
        self.devices = devices
        lane = lane_position(shape)
        row = row_position((devices, self.columns))
        self.last_z = lane % width == width - 1
        self.first_z = lane % width == 0
        self.last_y = lane >= self.columns - width
        self.first_y = lane < width
        self.last_x = row == devices - 1
        self.first_x = row == 0

    def up_z(self, v):
        return jnp.where(self.last_z, 0.0, pltpu.roll(v, self.columns - 1, 1))

    def up_y(self, v):
        return jnp.where(self.last_y, 0.0, pltpu.roll(v, self.columns - self.width, 1))

    def up_x(self, v):
        wrapped = jnp.where(self.last_x, 0.0, pltpu.roll(v[: self.devices], self.devices - 1, 0))
        return wrapped if self.rows == self.devices else jnp.concatenate([v[self.devices :], wrapped], axis=0)

    def down_z(self, v):
        return jnp.where(self.first_z, 0.0, pltpu.roll(v, 1, 1))

    def down_y(self, v):
        return jnp.where(self.first_y, 0.0, pltpu.roll(v, self.width, 1))

    def down_x(self, v):
        wrapped = jnp.where(self.first_x, 0.0, pltpu.roll(v[self.rows - self.devices :], 1, 0))
        return wrapped if self.rows == self.devices else jnp.concatenate([wrapped, v[: self.rows - self.devices]], axis=0)

    def strain(self, field):
        slopes = []
        for v in field:
            sums, along_y, along_z = plane_slopes(self, v)
            slopes.append((self.up_x(sums) - sums, along_y + self.up_x(along_y), along_z + self.up_x(along_z)))
        return strain_from(slopes)

    def force(self, stress):
        result = []
        for b in range(3):
            along_x, along_y, along_z = (stress[SLOT[(a, b)]] for a in range(3))
            sum_x = along_x + self.down_z(along_x)
            first = sum_x + self.down_y(sum_x)
            sum_y = along_y + self.down_z(along_y)
            dif_z = self.down_z(along_z) - along_z
            back = self.down_y(sum_y)
            rest = (back - sum_y) + (dif_z + self.down_y(dif_z))
            result.append(0.25 * ((self.down_x(first) - first) + (rest + self.down_x(rest))))
        return result


def total(value):
    return jnp.sum(jnp.sum(value, axis=0, keepdims=True), axis=1, keepdims=True)


def measure(stress):
    return (
        stress[0] * stress[0]
        + stress[1] * stress[1]
        + stress[2] * stress[2]
        + 2.0 * (stress[3] * stress[3] + stress[4] * stress[4] + stress[5] * stress[5])
    )


def remaining(shear, size, steps, most):
    stiff = (2.0 * shear) * (2.0 * shear) * size

    def relax(count, left):
        ratio = stiff * left * left
        return left * ((1.0 - relax_rate) + relax_rate / (1.0 + ratio))

    left = lax.fori_loop(0, steps, relax, jnp.ones_like(stiff))
    return left, stiff * left * left


def deviator_of(strain):
    trace = strain[0] + strain[1] + strain[2]
    third = trace / 3.0
    return trace, [strain[0] - third, strain[1] - third, strain[2] - third] + list(strain[3:])


LAME_UNIT = 2.0**8
SHEAR_UNIT = 2.0**9
CODE_BASE = 2.0**11
LABEL_BASE = 2.0**12
LANES = 128
SUM_ROWS = 4


def encode(lame, shear):
    return (lame.astype(f32) * LAME_UNIT) * CODE_BASE + shear.astype(f32) * SHEAR_UNIT


def decode(code):
    high = jnp.floor(code * (1.0 / CODE_BASE))
    return high * (1.0 / LAME_UNIT), (code - high * CODE_BASE) * (1.0 / SHEAR_UNIT)


def pack_kernel(layers, moved_ref, sample_ref, force_ref, lame_ref, shear_ref, packet_ref, wide):
    devices, local_count, planes, columns = lame_ref.shape
    tiles = columns // LANES
    for device in range(devices):
        for local in range(local_count):
            code = encode(lame_ref[device, local], shear_ref[device, local])
            for tile in range(tiles):
                packet_ref[device, pl.ds(local * planes * tiles + tile, planes, stride=tiles), :] = code[
                    :, tile * LANES : (tile + 1) * LANES
                ]
    width = moved_ref.shape[1]
    beside = LANES // width
    start = 0
    for ref in (moved_ref, sample_ref, force_ref):
        rows = ref.shape[0]
        wide[start : start + rows, :] = jnp.concatenate([ref[...].astype(f32)] * beside, axis=1)
        start += rows
    count = start // beside
    slot = lane_position((count, LANES)) // width
    merged = wide[pl.ds(0, count, stride=beside), :]
    for place in range(1, beside):
        merged = jnp.where(slot == place, wide[pl.ds(place, count, stride=beside), :], merged)
    nodes = 3 * count // 7
    each = nodes // (3 * layers)
    labels = [merged[nodes + layer * each : nodes + (layer + 1) * each] for layer in range(layers)]
    at = local_count * planes * tiles
    for part in range(3):
        for device in range(devices):
            packet_ref[device, at : at + each, :] = merged[part * layers * each : (part * layers + 1) * each]
        at += each
    for first in range(0, layers, 2):
        pair = labels[first] * LABEL_BASE
        if first + 1 < layers:
            pair = pair + labels[first + 1]
        for device in range(devices):
            packet_ref[device, at : at + each, :] = pair
        at += each
    pull = merged[count - nodes :] - spring_rate * merged[:nodes]
    part = nodes // 4
    upper = lax.axis_index("grp") % 2 == 1
    for core in range(2):
        quarter = jnp.where(upper, pull[(2 + core) * part : (3 + core) * part], pull[core * part : (core + 1) * part])
        for device in range(core, devices, 2):
            packet_ref[device, at : at + part, :] = quarter
    at += part
    stencil = TileStencil((each, LANES), width)
    slopes = [
        [plane_slopes(stencil, merged[(c * layers + layer) * each : (c * layers + layer + 1) * each]) for c in range(3)]
        for layer in range(layers)
    ]
    strains = []
    for layer in range(layers):
        below = [(-sums, along_y, along_z) for sums, along_y, along_z in slopes[layer]]
        if layer + 1 < layers:
            below = [tuple(low + high for low, high in zip(*both)) for both in zip(below, slopes[layer + 1])]
        strains.append(strain_from(below) + [jnp.ones((each, LANES), f32)])
    start = lax.axis_index("grp") * (devices * local_count)
    left = lane_position((1, LANES)) < LANES // 2
    for device in range(devices):
        for local in range(local_count):
            own = (start + device * local_count + local).astype(f32)
            hits = [label == own for label in labels]
            sums = []
            for c in range(7):
                value = sum(jnp.where(hit, strain[c], 0.0) for hit, strain in zip(hits, strains))
                value = jnp.sum(value, axis=0, keepdims=True)
                sums.append(value + pltpu.roll(value, LANES // 2, 1))
            sums.append(jnp.zeros((1, LANES), f32))
            for c in range(SUM_ROWS):
                row = at + local * SUM_ROWS + c
                packet_ref[device, row : row + 1, :] = jnp.where(left, sums[c], sums[c + SUM_ROWS])


def read_plane(packet_ref, row, devices, tiles):
    step = packet_ref.shape[0] // devices
    return jnp.concatenate(
        [packet_ref[pl.ds(row + tile, devices, stride=step), :] for tile in range(tiles)], axis=1
    )


def read_label(packet_ref, base, layer, devices, tiles):
    both = read_plane(packet_ref, base + (3 + layer // 2) * tiles, devices, tiles)
    high = jnp.floor(both * (1.0 / LABEL_BASE))
    return high if layer % 2 == 0 else both - high * LABEL_BASE


def read_force(tail_refs, layers, forces):
    _, rows, columns = forces.shape
    devices = rows // layers
    tiles = columns // LANES
    step = tail_refs[0].shape[0] // devices
    part = 3 * layers * tiles // 4
    odd_core = lax.axis_index("dev") % 2
    odd_group = lax.axis_index("grp") % 2
    for row in range(3 * layers):
        for tile in range(tiles):
            quarter, at = divmod(row * tiles + tile, part)
            own, core, side, across = (ref[pl.ds(at, devices, stride=step), :] for ref in tail_refs)
            same_core = odd_core == quarter % 2
            here, there = jnp.where(same_core, own, core), jnp.where(same_core, side, across)
            c, layer = divmod(row, layers)
            forces[c, layer * devices : (layer + 1) * devices, tile * LANES : (tile + 1) * LANES] = jnp.where(
                odd_group == quarter // 2, here, there
            )


def micro_kernel(
    local, local_count, layers, steps_hbm, packet_hbm, mult_hbm, fwd_hbm, bwd_hbm, table_hbm,
    sent_hbm, response_hbm, packet_ref, moduli, mult_ref, fwd_ref, bwd_ref, table, spectrum, ordered, sent_ref, response_ref, steps_ref, sem
):
    devices, planes = sent_ref.shape[0], sent_ref.shape[1] // 6
    vox, columns = moduli.shape[1:]
    half = vox // 2
    quarter = half * half
    pairs = [(packet_hbm, packet_ref), (steps_hbm, steps_ref)]
    pairs += [(table_hbm.at[part, fold], table.at[part, fold]) for fold in range(2) for part in range(2)]
    pairs += [(fwd_hbm, fwd_ref), (mult_hbm, mult_ref), (bwd_hbm, bwd_ref)]
    copies = [pltpu.make_async_copy(source, target, sem.at[i]) for i, (source, target) in enumerate(pairs)]
    for copy in copies:
        copy.start()
    own = (lax.axis_index("grp") * lax.axis_size("dev") + lax.axis_index("dev")) * local_count + local
    copies[0].wait()
    tiles = columns // LANES
    step = packet_ref.shape[0] // devices
    for device in range(devices):
        for tile in range(tiles):
            at = device * step + local * planes * tiles + tile
            code = packet_ref[pl.ds(at, planes, stride=tiles), :]
            for kind, value in enumerate(decode(code)):
                moduli[
                    kind, device * planes : (device + 1) * planes, tile * LANES : (tile + 1) * LANES
                ] = value
    base = local_count * planes * tiles
    stencil = Stencil((devices, columns), vox_width(columns), devices)
    following = []
    for c in range(3):
        plane = read_plane(packet_ref, base + c * tiles, devices, tiles)
        following.append(plane_slopes(stencil, stencil.up_x(plane)))
    mine = read_label(packet_ref, base, layers - 1, devices, tiles) == own.astype(f32)
    sums = 0.0
    for device in range(devices):
        at = (device + 1) * step - (local_count - local) * SUM_ROWS
        sums = sums + packet_ref[at : at + SUM_ROWS, :]
    left_half = lane_position(sums.shape) < LANES // 2
    sums = [jnp.sum(jnp.where(left_half == side, sums, 0.0), axis=1, keepdims=True) for side in (True, False)]
    sums = [half_sums[row : row + 1] for half_sums in sums for row in range(SUM_ROWS)]
    load = [
        (sums[c] + total(jnp.where(mine, part, 0.0))) / sums[6] for c, part in enumerate(strain_from(following))
    ]
    copies[1].wait()
    steps = steps_ref[own]
    trace, dev = deviator_of(load)
    lame = moduli[0]
    shear = moduli[1]
    size = measure([0.5 * part for part in dev])
    left, _ = remaining(shear, jnp.broadcast_to(size, shear.shape), steps, 4)
    bulk = lame + (2.0 / 3.0) * shear
    sources = jnp.concatenate([bulk * trace, 2.0 * shear * left], axis=0)
    for copy in copies[2:7]:
        copy.wait()
    spectral = table_by(fwd_ref[0], fwd_ref[1], forward_plane(sources, table))

    def block(field, px, py, pz):
        rows = slice(field * vox + px * half, field * vox + (px + 1) * half)
        start = (pz * 2 + py) * quarter // 2
        return rows, [slice(fold * 2 * quarter + start, fold * 2 * quarter + start + quarter // 2) for fold in range(2)]

    def take(field, parity):
        rows, pieces = block(field, *parity)
        return jnp.concatenate([spectral[rows, lanes] for lanes in pieces], axis=1)

    parities = [(px, py, pz) for px in range(2) for py in range(2) for pz in range(2)]
    copies[7].wait()
    product = [mult_ref[i] for i in range(6)]
    inverse = mult_ref[6]
    scaled = mult_ref[7]

    def second(blocks, parity, a, b):
        if a == b:
            return -(product[SLOT[(a, b)]] * blocks[parity])
        other = tuple(1 - p if axis in (a, b) else p for axis, p in enumerate(parity))
        value = product[SLOT[(a, b)]] * blocks[other]
        return value if parity[a] == parity[b] else -value

    psi = {}
    raw = {}
    for parity in parities:
        raw[parity] = take(1, parity)
        psi[parity] = inverse * raw[parity]
    phi = {}
    for parity in parities:
        pressed = sum(
            (1.0 if a == b else 2.0) * dev[SLOT[(a, b)]] * second(psi, parity, a, b) for a, b in PAIRS
        )
        phi[parity] = (1.0 - green_ratio) * inverse * take(0, parity) + scaled * pressed
    for parity in parities:
        curl = {pair: second(psi, parity, *pair) for pair in PAIRS}
        for index, (a, b) in enumerate(PAIRS):
            def at(i, j):
                return curl[(min(i, j), max(i, j))]
            if a == b:
                sheared = sum(dev[SLOT[(b, c)]] * at(a, c) for c in range(3))
            else:
                sheared = 0.5 * sum(dev[SLOT[(b, c)]] * at(a, c) + dev[SLOT[(a, c)]] * at(b, c) for c in range(3))
            value = second(phi, parity, a, b) + sheared
            rows, pieces = block(index, *parity)
            for fold, lanes in enumerate(pieces):
                spectrum[rows, lanes] = value[:, fold * quarter // 2 : (fold + 1) * quarter // 2]
    lines = backward_plane(spectrum[...], table)
    copies[8].wait()
    moved = jnp.concatenate(
        [table_by(bwd_ref[0], bwd_ref[1], lines[i * vox : (i + 2) * vox]) for i in range(0, 6, 2)], axis=0
    )
    if 2 * planes == 8:
        low = row_position((2 * planes, columns)) < planes
        for pair in range(3):
            for chip in range(devices // 2):
                first, second_ = (
                    moved[i * vox + 2 * chip * planes : i * vox + 2 * (chip + 1) * planes]
                    for i in (2 * pair, 2 * pair + 1)
                )
                rows = slice(2 * pair * planes, 2 * (pair + 1) * planes)
                ordered[2 * chip, rows] = jnp.where(low, first, pltpu.roll(second_, planes, 0))
                ordered[2 * chip + 1, rows] = jnp.where(low, pltpu.roll(first, planes, 0), second_)
    else:
        for i in range(6):
            for device in range(devices):
                ordered[device, i * planes : (i + 1) * planes] = moved[
                    i * vox + device * planes : i * vox + (device + 1) * planes
                ]
    for device in range(devices):
        sent_ref[device] = ordered[device].astype(bf16)
    send = pltpu.make_async_copy(sent_ref, sent_hbm, sem.at[len(pairs)])
    send.start()
    strain = [load[i] + moved[i * vox : (i + 1) * vox] for i in range(6)]
    trace, dev = deviator_of(strain)
    left, ratio = remaining(shear, measure([0.5 * part for part in dev]), steps, 4)
    push = bulk * trace
    pull = 2.0 * shear * left
    stress = [push + pull * dev[i] for i in range(3)] + [pull * dev[i] for i in range(3, 6)]
    parts = stress + [lame, shear / (1.0 + ratio)]
    lane = lane_position((1, response_ref.shape[1]))
    row = jnp.zeros(lane.shape, f32)
    for index, part in enumerate(parts):
        row = jnp.where(lane == index, total(part) / float(vox * columns), row)
    for index, part in enumerate(load):
        row = jnp.where(lane == 8 + index, part, row)
    response_ref[...] = jnp.broadcast_to(row, response_ref.shape)
    answer = pltpu.make_async_copy(response_ref, response_hbm, sem.at[len(pairs) + 1])
    answer.start()
    send.wait()
    answer.wait()


def vox_width(columns):
    width = int(round(columns**0.5))
    return width


def macro_kernel(
    layers, base, slots_ref, table_ref, table_v_ref, packet_ref, own_ref, core_ref, side_ref, across_ref, next_ref, row_ref, labels, forces, cells, result
):
    columns = next_ref.shape[2]
    devices = labels.shape[0] // layers
    samples = table_v_ref.shape[0]
    rank = lax.axis_index("dev")
    group = lax.axis_index("grp")
    local_count = row_ref.shape[0]
    group_size = local_count * devices
    start = group * group_size
    for local in range(local_count):
        chosen = jnp.int32(0)
        for j in range(group_size):
            chosen = jnp.where(slots_ref[start + j] == rank * local_count + local, start + j, chosen)
        row_ref[local : local + 1, :] = table_v_ref[pl.ds(chosen, 1), 0:8]
    for layer in range(layers):
        labels[layer * devices : (layer + 1) * devices, :] = read_label(
            packet_ref, base, layer, devices, columns // LANES
        )
    read_force((own_ref, core_ref, side_ref, across_ref), layers, forces)
    rows = labels.shape[0]
    height = min(8, rows)
    span = min(512, columns)
    for top in range(0, rows, height):
        for side in range(0, columns, span):
            where = (slice(top, top + height), slice(side, side + span))
            label = labels[where]

            def pick(sample, held):
                here = label == sample.astype(f32)
                return tuple(jnp.where(here, table_ref[sample, c], held[c]) for c in range(8))

            zero = jnp.zeros((height, span), f32)
            held = lax.fori_loop(0, samples, pick, (zero,) * 8, unroll=4)
            for c in range(8):
                cells[(c,) + where] = held[c]
    stencil = Stencil(labels.shape, vox_width(columns), devices)
    stress = [cells[c] for c in range(6)]
    pulled = stencil.force(stress)
    remainder = [forces[b] - pulled[b] for b in range(3)]
    direction = remainder
    norm_now = total(sum(r * r for r in remainder))
    update = None
    lame = cells[6]
    shear = 2.0 * cells[7]
    for turn in range(CG_STEPS):
        strain = stencil.strain(direction)
        pressure = lame * (strain[0] + strain[1] + strain[2])
        stress = [shear * strain[i] + pressure for i in range(3)] + [shear * strain[i] for i in range(3, 6)]
        pulled = stencil.force(stress)
        image = [pulled[b] + spring_rate * direction[b] for b in range(3)]
        alpha = norm_now / total(sum(direction[b] * image[b] for b in range(3)))
        moved = [alpha * direction[b] for b in range(3)]
        update = moved if update is None else [update[b] + moved[b] for b in range(3)]
        if turn + 1 < CG_STEPS:
            remainder = [remainder[b] - alpha * image[b] for b in range(3)]
            norm_next = total(sum(r * r for r in remainder))
            grow = norm_next / norm_now
            direction = [remainder[b] + grow * direction[b] for b in range(3)]
            norm_now = norm_next
    for b in range(3):
        result[b] = update[b]
        for layer in range(layers):
            next_ref[b, layer : layer + 1, :] = result[b, pl.ds(layer * devices + rank, 1), :]


def vmem():
    return pl.BlockSpec(memory_space=pltpu.VMEM)


def hbm():
    return pl.BlockSpec(memory_space=pltpu.HBM)


def smem():
    return pl.BlockSpec(memory_space=pltpu.SMEM)


def shards(
    displacement, external_force, element_sample, lame_field, shear_field, plastic_steps, owner_slot
):
    group_size, planes, columns = lame_field.shape
    devices = lax.axis_size("dev")
    groups = lax.axis_size("grp")
    local_count = group_size // devices
    vox = planes * devices
    layers = displacement.shape[1]
    width = displacement.shape[2] * displacement.shape[3]
    plane, forward_line, backward_line, multipliers = tables(vox)
    pack_params, params, macro_params = (
        pltpu.CompilerParams(vmem_limit_bytes=size * 1024 * 1024) for size in (60, 60, 16)
    )

    side = displacement.shape[3]
    lines = layers * displacement.shape[2]
    tiles = columns // LANES
    base = local_count * planes * tiles
    tail = base + (3 + (layers + 1) // 2) * tiles
    length = tail + 3 * layers * tiles // 4 + local_count * SUM_ROWS
    packet = pl.pallas_call(
        functools.partial(pack_kernel, layers),
        name="pack",
        out_shape=jax.ShapeDtypeStruct((devices, length, LANES), f32),
        in_specs=[vmem()] * 5,
        out_specs=vmem(),
        scratch_shapes=[pltpu.VMEM((7 * lines, LANES), f32)],
        compiler_params=pack_params,
    )(
        displacement.reshape(3 * lines, side), element_sample.reshape(lines, side),
        external_force.reshape(3 * lines, side),
        lame_field.reshape(devices, local_count, planes, columns),
        shear_field.reshape(devices, local_count, planes, columns),
    )
    packets = lax.all_to_all(packet, "dev", split_axis=0, concat_axis=0, tiled=True).reshape(devices * length, LANES)
    own_tail = packets.reshape(devices, length, LANES)[:, tail:].reshape(-1, LANES)
    tails = [own_tail, lax.ppermute(own_tail, "dev", [(i, i ^ 1) for i in range(devices)])]
    tails.append(lax.ppermute(own_tail, "grp", [(i, i ^ 1) for i in range(groups)]))
    flips = [(i, i ^ 1 ^ devices) for i in range(groups * devices)]
    tails.append(lax.ppermute(own_tail, ("grp", "dev"), flips))
    everyone = groups * devices
    sents = []
    rows = []
    for local in range(local_count):
        sent, response = pl.pallas_call(
            functools.partial(micro_kernel, local, local_count, layers),
            name="micro",
            out_shape=(
                jax.ShapeDtypeStruct((devices, 6 * planes, columns), bf16),
                jax.ShapeDtypeStruct((everyone, 16), f32),
            ),
            in_specs=[hbm()] * 6,
            out_specs=(hbm(), hbm()),
            scratch_shapes=[
                pltpu.VMEM((devices * length, LANES), f32),
                pltpu.VMEM((2, vox, columns), f32),
                pltpu.VMEM(multipliers.shape, f32),
                pltpu.VMEM(forward_line.shape, bf16),
                pltpu.VMEM(backward_line.shape, bf16),
                pltpu.VMEM(plane.shape, bf16),
                pltpu.VMEM((6 * vox, columns), f32),
                pltpu.VMEM((devices, 6 * planes, columns), f32),
                pltpu.VMEM((devices, 6 * planes, columns), bf16),
                pltpu.VMEM((everyone, 16), f32),
                pltpu.SMEM(plastic_steps.shape, jnp.int32),
                pltpu.SemaphoreType.DMA((11,)),
            ],
            compiler_params=params,
        )(
            plastic_steps, packets, multipliers, forward_line, backward_line, plane,
        )
        sents.append(sent)
        rows.append(response)
    gathered = lax.all_to_all(
        jnp.stack(rows, axis=1), ("grp", "dev"), split_axis=0, concat_axis=0, tiled=True
    ).reshape(everyone * local_count, 16)
    moved = lax.all_to_all(jnp.stack(sents, axis=1), "dev", split_axis=0, concat_axis=0, tiled=True)
    group_rows = lax.dynamic_slice_in_dim(gathered, lax.axis_index("grp") * group_size, group_size)
    loads = group_rows[:, 8:14].T
    change = jnp.transpose(moved.reshape(group_size, 6, planes, columns), (1, 0, 2, 3))
    micro_strain = loads[:, :, None, None] + change.astype(f32)
    following, picked = pl.pallas_call(
        functools.partial(macro_kernel, layers, base),
        name="macro",
        out_shape=(
            jax.ShapeDtypeStruct((3, layers, width), f32),
            jax.ShapeDtypeStruct((local_count, 8), f32),
        ),
        in_specs=[smem(), smem()] + [vmem()] * 6,
        out_specs=(vmem(), vmem()),
        scratch_shapes=[
            pltpu.VMEM((devices * layers, width), f32),
            pltpu.VMEM((3, devices * layers, width), f32),
            pltpu.VMEM((8, devices * layers, width), f32),
            pltpu.VMEM((3, devices * layers, width), f32),
        ],
        compiler_params=macro_params,
    )(owner_slot, gathered, gathered, packets, *tails)
    return (displacement + following.reshape(displacement.shape), picked, micro_strain)


def solution(mesh):
    in_specs = (
        P(None, "dev", None, None),
        P(None, "dev", None, None),
        P("dev", None, None),
        P("grp", "dev", None),
        P("grp", "dev", None),
        P(),
        P(),
    )
    out_specs = (P(None, "dev", None, None), P(("grp", "dev"), None), P(None, "grp", "dev", None))
    return jax.shard_map(shards, mesh=mesh, in_specs=in_specs, out_specs=out_specs, check_vma=False)
```

```python
import functools
import jax
import jax.numpy as jnp
import numpy as np
from jax import lax
from jax.experimental import pallas as pl
from jax.experimental.pallas import tpu as pltpu
from jax.sharding import PartitionSpec as P

CG_STEPS = 3
shear_ref = 1.65
lame_ref = 1.25
green_ratio = (lame_ref + shear_ref) / (lame_ref + 2.0 * shear_ref)
relax_rate = 0.35
flow_scale = 4.0
spring_rate = 0.2
f32 = jnp.float32
bf16 = jnp.bfloat16
DIAG = ((0, 0), (1, 1), (2, 2))
PAIRS = ((0, 0), (1, 1), (2, 2), (1, 2), (0, 2), (0, 1))
SLOT = {(0, 0): 0, (1, 1): 1, (2, 2): 2, (1, 2): 3, (2, 1): 3, (0, 2): 4, (2, 0): 4, (0, 1): 5, (1, 0): 5}


def split_table(table):
    high = table.astype(np.float32).astype(bf16)
    low = (table - high.astype(np.float64)).astype(np.float32).astype(bf16)
    return np.stack([high, low])


def tables(vox):
    half = vox // 2
    n = np.arange(vox)[:, None]
    k = np.arange(half)[None, :]
    angle = 2.0 * np.pi * (n * k % vox) / vox
    cosine = np.cos(angle) * np.sqrt(2.0 / vox)
    sine = np.sin(angle) * np.sqrt(2.0 / vox)
    cosine[:, 0] = 1.0 / np.sqrt(vox)
    sine[:, 0] = (1.0 - 2.0 * (np.arange(vox) % 2)) / np.sqrt(vox)
    basis = np.concatenate([cosine, sine], axis=1)
    order = np.concatenate([np.arange(0, half, 2), np.arange(1, half, 2)])
    by_parity = basis.reshape(vox, 2, half)
    folded = by_parity[:half, :, order].reshape(half, 2, 2, half // 2)
    plane = np.einsum("ypek,zql->eyzqpkl", folded, by_parity).reshape(2, half * vox, half * vox)
    line = basis.T
    forward_line = np.kron(np.eye(2), line)
    backward_line = np.kron(np.eye(2), line.T)
    wave = np.sin(2.0 * np.pi * np.arange(half) / vox)
    wave[0] = 0.0
    first = np.broadcast_to(wave[:, None, None], (half, half, half))
    second = np.broadcast_to(wave[order][None, :, None], (half, half, half))
    third = np.broadcast_to(wave[None, None, :], (half, half, half))
    square = first**2 + second**2 + third**2
    inverse = np.where(square > 0.0, 1.0 / np.where(square > 0.0, square, 1.0), 0.0)
    waves = (first, second, third)
    products = [waves[a] * waves[b] for a, b in PAIRS]
    rows = products + [inverse / shear_ref, green_ratio * inverse]
    multipliers = np.stack(rows).reshape(len(rows), half, half * half).astype(np.float32)
    return split_table(plane), split_table(forward_line), split_table(backward_line), multipliers


def split(value):
    high = value.astype(bf16)
    return high, (value - high.astype(f32)).astype(bf16)


def dot(left, right):
    return lax.dot_general(left, right, (((1,), (0,)), ((), ())), preferred_element_type=f32)


def dot_t(left, right):
    return lax.dot_general(left, right, (((1,), (1,)), ((), ())), preferred_element_type=f32)


def by_table(value, high, low, contract):
    rows = value.shape[0]
    value_high, value_low = split(value)
    both = contract(jnp.concatenate([value_high, value_low], axis=0), high)
    return both[:rows] + both[rows:] + contract(value_high, low)


def table_by(high, low, value):
    value_high, value_low = split(value)
    deep = jnp.concatenate([high, low, high], axis=1)
    return dot(deep, jnp.concatenate([value_high, value_high, value_low], axis=0))


def forward_plane(value, table):
    half = value.shape[1] // 2
    low, high = value[:, :half], value[:, half:]
    even = by_table(low + high, table[0, 0], table[1, 0], dot)
    odd = by_table(low - high, table[0, 1], table[1, 1], dot)
    return jnp.concatenate([even, odd], axis=1)


def backward_plane(value, table):
    half = value.shape[1] // 2
    even = by_table(value[:, :half], table[0, 0], table[1, 0], dot_t)
    odd = by_table(value[:, half:], table[0, 1], table[1, 1], dot_t)
    return jnp.concatenate([even + odd, even - odd], axis=1)


def lane_position(shape):
    return lax.broadcasted_iota(jnp.int32, shape, 1)


def row_position(shape):
    return lax.broadcasted_iota(jnp.int32, shape, 0)


def plane_slopes(stencil, v):
    next_z = stencil.up_z(v)
    sum_z = v + next_z
    dif_z = next_z - v
    next_y = stencil.up_y(sum_z)
    return sum_z + next_y, next_y - sum_z, dif_z + stencil.up_y(dif_z)


def strain_from(slopes):
    return [
        0.25 * slopes[0][0],
        0.25 * slopes[1][1],
        0.25 * slopes[2][2],
        0.125 * (slopes[2][1] + slopes[1][2]),
        0.125 * (slopes[2][0] + slopes[0][2]),
        0.125 * (slopes[1][0] + slopes[0][1]),
    ]


class TileStencil:
    def __init__(self, shape, width):
        self.rows, self.width = shape[0], width
        lane = lane_position(shape)
        self.last_z = lane % width == width - 1
        self.inside = lane < LANES - width
        self.last_y = (lane >= LANES - width) & (row_position(shape) == self.rows - 1)

    def up_z(self, v):
        return jnp.where(self.last_z, 0.0, pltpu.roll(v, LANES - 1, 1))

    def up_y(self, v):
        turned = pltpu.roll(v, LANES - self.width, 1)
        following = pltpu.roll(turned, self.rows - 1, 0)
        return jnp.where(self.last_y, 0.0, jnp.where(self.inside, turned, following))


class Stencil:
    def __init__(self, shape, width, devices):
        self.rows, self.columns = shape
        self.width = width
        self.devices = devices
        lane = lane_position(shape)
        row = row_position((devices, self.columns))
        self.last_z = lane % width == width - 1
        self.first_z = lane % width == 0
        self.last_y = lane >= self.columns - width
        self.first_y = lane < width
        self.last_x = row == devices - 1
        self.first_x = row == 0

    def up_z(self, v):
        return jnp.where(self.last_z, 0.0, pltpu.roll(v, self.columns - 1, 1))

    def up_y(self, v):
        return jnp.where(self.last_y, 0.0, pltpu.roll(v, self.columns - self.width, 1))

    def up_x(self, v):
        wrapped = jnp.where(self.last_x, 0.0, pltpu.roll(v[: self.devices], self.devices - 1, 0))
        return wrapped if self.rows == self.devices else jnp.concatenate([v[self.devices :], wrapped], axis=0)

    def down_z(self, v):
        return jnp.where(self.first_z, 0.0, pltpu.roll(v, 1, 1))

    def down_y(self, v):
        return jnp.where(self.first_y, 0.0, pltpu.roll(v, self.width, 1))

    def down_x(self, v):
        wrapped = jnp.where(self.first_x, 0.0, pltpu.roll(v[self.rows - self.devices :], 1, 0))
        return wrapped if self.rows == self.devices else jnp.concatenate([wrapped, v[: self.rows - self.devices]], axis=0)

    def strain(self, field):
        slopes = []
        for v in field:
            sums, along_y, along_z = plane_slopes(self, v)
            slopes.append((self.up_x(sums) - sums, along_y + self.up_x(along_y), along_z + self.up_x(along_z)))
        return strain_from(slopes)

    def force(self, stress):
        result = []
        for b in range(3):
            along_x, along_y, along_z = (stress[SLOT[(a, b)]] for a in range(3))
            sum_x = along_x + self.down_z(along_x)
            first = sum_x + self.down_y(sum_x)
            sum_y = along_y + self.down_z(along_y)
            dif_z = self.down_z(along_z) - along_z
            back = self.down_y(sum_y)
            rest = (back - sum_y) + (dif_z + self.down_y(dif_z))
            result.append(0.25 * ((self.down_x(first) - first) + (rest + self.down_x(rest))))
        return result


def total(value):
    return jnp.sum(jnp.sum(value, axis=0, keepdims=True), axis=1, keepdims=True)


def measure(stress):
    return (
        stress[0] * stress[0]
        + stress[1] * stress[1]
        + stress[2] * stress[2]
        + 2.0 * (stress[3] * stress[3] + stress[4] * stress[4] + stress[5] * stress[5])
    )


def remaining(shear, size, steps, most):
    stiff = (2.0 * shear) * (2.0 * shear) * size

    rows = 8 if stiff.shape[0] % 8 == 0 else stiff.shape[0]
    lefts = []
    for top in range(0, stiff.shape[0], rows):
        part = stiff[top : top + rows]

        def relax(count, left, part=part):
            return left * ((1.0 - relax_rate) + relax_rate / (1.0 + part * left * left))

        lefts.append(lax.fori_loop(0, steps, relax, jnp.ones_like(part)))
    left = jnp.concatenate(lefts, axis=0)
    return left, stiff * left * left


def deviator_of(strain):
    trace = strain[0] + strain[1] + strain[2]
    third = trace / 3.0
    return trace, [strain[0] - third, strain[1] - third, strain[2] - third] + list(strain[3:])


LAME_UNIT = 2.0**8
SHEAR_UNIT = 2.0**9
CODE_BASE = 2.0**11
LABEL_BASE = 2.0**12
LANES = 128
SUM_ROWS = 4


def encode(lame, shear):
    return (lame.astype(f32) * LAME_UNIT) * CODE_BASE + shear.astype(f32) * SHEAR_UNIT


def decode(code):
    high = jnp.floor(code * (1.0 / CODE_BASE))
    return high * (1.0 / LAME_UNIT), (code - high * CODE_BASE) * (1.0 / SHEAR_UNIT)


def pack_kernel(layers, moved_ref, sample_ref, force_ref, lame_ref, shear_ref, packet_ref, wide):
    devices, local_count, planes, columns = lame_ref.shape
    tiles = columns // LANES
    for device in range(devices):
        for local in range(local_count):
            code = encode(lame_ref[device, local], shear_ref[device, local])
            for tile in range(tiles):
                packet_ref[device, pl.ds(local * planes * tiles + tile, planes, stride=tiles), :] = code[
                    :, tile * LANES : (tile + 1) * LANES
                ]
    width = moved_ref.shape[1]
    beside = LANES // width
    start = 0
    for ref in (moved_ref, sample_ref, force_ref):
        rows = ref.shape[0]
        wide[start : start + rows, :] = jnp.concatenate([ref[...].astype(f32)] * beside, axis=1)
        start += rows
    count = start // beside
    slot = lane_position((count, LANES)) // width
    merged = wide[pl.ds(0, count, stride=beside), :]
    for place in range(1, beside):
        merged = jnp.where(slot == place, wide[pl.ds(place, count, stride=beside), :], merged)
    nodes = 3 * count // 7
    each = nodes // (3 * layers)
    labels = [merged[nodes + layer * each : nodes + (layer + 1) * each] for layer in range(layers)]
    at = local_count * planes * tiles
    for part in range(3):
        for device in range(devices):
            packet_ref[device, at : at + each, :] = merged[part * layers * each : (part * layers + 1) * each]
        at += each
    for first in range(0, layers, 2):
        pair = labels[first] * LABEL_BASE
        if first + 1 < layers:
            pair = pair + labels[first + 1]
        for device in range(devices):
            packet_ref[device, at : at + each, :] = pair
        at += each
    pull = merged[count - nodes :] - spring_rate * merged[:nodes]
    part = nodes // 4
    upper = lax.axis_index("grp") % 2 == 1
    for core in range(2):
        quarter = jnp.where(upper, pull[(2 + core) * part : (3 + core) * part], pull[core * part : (core + 1) * part])
        for device in range(core, devices, 2):
            packet_ref[device, at : at + part, :] = quarter
    at += part
    stencil = TileStencil((each, LANES), width)
    slopes = [
        [plane_slopes(stencil, merged[(c * layers + layer) * each : (c * layers + layer + 1) * each]) for c in range(3)]
        for layer in range(layers)
    ]
    strains = []
    for layer in range(layers):
        below = [(-sums, along_y, along_z) for sums, along_y, along_z in slopes[layer]]
        if layer + 1 < layers:
            below = [tuple(low + high for low, high in zip(*both)) for both in zip(below, slopes[layer + 1])]
        strains.append(strain_from(below) + [jnp.ones((each, LANES), f32)])
    start = lax.axis_index("grp") * (devices * local_count)
    left = lane_position((1, LANES)) < LANES // 2
    for device in range(devices):
        for local in range(local_count):
            own = (start + device * local_count + local).astype(f32)
            hits = [label == own for label in labels]
            sums = []
            for c in range(7):
                value = sum(jnp.where(hit, strain[c], 0.0) for hit, strain in zip(hits, strains))
                value = jnp.sum(value, axis=0, keepdims=True)
                sums.append(value + pltpu.roll(value, LANES // 2, 1))
            sums.append(jnp.zeros((1, LANES), f32))
            for c in range(SUM_ROWS):
                row = at + local * SUM_ROWS + c
                packet_ref[device, row : row + 1, :] = jnp.where(left, sums[c], sums[c + SUM_ROWS])


def read_plane(packet_ref, row, devices, tiles):
    step = packet_ref.shape[0] // devices
    return jnp.concatenate(
        [packet_ref[pl.ds(row + tile, devices, stride=step), :] for tile in range(tiles)], axis=1
    )


def read_label(packet_ref, base, layer, devices, tiles):
    both = read_plane(packet_ref, base + (3 + layer // 2) * tiles, devices, tiles)
    high = jnp.floor(both * (1.0 / LABEL_BASE))
    return high if layer % 2 == 0 else both - high * LABEL_BASE


def read_force(tail_refs, layers, forces):
    _, rows, columns = forces.shape
    devices = rows // layers
    tiles = columns // LANES
    step = tail_refs[0].shape[0] // devices
    part = 3 * layers * tiles // 4
    odd_core = lax.axis_index("dev") % 2
    odd_group = lax.axis_index("grp") % 2
    for row in range(3 * layers):
        for tile in range(tiles):
            quarter, at = divmod(row * tiles + tile, part)
            own, core, side, across = (ref[pl.ds(at, devices, stride=step), :] for ref in tail_refs)
            same_core = odd_core == quarter % 2
            here, there = jnp.where(same_core, own, core), jnp.where(same_core, side, across)
            c, layer = divmod(row, layers)
            forces[c, layer * devices : (layer + 1) * devices, tile * LANES : (tile + 1) * LANES] = jnp.where(
                odd_group == quarter // 2, here, there
            )


def micro_kernel(
    local, local_count, layers, steps_hbm, packet_hbm, mult_hbm, fwd_hbm, bwd_hbm, table_hbm,
    sent_hbm, response_hbm, packet_ref, moduli, mult_ref, fwd_ref, bwd_ref, table, spectrum, ordered, sent_ref, response_ref, steps_ref, sem
):
    devices, planes = sent_ref.shape[0], sent_ref.shape[1] // 6
    vox, columns = moduli.shape[1:]
    half = vox // 2
    quarter = half * half
    pairs = [(packet_hbm, packet_ref), (steps_hbm, steps_ref)]
    pairs += [(table_hbm.at[part, fold], table.at[part, fold]) for fold in range(2) for part in range(2)]
    pairs += [(fwd_hbm, fwd_ref), (mult_hbm, mult_ref), (bwd_hbm, bwd_ref)]
    copies = [pltpu.make_async_copy(source, target, sem.at[i]) for i, (source, target) in enumerate(pairs)]
    for copy in copies:
        copy.start()
    own = (lax.axis_index("grp") * lax.axis_size("dev") + lax.axis_index("dev")) * local_count + local
    copies[0].wait()
    tiles = columns // LANES
    step = packet_ref.shape[0] // devices
    for device in range(devices):
        for tile in range(tiles):
            at = device * step + local * planes * tiles + tile
            code = packet_ref[pl.ds(at, planes, stride=tiles), :]
            for kind, value in enumerate(decode(code)):
                moduli[
                    kind, device * planes : (device + 1) * planes, tile * LANES : (tile + 1) * LANES
                ] = value
    base = local_count * planes * tiles
    stencil = Stencil((devices, columns), vox_width(columns), devices)
    following = []
    for c in range(3):
        plane = read_plane(packet_ref, base + c * tiles, devices, tiles)
        following.append(plane_slopes(stencil, stencil.up_x(plane)))
    mine = read_label(packet_ref, base, layers - 1, devices, tiles) == own.astype(f32)
    sums = 0.0
    for device in range(devices):
        at = (device + 1) * step - (local_count - local) * SUM_ROWS
        sums = sums + packet_ref[at : at + SUM_ROWS, :]
    left_half = lane_position(sums.shape) < LANES // 2
    sums = [jnp.sum(jnp.where(left_half == side, sums, 0.0), axis=1, keepdims=True) for side in (True, False)]
    sums = [half_sums[row : row + 1] for half_sums in sums for row in range(SUM_ROWS)]
    load = [
        (sums[c] + total(jnp.where(mine, part, 0.0))) / sums[6] for c, part in enumerate(strain_from(following))
    ]
    copies[1].wait()
    steps = steps_ref[own]
    trace, dev = deviator_of(load)
    lame = moduli[0]
    shear = moduli[1]
    size = measure([0.5 * part for part in dev])
    left, _ = remaining(shear, jnp.broadcast_to(size, shear.shape), steps, 4)
    bulk = lame + (2.0 / 3.0) * shear
    sources = jnp.concatenate([bulk * trace, 2.0 * shear * left], axis=0)
    for copy in copies[2:7]:
        copy.wait()
    spectral = table_by(fwd_ref[0], fwd_ref[1], forward_plane(sources, table))

    def block(field, px, py, pz):
        rows = slice(field * vox + px * half, field * vox + (px + 1) * half)
        start = (pz * 2 + py) * quarter // 2
        return rows, [slice(fold * 2 * quarter + start, fold * 2 * quarter + start + quarter // 2) for fold in range(2)]

    def take(field, parity):
        rows, pieces = block(field, *parity)
        return jnp.concatenate([spectral[rows, lanes] for lanes in pieces], axis=1)

    parities = [(px, py, pz) for px in range(2) for py in range(2) for pz in range(2)]
    copies[7].wait()
    product = [mult_ref[i] for i in range(6)]
    inverse = mult_ref[6]
    scaled = mult_ref[7]

    def second(blocks, parity, a, b):
        if a == b:
            return -(product[SLOT[(a, b)]] * blocks[parity])
        other = tuple(1 - p if axis in (a, b) else p for axis, p in enumerate(parity))
        value = product[SLOT[(a, b)]] * blocks[other]
        return value if parity[a] == parity[b] else -value

    psi = {}
    raw = {}
    for parity in parities:
        raw[parity] = take(1, parity)
        psi[parity] = inverse * raw[parity]
    phi = {}
    for parity in parities:
        pressed = sum(
            (1.0 if a == b else 2.0) * dev[SLOT[(a, b)]] * second(psi, parity, a, b) for a, b in PAIRS
        )
        phi[parity] = (1.0 - green_ratio) * inverse * take(0, parity) + scaled * pressed
    for parity in parities:
        curl = {pair: second(psi, parity, *pair) for pair in PAIRS}
        for index, (a, b) in enumerate(PAIRS):
            def at(i, j):
                return curl[(min(i, j), max(i, j))]
            if a == b:
                sheared = sum(dev[SLOT[(b, c)]] * at(a, c) for c in range(3))
            else:
                sheared = 0.5 * sum(dev[SLOT[(b, c)]] * at(a, c) + dev[SLOT[(a, c)]] * at(b, c) for c in range(3))
            value = second(phi, parity, a, b) + sheared
            rows, pieces = block(index, *parity)
            for fold, lanes in enumerate(pieces):
                spectrum[rows, lanes] = value[:, fold * quarter // 2 : (fold + 1) * quarter // 2]
    lines = backward_plane(spectrum[...], table)
    copies[8].wait()
    moved = jnp.concatenate(
        [table_by(bwd_ref[0], bwd_ref[1], lines[i * vox : (i + 2) * vox]) for i in range(0, 6, 2)], axis=0
    )
    if 2 * planes == 8:
        low = row_position((2 * planes, columns)) < planes
        for pair in range(3):
            for chip in range(devices // 2):
                first, second_ = (
                    moved[i * vox + 2 * chip * planes : i * vox + 2 * (chip + 1) * planes]
                    for i in (2 * pair, 2 * pair + 1)
                )
                rows = slice(2 * pair * planes, 2 * (pair + 1) * planes)
                ordered[2 * chip, rows] = jnp.where(low, first, pltpu.roll(second_, planes, 0))
                ordered[2 * chip + 1, rows] = jnp.where(low, pltpu.roll(first, planes, 0), second_)
    else:
        for i in range(6):
            for device in range(devices):
                ordered[device, i * planes : (i + 1) * planes] = moved[
                    i * vox + device * planes : i * vox + (device + 1) * planes
                ]
    for device in range(devices):
        sent_ref[device] = ordered[device].astype(bf16)
    send = pltpu.make_async_copy(sent_ref, sent_hbm, sem.at[len(pairs)])
    send.start()
    strain = [load[i] + moved[i * vox : (i + 1) * vox] for i in range(6)]
    trace, dev = deviator_of(strain)
    left, ratio = remaining(shear, measure([0.5 * part for part in dev]), steps, 4)
    push = bulk * trace
    pull = 2.0 * shear * left
    stress = [push + pull * dev[i] for i in range(3)] + [pull * dev[i] for i in range(3, 6)]
    parts = stress + [lame, shear / (1.0 + ratio)]
    lane = lane_position((1, response_ref.shape[1]))
    row = jnp.zeros(lane.shape, f32)
    for index, part in enumerate(parts):
        row = jnp.where(lane == index, total(part) / float(vox * columns), row)
    for index, part in enumerate(load):
        row = jnp.where(lane == 8 + index, part, row)
    response_ref[...] = jnp.broadcast_to(row, response_ref.shape)
    answer = pltpu.make_async_copy(response_ref, response_hbm, sem.at[len(pairs) + 1])
    answer.start()
    send.wait()
    answer.wait()


def vox_width(columns):
    width = int(round(columns**0.5))
    return width


def macro_kernel(
    layers, base, slots_ref, table_ref, table_v_ref, packet_ref, own_ref, core_ref, side_ref, across_ref, next_ref, row_ref, labels, forces, cells, result
):
    columns = next_ref.shape[2]
    devices = labels.shape[0] // layers
    samples = table_v_ref.shape[0]
    rank = lax.axis_index("dev")
    group = lax.axis_index("grp")
    local_count = row_ref.shape[0]
    group_size = local_count * devices
    start = group * group_size
    for local in range(local_count):
        chosen = jnp.int32(0)
        for j in range(group_size):
            chosen = jnp.where(slots_ref[start + j] == rank * local_count + local, start + j, chosen)
        row_ref[local : local + 1, :] = table_v_ref[pl.ds(chosen, 1), 0:8]
    for layer in range(layers):
        labels[layer * devices : (layer + 1) * devices, :] = read_label(
            packet_ref, base, layer, devices, columns // LANES
        )
    read_force((own_ref, core_ref, side_ref, across_ref), layers, forces)
    rows = labels.shape[0]
    height = min(8, rows)
    span = min(512, columns)
    for top in range(0, rows, height):
        for side in range(0, columns, span):
            where = (slice(top, top + height), slice(side, side + span))
            label = labels[where]

            def pick(sample, held):
                here = label == sample.astype(f32)
                return tuple(jnp.where(here, table_ref[sample, c], held[c]) for c in range(8))

            zero = jnp.zeros((height, span), f32)
            held = lax.fori_loop(0, samples, pick, (zero,) * 8, unroll=4)
            for c in range(8):
                cells[(c,) + where] = held[c]
    stencil = Stencil(labels.shape, vox_width(columns), devices)
    stress = [cells[c] for c in range(6)]
    pulled = stencil.force(stress)
    remainder = [forces[b] - pulled[b] for b in range(3)]
    direction = remainder
    norm_now = total(sum(r * r for r in remainder))
    update = None
    lame = cells[6]
    shear = 2.0 * cells[7]
    for turn in range(CG_STEPS):
        strain = stencil.strain(direction)
        pressure = lame * (strain[0] + strain[1] + strain[2])
        stress = [shear * strain[i] + pressure for i in range(3)] + [shear * strain[i] for i in range(3, 6)]
        pulled = stencil.force(stress)
        image = [pulled[b] + spring_rate * direction[b] for b in range(3)]
        alpha = norm_now / total(sum(direction[b] * image[b] for b in range(3)))
        moved = [alpha * direction[b] for b in range(3)]
        update = moved if update is None else [update[b] + moved[b] for b in range(3)]
        if turn + 1 < CG_STEPS:
            remainder = [remainder[b] - alpha * image[b] for b in range(3)]
            norm_next = total(sum(r * r for r in remainder))
            grow = norm_next / norm_now
            direction = [remainder[b] + grow * direction[b] for b in range(3)]
            norm_now = norm_next
    for b in range(3):
        result[b] = update[b]
        for layer in range(layers):
            next_ref[b, layer : layer + 1, :] = result[b, pl.ds(layer * devices + rank, 1), :]


def vmem():
    return pl.BlockSpec(memory_space=pltpu.VMEM)


def hbm():
    return pl.BlockSpec(memory_space=pltpu.HBM)


def smem():
    return pl.BlockSpec(memory_space=pltpu.SMEM)


def shards(
    displacement, external_force, element_sample, lame_field, shear_field, plastic_steps, owner_slot
):
    group_size, planes, columns = lame_field.shape
    devices = lax.axis_size("dev")
    groups = lax.axis_size("grp")
    local_count = group_size // devices
    vox = planes * devices
    layers = displacement.shape[1]
    width = displacement.shape[2] * displacement.shape[3]
    plane, forward_line, backward_line, multipliers = tables(vox)
    pack_params, params, macro_params = (
        pltpu.CompilerParams(vmem_limit_bytes=size * 1024 * 1024) for size in (60, 60, 16)
    )

    side = displacement.shape[3]
    lines = layers * displacement.shape[2]
    tiles = columns // LANES
    base = local_count * planes * tiles
    tail = base + (3 + (layers + 1) // 2) * tiles
    length = tail + 3 * layers * tiles // 4 + local_count * SUM_ROWS
    packet = pl.pallas_call(
        functools.partial(pack_kernel, layers),
        name="pack",
        out_shape=jax.ShapeDtypeStruct((devices, length, LANES), f32),
        in_specs=[vmem()] * 5,
        out_specs=vmem(),
        scratch_shapes=[pltpu.VMEM((7 * lines, LANES), f32)],
        compiler_params=pack_params,
    )(
        displacement.reshape(3 * lines, side), element_sample.reshape(lines, side),
        external_force.reshape(3 * lines, side),
        lame_field.reshape(devices, local_count, planes, columns),
        shear_field.reshape(devices, local_count, planes, columns),
    )
    packets = lax.all_to_all(packet, "dev", split_axis=0, concat_axis=0, tiled=True).reshape(devices * length, LANES)
    own_tail = packets.reshape(devices, length, LANES)[:, tail:].reshape(-1, LANES)
    tails = [own_tail, lax.ppermute(own_tail, "dev", [(i, i ^ 1) for i in range(devices)])]
    tails.append(lax.ppermute(own_tail, "grp", [(i, i ^ 1) for i in range(groups)]))
    flips = [(i, i ^ 1 ^ devices) for i in range(groups * devices)]
    tails.append(lax.ppermute(own_tail, ("grp", "dev"), flips))
    everyone = groups * devices
    sents = []
    rows = []
    for local in range(local_count):
        sent, response = pl.pallas_call(
            functools.partial(micro_kernel, local, local_count, layers),
            name="micro",
            out_shape=(
                jax.ShapeDtypeStruct((devices, 6 * planes, columns), bf16),
                jax.ShapeDtypeStruct((everyone, 16), f32),
            ),
            in_specs=[hbm()] * 6,
            out_specs=(hbm(), hbm()),
            scratch_shapes=[
                pltpu.VMEM((devices * length, LANES), f32),
                pltpu.VMEM((2, vox, columns), f32),
                pltpu.VMEM(multipliers.shape, f32),
                pltpu.VMEM(forward_line.shape, bf16),
                pltpu.VMEM(backward_line.shape, bf16),
                pltpu.VMEM(plane.shape, bf16),
                pltpu.VMEM((6 * vox, columns), f32),
                pltpu.VMEM((devices, 6 * planes, columns), f32),
                pltpu.VMEM((devices, 6 * planes, columns), bf16),
                pltpu.VMEM((everyone, 16), f32),
                pltpu.SMEM(plastic_steps.shape, jnp.int32),
                pltpu.SemaphoreType.DMA((11,)),
            ],
            compiler_params=params,
        )(
            plastic_steps, packets, multipliers, forward_line, backward_line, plane,
        )
        sents.append(sent)
        rows.append(response)
    gathered = lax.all_to_all(
        jnp.stack(rows, axis=1), ("grp", "dev"), split_axis=0, concat_axis=0, tiled=True
    ).reshape(everyone * local_count, 16)
    moved = lax.all_to_all(jnp.stack(sents, axis=1), "dev", split_axis=0, concat_axis=0, tiled=True)
    group_rows = lax.dynamic_slice_in_dim(gathered, lax.axis_index("grp") * group_size, group_size)
    loads = group_rows[:, 8:14].T
    change = jnp.transpose(moved.reshape(group_size, 6, planes, columns), (1, 0, 2, 3))
    micro_strain = loads[:, :, None, None] + change.astype(f32)
    following, picked = pl.pallas_call(
        functools.partial(macro_kernel, layers, base),
        name="macro",
        out_shape=(
            jax.ShapeDtypeStruct((3, layers, width), f32),
            jax.ShapeDtypeStruct((local_count, 8), f32),
        ),
        in_specs=[smem(), smem()] + [vmem()] * 6,
        out_specs=(vmem(), vmem()),
        scratch_shapes=[
            pltpu.VMEM((devices * layers, width), f32),
            pltpu.VMEM((3, devices * layers, width), f32),
            pltpu.VMEM((8, devices * layers, width), f32),
            pltpu.VMEM((3, devices * layers, width), f32),
        ],
        compiler_params=macro_params,
    )(owner_slot, gathered, gathered, packets, *tails)
    return (displacement + following.reshape(displacement.shape), picked, micro_strain)


def solution(mesh):
    in_specs = (
        P(None, "dev", None, None),
        P(None, "dev", None, None),
        P("dev", None, None),
        P("grp", "dev", None),
        P("grp", "dev", None),
        P(),
        P(),
    )
    out_specs = (P(None, "dev", None, None), P(("grp", "dev"), None), P(None, "grp", "dev", None))
    return jax.shard_map(shards, mesh=mesh, in_specs=in_specs, out_specs=out_specs, check_vma=False)
```
